32 devices in a mesh: ctx: 8 (over z, x), head: 4 (over y, core).
Axes of the slice: x: 2, y: 2, z: 4, core: 2. Of those that a mesh axis runs over, the one named last changes fastest.
Arguments:
- queries: float32 [2048, 4096], P('ctx', 'head'), may hold values from -48 to 48
- keys: float32 [2048, 4096], P('ctx', 'head'), may hold values from -48 to 48
- values: float32 [2048, 4096], P('ctx', 'head'), may hold values from -8 to 8
- query_map: float32 [32, 128, 128], P('head'), may hold values from -2 to 2
- key_map: float32 [32, 128, 128], P('head'), may hold values from -2 to 2
- out_weight: float32 [4096, 4096], P(None, ('ctx', 'head')), may hold values from -0.09375 to 0.09375
- residual: float32 [2048, 4096], P('ctx', 'head'), may hold values from -1.5 to 1.5
Outputs:
- layer_out: float32 [2048, 4096], P('ctx', 'head')
The draws below stay inside these ranges and needn't reach their ends.
All inputs are finite; a program needn't handle non-finite values.
Results may differ from the reference program's by a relative error of at most 0.0001.
Values sent between devices are 32-bit elements; how exact they have to be, the bound alone decides.
No kernel may reach another device: no remote copies, remote signals or barrier semaphores. Data moves between devices by JAX's collectives and lax.ppermute only.
A program may use at most 192 MiB of HBM per device.

```python
import math
import jax
import jax.numpy as jnp
from jax import lax

D = 4096
H = 32
HD = 128
F = 128
TOKENS = 2048


def map_draw(key, salt):
    weights = jax.random.normal(jax.random.fold_in(key, salt), (H, HD, F), jnp.float32) * (2.0 / math.sqrt(HD))
    return jnp.clip(weights, -2.0, 2.0)


def drift_draw(key, salt):
    cycle_key, phase_key, level_key = jax.random.split(jax.random.fold_in(key, salt), 3)
    cycles = jax.random.uniform(cycle_key, (1, H, HD), jnp.float32, 0.5, 3.0)
    phase = jax.random.uniform(phase_key, (1, H, HD), jnp.float32, -math.pi, math.pi)
    levels = jax.random.uniform(level_key, (1, H, HD), jnp.float32, 0.5, 1.5)
    position = jnp.arange(TOKENS, dtype=jnp.float32)[:, None, None] / TOKENS
    return levels * jnp.sin(2.0 * math.pi * cycles * position + phase)


def input_draw(key, salt, drifting):
    base = jnp.clip(jax.random.normal(jax.random.fold_in(key, salt), (TOKENS, H, HD), jnp.float32), -6.0, 6.0)
    if drifting:
        base = base + drift_draw(key, salt + 200)
    return jnp.clip(base, -48.0, 48.0).reshape(TOKENS, D)


def draw_query_map(key, part):
    return map_draw(key, 11)


def draw_key_map(key, part):
    return map_draw(key, 12)


def draw_queries(key, part):
    return input_draw(key, 21, False)


def draw_keys(key, part):
    return input_draw(key, 22, True)


def draw_values(key, part):
    noise_key, offset_key = jax.random.split(jax.random.fold_in(key, 31))
    noise = jnp.clip(jax.random.normal(noise_key, (TOKENS, H, HD), jnp.float32), -4.0, 4.0)
    offset = jax.random.uniform(offset_key, (1, H, HD), jnp.float32, -1.0, 1.0)
    total = noise + offset + drift_draw(key, 33)
    return jnp.clip(total, -8.0, 8.0).reshape(TOKENS, D)


def steps_of(key, extent, cuts, least, top_value):
    def one(dim, parts):
        heights = jax.random.uniform(jax.random.fold_in(jax.random.fold_in(key, 6), dim), (parts,), jnp.float32, least / len(cuts), top_value / len(cuts))
        return jnp.repeat(jnp.exp(heights), extent[dim] // parts).reshape((-1,) + (1,) * (len(extent) - dim - 1))

    loudness = one(*cuts[0])
    for cut in cuts[1:]:
        loudness = loudness * one(*cut)
    return loudness


def bell_draw(rng, extent, scale, limit, cuts=(), kind=jnp.bfloat16):
    factor_of = steps_of(rng, extent, cuts, -0.22, 0.18) if cuts else 1.0
    entries = jax.random.normal(rng, extent, jnp.float32) * scale * factor_of
    return jnp.minimum(jnp.maximum(entries, -limit), limit).astype(kind)


def setup_inputs(seed: int = 0) -> dict:
    splits = jax.random.split(jax.random.key(seed), 8)
    queries = draw_queries(jax.random.fold_in(splits[7], 71), 0)
    keys = draw_keys(jax.random.fold_in(splits[7], 71), 0)
    values = draw_values(jax.random.fold_in(splits[7], 71), 0)
    query_map = draw_query_map(jax.random.fold_in(splits[7], 71), 0)
    key_map = draw_key_map(jax.random.fold_in(splits[7], 71), 0)
    out_weight = bell_draw(splits[5], (D, D), D ** -0.5, 0.09375, ((1, 32),), jnp.float32)
    residual = bell_draw(splits[6], (TOKENS, D), 0.25, 1.5, ((0, 8), (1, 4)), jnp.float32)
    return {"queries": queries, "keys": keys, "values": values, "query_map": query_map, "key_map": key_map, "out_weight": out_weight, "residual": residual}


HIGH = lax.Precision.HIGHEST


def feature_map(inputs, weights):
    scores = jnp.einsum("nhd,hdf->hnf", inputs, weights, precision=HIGH)
    return jnp.concatenate([jax.nn.softmax(scores, axis=-1), jax.nn.softmax(-scores, axis=-1)], axis=-1)


def reference(queries, keys, values, query_map, key_map, out_weight, residual):
    block = math.gcd(TOKENS, 512)
    count = TOKENS // block
    causal = jnp.tril(jnp.ones((block, block), jnp.float32))

    def split_rows(array):
        return array.reshape(count, block, H, HD)

    def advance(carry, pieces):
        state, norm = carry
        q_block, k_block, v_block = pieces
        query_feat = feature_map(q_block, query_map)
        key_feat = feature_map(k_block, key_map)
        value_heads = v_block.transpose(1, 0, 2)
        weights = jnp.einsum("hqf,hkf->hqk", query_feat, key_feat, precision=HIGH) * causal
        numer = jnp.einsum("hqk,hkd->hqd", weights, value_heads, precision=HIGH)
        numer = numer + jnp.einsum("hqf,hfd->hqd", query_feat, state, precision=HIGH)
        denom = jnp.sum(weights, axis=-1) + jnp.einsum("hqf,hf->hq", query_feat, norm, precision=HIGH)
        mixed = (numer / denom[..., None]).transpose(1, 0, 2).reshape(block, D)
        state = state + jnp.einsum("hkf,hkd->hfd", key_feat, value_heads, precision=HIGH)
        norm = norm + jnp.sum(key_feat, axis=1)
        return (state, norm), mixed

    start = (jnp.zeros((H, 2 * F, HD), jnp.float32), jnp.zeros((H, 2 * F), jnp.float32))
    _, mixed = lax.scan(advance, start, (split_rows(queries), split_rows(keys), split_rows(values)))
    mixed = mixed.reshape(TOKENS, D)
    return residual + jnp.dot(mixed, out_weight, precision=HIGH, preferred_element_type=jnp.float32)
```

```python
import functools

import numpy as np

import jax
import jax.numpy as jnp
from jax import lax
from jax.experimental import pallas as pl
from jax.experimental.pallas import tpu as pltpu
from jax.sharding import PartitionSpec as P

HIGH = lax.Precision.HIGHEST
AXES = ("ctx", "head")
PAIR = 2
EXTRA = 8
VMEM_LIMIT = 48 * 1024 * 1024


def split(x):
    high = x.astype(jnp.bfloat16)
    return high, (x - high.astype(jnp.float32)).astype(jnp.bfloat16)


def dot3(a, b, dims=(((1,), (0,)), ((), ()))):
    a_high, a_low = split(a)
    b_high, b_low = split(b)
    dot = functools.partial(lax.dot_general, dimension_numbers=dims, preferred_element_type=jnp.float32)
    return dot(a_high, b_high) + (dot(a_high, b_low) + dot(a_low, b_high))


def features(rows, weights):
    scores = jnp.dot(rows, weights, precision=HIGH, preferred_element_type=jnp.float32)
    up = jnp.exp(scores - jnp.max(scores, axis=-1, keepdims=True))
    down = jnp.exp(jnp.min(scores, axis=-1, keepdims=True) - scores)
    up = up / jnp.sum(up, axis=-1, keepdims=True)
    down = down / jnp.sum(down, axis=-1, keepdims=True)
    return jnp.concatenate([up, down], axis=-1)


def key_kernel(first, k_ref, map_ref, v_ref, state_ref, feat_ref):
    feat = features(k_ref[...], map_ref[0])
    feat_ref[0] = feat
    size = feat.shape[1]
    half = size // 2
    state_ref[0, :size, :] = dot3(feat, v_ref[...], (((0,), (0,)), ((), ())))
    norm = jnp.sum(feat, axis=0, keepdims=True)
    row = lax.broadcasted_iota(jnp.int32, (EXTRA, half), 0)
    state_ref[0, size:, :] = jnp.where(row < EXTRA // 2, norm[:, :half], norm[:, half:])


def query_kernel(first, q_ref, map_ref, feat_ref, v_ref, qfeat_ref, numer_ref, denom_ref):
    feat = features(q_ref[...], map_ref[0])
    qfeat_ref[0] = feat
    weights = dot3(feat, feat_ref[0], (((1,), (1,)), ((), ())))
    row = lax.broadcasted_iota(jnp.int32, weights.shape, 0)
    column = lax.broadcasted_iota(jnp.int32, weights.shape, 1)
    weights = jnp.where(column <= row, weights, 0.0)
    numer_ref[0] = dot3(weights, v_ref[...])
    denom_ref[0] = jnp.broadcast_to(jnp.sum(weights, axis=-1, keepdims=True), denom_ref.shape[1:])


def mix_kernel(qfeat_ref, numer_ref, denom_ref, prior_ref, out_ref):
    feat = qfeat_ref[0]
    size = feat.shape[1]
    norm = jnp.concatenate(
        [prior_ref[0, size : size + 1, :], prior_ref[0, size + EXTRA // 2 : size + EXTRA // 2 + 1, :]], axis=1
    )
    denom = denom_ref[0] + jnp.sum(feat * norm, axis=-1, keepdims=True)
    out_ref[...] = (numer_ref[0] + dot3(feat, prior_ref[0, :size, :])) / denom


def project_kernel(pieces, strips, has_total, first, *refs):
    blocks = len(pieces[0])
    a_refs, refs = refs[: 2 * blocks], refs[2 * blocks :]
    w_refs, refs = refs[: strips * blocks], refs[strips * blocks :]
    out_ref = refs[-1]
    rows = a_refs[0].shape[0]
    total = refs[0][...] if has_total else None
    for block in range(blocks):
        a = jnp.concatenate([a_refs[block][...], a_refs[blocks + block][...]], axis=0)
        w = jnp.concatenate([w_refs[s * blocks + block][...] for s in range(strips)], axis=1)
        part = dot3(a, w)
        total = part if total is None else total + part
    out_ref[...] = total


def route_tables(ctx, heads, rels):
    groups = {}
    for column, rel in enumerate(rels):
        groups.setdefault(rel * heads // ctx, []).append(column)
    groups = [groups[key] for key in sorted(groups)]
    size = len(groups[0])
    targets = {}
    for c in range(ctx):
        for h in range(heads):
            found = {}
            for d, step in enumerate((0, PAIR)):
                for g, columns in enumerate(groups):
                    to = (c ^ step) * heads + (c ^ rels[columns[0]]) * heads // ctx
                    found[to] = d * len(groups) + g
            targets[c * heads + h] = found
    classes = {}
    for device in sorted(targets):
        classes.setdefault(tuple(sorted(targets[device])), []).append(device)
    steps = 2 * len(groups)
    perms = [[] for _ in range(steps)]
    send = np.zeros((ctx * heads, steps), np.int32)
    arrives = {}
    for ends, sources in classes.items():
        for i, source in enumerate(sources):
            for k in range(steps):
                to = ends[i ^ k]
                perms[k].append((source, to))
                send[source, k] = targets[source][to]
                arrives[to, source] = k
    place = np.zeros((ctx * heads, ctx), np.int32)
    for c in range(ctx):
        for h in range(heads):
            for p in range(ctx):
                column_ctx, source_h = divmod(h * ctx + p, heads)
                source_c = (c & ~PAIR) | (column_ctx & PAIR)
                k = arrives[c * heads + h, source_c * heads + source_h]
                rel = source_c ^ column_ctx
                group = [g for g in groups if rels.index(rel) in g][0]
                place[c * heads + h, p] = k * size + group.index(rels.index(rel))
    return groups, perms, send, place


def body(ctx, heads, queries, keys, values, query_map, key_map, out_weight, residual):
    rows, width = queries.shape
    heads_here, head_size, feat_half = query_map.shape
    feat_size = 2 * feat_half
    half = heads_here // 2
    wide = half * head_size
    depth = out_weight.shape[0] // heads
    strip_width = out_weight.shape[1]
    c = lax.axis_index("ctx")
    h = lax.axis_index("head")
    me = c * heads + h
    odd = c & 1

    def swap(x, by_ctx, by_head=0, keep=lambda c: True):
        pairs = [
            (i * heads + j, (i ^ by_ctx) * heads + (j ^ by_head))
            for i in range(ctx)
            for j in range(heads)
            if keep(i)
        ]
        return lax.ppermute(x, AXES, pairs)

    params = pltpu.CompilerParams(vmem_limit_bytes=VMEM_LIMIT)
    column_block = pl.BlockSpec((rows, head_size), lambda i, first: (0, first[0] + i))
    map_block = pl.BlockSpec((1, head_size, feat_half), lambda i, first: (first[0] + i, 0, 0))

    def head_block(size, lanes):
        return pl.BlockSpec((1, size, lanes), lambda i, *_: (i, 0, 0))

    def key_part(first):
        return pl.pallas_call(
            key_kernel,
            grid_spec=pltpu.PrefetchScalarGridSpec(
                num_scalar_prefetch=1,
                grid=(half,),
                in_specs=[column_block, map_block, column_block],
                out_specs=[head_block(feat_size + EXTRA, head_size), head_block(rows, feat_size)],
            ),
            out_shape=[
                jax.ShapeDtypeStruct((half, feat_size + EXTRA, head_size), jnp.float32),
                jax.ShapeDtypeStruct((half, rows, feat_size), jnp.float32),
            ],
            compiler_params=params,
            name="key_part",
            cost_estimate=pl.CostEstimate(
                flops=12 * half * rows * head_size * (feat_half + feat_size),
                bytes_accessed=4 * half * rows * (2 * head_size + 2 * feat_size),
                transcendentals=half * rows * feat_size,
            ),
        )(first, keys, key_map, values)

    def query_part(first, feat):
        return pl.pallas_call(
            query_kernel,
            grid_spec=pltpu.PrefetchScalarGridSpec(
                num_scalar_prefetch=1,
                grid=(half,),
                in_specs=[column_block, map_block, head_block(rows, feat_size), column_block],
                out_specs=[head_block(rows, feat_size), head_block(rows, head_size), head_block(rows, head_size)],
            ),
            out_shape=[
                jax.ShapeDtypeStruct((half, rows, feat_size), jnp.float32),
                jax.ShapeDtypeStruct((half, rows, head_size), jnp.float32),
                jax.ShapeDtypeStruct((half, rows, head_size), jnp.float32),
            ],
            compiler_params=params,
            name="query_part",
            cost_estimate=pl.CostEstimate(
                flops=12 * half * rows * (head_size * feat_half + rows * (feat_size + head_size)),
                bytes_accessed=4 * half * rows * (4 * head_size + 2 * feat_size),
                transcendentals=half * rows * feat_size,
            ),
        )(first, queries, query_map, feat, values)

    def mix(qfeat, numer, denom, prior):
        return pl.pallas_call(
            mix_kernel,
            grid=(half,),
            in_specs=[
                head_block(rows, feat_size),
                head_block(rows, head_size),
                head_block(rows, head_size),
                head_block(feat_size + EXTRA, head_size),
            ],
            out_specs=pl.BlockSpec((rows, head_size), lambda i: (0, i)),
            out_shape=jax.ShapeDtypeStruct((rows, wide), jnp.float32),
            compiler_params=params,
            name="mix",
            cost_estimate=pl.CostEstimate(
                flops=6 * half * rows * feat_size * head_size,
                bytes_accessed=4 * half * rows * (3 * head_size + 2 * feat_size),
                transcendentals=0,
            ),
        )(qfeat, numer, denom, prior)

    own_first = (odd * half).reshape(1)
    other_first = ((1 - odd) * half).reshape(1)
    other_state, other_feat = key_part(other_first)
    from_neighbour = swap(other_state, 1)
    own_state, own_feat = key_part(own_first)

    chunks = [lax.dynamic_slice_in_dim(out_weight, (h ^ d) * depth, depth, 0) for d in range(heads)]
    bits = [1 << b for b in reversed(range(ctx.bit_length() - 1)) if 1 << b != PAIR]
    rels = [0]
    for bit in bits[:-2]:
        chunks = [jnp.concatenate([chunk, swap(chunk, bit)], axis=1) for chunk in chunks]
        rels = rels + [r | bit for r in rels]
    far, near = bits[-2:]
    rels = [r | s for s in (0, near, far, far | near) for r in rels]

    earlier = jnp.where(odd == 0, own_state, from_neighbour)
    total = own_state + from_neighbour
    before = jnp.zeros_like(total)
    bit = 2
    while bit < ctx:
        last = 2 * bit >= ctx
        got = swap(total, bit, keep=lambda i: not i & bit) if last else swap(total, bit)
        before = before + jnp.where((c & bit) != 0, got, 0.0)
        total = total + got
        bit *= 2
    own_prior = before + jnp.where(odd == 1, earlier, 0.0)
    other_prior = swap(before + jnp.where(odd == 0, earlier, 0.0), 1)

    strips = {0: chunks, near: [swap(chunk, near) for chunk in chunks], far: [], far | near: []}
    for d, chunk in enumerate(chunks):
        if d >= heads // 2:
            chunk, _ = lax.optimization_barrier((chunk, before[0, 0]))
        strips[far].append(swap(chunk, far))
        strips[far | near].append(swap(strips[far][-1], near))

    own_query = query_part(own_first, own_feat)
    other_query = query_part(other_first, other_feat)

    def gather(part):
        pieces = {(0, 0): part}
        for by_head in range(0, heads, 2):
            for by_ctx in (0, PAIR):
                if by_head or by_ctx:
                    pieces[by_ctx, by_head] = swap(part, by_ctx, by_head)
        for by_ctx, by_head in list(pieces):
            pieces[by_ctx, by_head | 1] = swap(pieces[by_ctx, by_head], 0, 1)
        return [[pieces[d, j] for j in range(heads)] for d in (0, PAIR)]

    names = (0, near, far, far | near)
    lanes = chunks[0].shape[1]

    def project(first, pieces, total):
        flat = pieces[0] + pieces[1]
        weights = [strips[s][d] for s in names for d in range(heads)]
        whole = pl.BlockSpec((rows, wide), lambda i, first: (0, 0))
        out_block = pl.BlockSpec((2 * rows, len(names) * lanes), lambda i, first: (0, 0))
        part = pl.BlockSpec((wide, lanes), lambda i, first: (first[0], 0))
        extra = [] if total is None else [total]
        return pl.pallas_call(
            functools.partial(project_kernel, pieces, len(names), total is not None),
            grid_spec=pltpu.PrefetchScalarGridSpec(
                num_scalar_prefetch=1,
                grid=(1,),
                in_specs=[whole] * len(flat) + [part] * len(weights) + [out_block] * len(extra),
                out_specs=out_block,
            ),
            out_shape=jax.ShapeDtypeStruct((2 * rows, len(names) * lanes), jnp.float32),
            compiler_params=params,
            name="project",
            cost_estimate=pl.CostEstimate(
                flops=12 * rows * wide * heads * len(names) * lanes,
                bytes_accessed=4 * wide * heads * (2 * rows + len(names) * lanes),
                transcendentals=0,
            ),
        )(first, *flat, *weights, *extra)

    own_mixed = mix(*own_query, own_prior)
    own_pieces = gather(own_mixed)
    other_mixed = mix(*other_query, other_prior)
    other_pieces = gather(other_mixed)
    product = project(odd.reshape(1), own_pieces, None)
    product = project((1 - odd).reshape(1), other_pieces, product)

    groups, perms, send, place = route_tables(ctx, heads, rels)
    parts = jnp.stack(
        [
            jnp.concatenate(
                [product[d * rows : (d + 1) * rows, b * strip_width : (b + 1) * strip_width] for b in group], axis=1
            )
            for d in range(2)
            for group in groups
        ]
    )
    send_here = jnp.asarray(send)[me]
    place_here = jnp.asarray(place)[me]
    arrived = [
        lax.ppermute(lax.dynamic_index_in_dim(parts, send_here[k], 0, False), AXES, perm)
        for k, perm in enumerate(perms)
    ]
    blocks = jnp.stack(
        [a[:, b * strip_width : (b + 1) * strip_width] for a in arrived for b in range(len(groups[0]))]
    )
    projected = jnp.concatenate(
        [lax.dynamic_index_in_dim(blocks, place_here[p], 0, False) for p in range(ctx)], axis=1
    )
    return residual + projected


def solution(mesh):
    placed = (
        P("ctx", "head"),
        P("ctx", "head"),
        P("ctx", "head"),
        P("head", None, None),
        P("head", None, None),
        P(None, ("ctx", "head")),
        P("ctx", "head"),
    )
    return jax.shard_map(
        functools.partial(body, mesh.shape["ctx"], mesh.shape["head"]),
        mesh=mesh,
        in_specs=placed,
        out_specs=P("ctx", "head"),
        check_vma=False,
    )
```

```python
import functools

import numpy as np

import jax
import jax.numpy as jnp
from jax import lax
from jax.experimental import pallas as pl
from jax.experimental.pallas import tpu as pltpu
from jax.sharding import PartitionSpec as P

HIGH = lax.Precision.HIGHEST
together = lax.optimization_barrier
AXES = ("ctx", "head")
PAIR = 2
EXTRA = 8
VMEM_LIMIT = 48 * 1024 * 1024


def split(x):
    high = x.astype(jnp.bfloat16)
    return high, (x - high.astype(jnp.float32)).astype(jnp.bfloat16)


def dot3(a, b, dims=(((1,), (0,)), ((), ()))):
    a_high, a_low = split(a)
    b_high, b_low = split(b)
    dot = functools.partial(lax.dot_general, dimension_numbers=dims, preferred_element_type=jnp.float32)
    return dot(a_high, b_high) + (dot(a_high, b_low) + dot(a_low, b_high))


def features(rows, weights):
    scores = jnp.dot(rows, weights, precision=HIGH, preferred_element_type=jnp.float32)
    up = jnp.exp(scores - jnp.max(scores, axis=-1, keepdims=True))
    down = jnp.exp(jnp.min(scores, axis=-1, keepdims=True) - scores)
    up = up / jnp.sum(up, axis=-1, keepdims=True)
    down = down / jnp.sum(down, axis=-1, keepdims=True)
    return jnp.concatenate([up, down], axis=-1)


def key_kernel(first, k_ref, map_ref, v_ref, state_ref, feat_ref):
    heads, head_size, feat_half = map_ref.shape
    size = 2 * feat_half
    row = lax.broadcasted_iota(jnp.int32, (EXTRA, feat_half), 0)
    for i in range(heads):
        columns = slice(i * head_size, (i + 1) * head_size)
        feat = features(k_ref[:, columns], map_ref[i])
        feat_ref[i] = feat
        state_ref[i, :size, :] = dot3(feat, v_ref[:, columns], (((0,), (0,)), ((), ())))
        norm = jnp.sum(feat, axis=0, keepdims=True)
        state_ref[i, size:, :] = jnp.where(row < EXTRA // 2, norm[:, :feat_half], norm[:, feat_half:])


def query_kernel(first, q_ref, map_ref, feat_ref, v_ref, qfeat_ref, numer_ref, denom_ref):
    feat = features(q_ref[...], map_ref[0])
    qfeat_ref[0] = feat
    weights = dot3(feat, feat_ref[0], (((1,), (1,)), ((), ())))
    row = lax.broadcasted_iota(jnp.int32, weights.shape, 0)
    column = lax.broadcasted_iota(jnp.int32, weights.shape, 1)
    weights = jnp.where(column <= row, weights, 0.0)
    numer_ref[0] = dot3(weights, v_ref[...])
    denom_ref[0] = jnp.broadcast_to(jnp.sum(weights, axis=-1, keepdims=True), denom_ref.shape[1:])


def mix_kernel(qfeat_ref, numer_ref, denom_ref, prior_ref, out_ref):
    feat = qfeat_ref[0]
    size = feat.shape[1]
    norm = jnp.concatenate(
        [prior_ref[0, size : size + 1, :], prior_ref[0, size + EXTRA // 2 : size + EXTRA // 2 + 1, :]], axis=1
    )
    denom = denom_ref[0] + jnp.sum(feat * norm, axis=-1, keepdims=True)
    out_ref[...] = (numer_ref[0] + dot3(feat, prior_ref[0, :size, :])) / denom


def project_kernel(count, strips, *refs):
    a_refs, b_refs, w_refs = refs[:count], refs[count : 2 * count], refs[2 * count : (2 + strips) * count]
    rest, out_ref = refs[(2 + strips) * count : -1], refs[-1]
    total = rest[0][...] if rest else None
    for i in range(count):
        a = jnp.concatenate([a_refs[i][...], b_refs[i][...]], axis=0)
        w = jnp.concatenate([ref[...] for ref in w_refs[i * strips : (i + 1) * strips]], axis=1)
        part = dot3(a, w)
        total = part if total is None else total + part
    out_ref[...] = total


def pieces_of(product, groups, width):
    rows = product.shape[0] // 2
    return [
        jnp.concatenate([product[d * rows : (d + 1) * rows, b * width : (b + 1) * width] for b in group], axis=1)
        for d in range(2)
        for group in groups
    ]


def route_kernel(groups, width, send, near_ref, far_ref, other_ref, *refs):
    out_refs, pieces_ref = refs[:-1], refs[-1]
    product = jnp.concatenate([near_ref[...], far_ref[...]], axis=1) + other_ref[...]
    for j, piece in enumerate(pieces_of(product, groups, width)):
        pieces_ref[j] = piece
    for k, out_ref in enumerate(out_refs):
        out_ref[...] = pieces_ref[send[k]]


def assemble_kernel(size, place, *refs):
    arrived, (residual_ref, out_ref, blocks_ref) = refs[:-3], refs[-3:]
    width = blocks_ref.shape[2]
    for k, ref in enumerate(arrived):
        for b in range(size):
            blocks_ref[k * size + b] = ref[:, b * width : (b + 1) * width]
    for p in range(blocks_ref.shape[0]):
        columns = slice(p * width, (p + 1) * width)
        out_ref[:, columns] = residual_ref[:, columns] + blocks_ref[place[p]]


def route_tables(ctx, heads, rels):
    groups = {}
    for column, rel in enumerate(rels):
        groups.setdefault(rel * heads // ctx, []).append(column)
    groups = [groups[key] for key in sorted(groups)]
    size = len(groups[0])
    targets = {}
    for c in range(ctx):
        for h in range(heads):
            found = {}
            for d, step in enumerate((0, PAIR)):
                for g, columns in enumerate(groups):
                    to = (c ^ step) * heads + (c ^ rels[columns[0]]) * heads // ctx
                    found[to] = d * len(groups) + g
            targets[c * heads + h] = found
    classes = {}
    for device in sorted(targets):
        classes.setdefault(tuple(sorted(targets[device])), []).append(device)
    steps = 2 * len(groups)
    perms = [[] for _ in range(steps)]
    send = np.zeros((ctx * heads, steps), np.int32)
    arrives = {}
    for ends, sources in classes.items():
        for i, source in enumerate(sources):
            for k in range(steps):
                to = ends[i ^ k]
                perms[k].append((source, to))
                send[source, k] = targets[source][to]
                arrives[to, source] = k
    place = np.zeros((ctx * heads, ctx), np.int32)
    for c in range(ctx):
        for h in range(heads):
            for p in range(ctx):
                column_ctx, source_h = divmod(h * ctx + p, heads)
                source_c = (c & ~PAIR) | (column_ctx & PAIR)
                k = arrives[c * heads + h, source_c * heads + source_h]
                rel = source_c ^ column_ctx
                group = [g for g in groups if rels.index(rel) in g][0]
                place[c * heads + h, p] = k * size + group.index(rels.index(rel))
    return groups, perms, send, place


def body(ctx, heads, queries, keys, values, query_map, key_map, out_weight, residual):
    rows = queries.shape[0]
    heads_here, head_size, feat_half = query_map.shape
    feat_size = 2 * feat_half
    half = heads_here // 2
    wide = half * head_size
    depth = out_weight.shape[0] // heads
    strip_width = out_weight.shape[1]
    c = lax.axis_index("ctx")
    h = lax.axis_index("head")
    me = c * heads + h
    odd = c & 1

    def swap(x, by_ctx, by_head=0, keep=lambda c: True):
        pairs = [
            (i * heads + j, (i ^ by_ctx) * heads + (j ^ by_head))
            for i in range(ctx)
            for j in range(heads)
            if keep(i)
        ]
        return lax.ppermute(x, AXES, pairs)

    def of(*shape):
        return jax.ShapeDtypeStruct(shape, jnp.float32)

    def cost(products, count, exps=0):
        return pl.CostEstimate(flops=2 * products, bytes_accessed=4 * count, transcendentals=exps)

    params = pltpu.CompilerParams(vmem_limit_bytes=VMEM_LIMIT)
    streaming = pltpu.CompilerParams(vmem_limit_bytes=60 * 1024 * 1024)
    column_block = pl.BlockSpec((rows, head_size), lambda i, first: (0, first[0] * half + i))
    map_block = pl.BlockSpec((1, head_size, feat_half), lambda i, first: (first[0] * half + i, 0, 0))

    def head_block(size, lanes):
        return pl.BlockSpec((1, size, lanes), lambda i, *_: (i, 0, 0))

    def key_part(first):
        columns = pl.BlockSpec((rows, wide), lambda i, first: (0, first[0]))
        maps = pl.BlockSpec((half, head_size, feat_half), lambda i, first: (first[0], 0, 0))
        shapes = [of(half, feat_size + EXTRA, head_size), of(half, rows, feat_size)]
        return pl.pallas_call(
            key_kernel,
            grid_spec=pltpu.PrefetchScalarGridSpec(
                num_scalar_prefetch=1,
                grid=(1,),
                in_specs=[columns, maps, columns],
                out_specs=[pl.BlockSpec(s.shape, lambda i, first: (0, 0, 0)) for s in shapes],
            ),
            out_shape=shapes,
            compiler_params=streaming,
            name="key_part",
            cost_estimate=cost(
                6 * half * rows * head_size * (feat_half + feat_size),
                half * rows * (2 * head_size + 2 * feat_size),
                half * rows * feat_size,
            ),
        )(first, keys, key_map, values)

    def query_part(first, feat):
        return pl.pallas_call(
            query_kernel,
            grid_spec=pltpu.PrefetchScalarGridSpec(
                num_scalar_prefetch=1,
                grid=(half,),
                in_specs=[column_block, map_block, head_block(rows, feat_size), column_block],
                out_specs=[head_block(rows, feat_size), head_block(rows, head_size), head_block(rows, head_size)],
            ),
            out_shape=[of(half, rows, feat_size), of(half, rows, head_size), of(half, rows, head_size)],
            compiler_params=params,
            name="query_part",
            cost_estimate=cost(
                6 * half * rows * (head_size * feat_half + rows * (feat_size + head_size)),
                half * rows * (4 * head_size + 2 * feat_size),
                half * rows * feat_size,
            ),
        )(first, queries, query_map, feat, values)

    def mix(qfeat, numer, denom, prior):
        return pl.pallas_call(
            mix_kernel,
            grid=(half,),
            in_specs=[
                head_block(rows, feat_size),
                head_block(rows, head_size),
                head_block(rows, head_size),
                head_block(feat_size + EXTRA, head_size),
            ],
            out_specs=pl.BlockSpec((rows, head_size), lambda i: (0, i)),
            out_shape=of(rows, wide),
            compiler_params=params,
            name="mix",
            cost_estimate=cost(
                3 * half * rows * feat_size * head_size, half * rows * (3 * head_size + 2 * feat_size)
            ),
        )(qfeat, numer, denom, prior)

    even = range(0, heads, 2)
    blocks = heads // 2
    units = 2 * blocks

    def unit_rows(flip):
        starts = [(h ^ flip ^ d) * depth + half_here * wide for half_here in (odd, 1 - odd) for d in even]
        return jnp.concatenate([lax.dynamic_slice_in_dim(out_weight, start, wide, 0) for start in starts])

    kept, given = unit_rows(0), unit_rows(1)
    taken = swap(given, 0, 1)
    bits = [1 << b for b in reversed(range(ctx.bit_length() - 1)) if 1 << b != PAIR]
    rels = [0]
    for bit in bits[:-2]:
        kept = jnp.concatenate([kept, swap(kept, bit)], axis=1)
        taken = jnp.concatenate([taken, swap(taken, bit)], axis=1)
        rels = rels + [r | bit for r in rels]
    far, near = bits[-2:]
    rels = [r | s for s in (0, near, far, far | near) for r in rels]
    taken_far = swap(taken, far)

    own, other = odd.reshape(1), (1 - odd).reshape(1)
    other_state, other_feat = key_part(other)
    from_neighbour = swap(other_state, 1)
    own_state, own_feat = key_part(own)
    taken, from_neighbour = together((taken, from_neighbour))
    taken_near = swap(taken, near)

    earlier = jnp.where(odd == 0, own_state, from_neighbour)
    total = own_state + from_neighbour
    before = jnp.zeros_like(total)
    bit = 2
    while bit < ctx:
        if 2 * bit < ctx:
            got = swap(total, bit)
        else:
            total, taken_far, taken_near = together((total, taken_far, taken_near))
            got = swap(total, bit, keep=lambda i: not i & bit)
        before = before + jnp.where((c & bit) != 0, got, 0.0)
        total = total + got
        bit *= 2
    kept, taken_near = together((kept, taken_near))
    kept_near = swap(kept, near)
    own_query = query_part(own, own_feat)
    other_query = query_part(other, other_feat)
    before, kept, kept_near, own_query, other_query = together((before, kept, kept_near, own_query, other_query))

    ends = [0, 1, units - 1, units]
    sent = [kept[ends[i] * wide : ends[i + 1] * wide] for i in range(3)]
    kept_far = [swap(sent[0], far)]
    own_prior = before + jnp.where(odd == 1, earlier, 0.0)
    other_prior = swap(before + jnp.where(odd == 0, earlier, 0.0), 1)

    def spread(pieces, bits):
        for bit in bits:
            pieces.update({(d, j | bit): swap(pieces[d, j], 0, bit) for d, j in list(pieces) if not j & bit})
        return [pieces[d, j] for d in (0, PAIR) for j in even]

    head_bits = [1 << b for b in range(1, heads.bit_length() - 1)]
    own_mixed = mix(*own_query, own_prior)
    met = swap(own_mixed, PAIR)
    across = swap(own_mixed, 0, head_bits[0])
    other_prior, kept_far[0], taken_far, met, across, sent[1] = together(
        (other_prior, kept_far[0], taken_far, met, across, sent[1])
    )
    taken_both = swap(taken_far, near)
    kept_both = [swap(kept_far[0], near)]
    kept_far.append(swap(sent[1], far))
    own_pieces = {(0, 0): own_mixed, (PAIR, 0): met, (0, head_bits[0]): across}
    own_pieces[PAIR, head_bits[0]] = swap(met, 0, head_bits[0])
    own_pieces = spread(own_pieces, head_bits[1:])
    other_mixed = mix(*other_query, other_prior)
    met = swap(other_mixed, PAIR)
    across = swap(other_mixed, 0, head_bits[0])
    met, across, kept_far[1], taken_both, sent[2] = together((met, across, kept_far[1], taken_both, sent[2]))
    kept_far.append(swap(sent[2], far))
    kept_both.append(swap(kept_far[1], near))
    other_pieces = {(0, 0): other_mixed, (PAIR, 0): met, (0, head_bits[0]): across}
    other_pieces[PAIR, head_bits[0]] = swap(met, 0, head_bits[0])
    other_pieces = spread(other_pieces, head_bits[1:])

    lanes = kept.shape[1]

    def strip(parts, crossed):
        places = [(part, i) for part in parts for i in range(part.shape[0] // wide)]
        return [places[(u + blocks * crossed) % units] for u in range(units)]

    def project(halves, strips, total=None):
        flat, weights, weight_specs = [[], []], [], []
        for which, pieces in halves:
            flat[0] += pieces[:blocks]
            flat[1] += pieces[blocks:]
            for j in range(blocks):
                for places in strips:
                    part, unit = places[which * blocks + j]
                    weights.append(part)
                    weight_specs.append(pl.BlockSpec((wide, lanes), lambda i, unit=unit: (unit, 0)))
        count = len(flat[0])
        out_block = pl.BlockSpec((2 * rows, len(strips) * lanes), lambda i: (0, 0))
        extra = [] if total is None else [total]
        return pl.pallas_call(
            functools.partial(project_kernel, count, len(strips)),
            grid=(1,),
            in_specs=[pl.BlockSpec((rows, wide), lambda i: (0, 0))] * (2 * count)
            + weight_specs
            + [out_block] * len(extra),
            out_specs=out_block,
            out_shape=of(2 * rows, len(strips) * lanes),
            compiler_params=params,
            name="project",
            cost_estimate=cost(
                3 * 2 * rows * wide * count * len(strips) * lanes, wide * count * (2 * rows + len(strips) * lanes)
            ),
        )(*flat[0], *flat[1], *weights, *extra)

    theirs = [strip([taken], 0), strip([taken_near], 1), strip([taken_far], 0), strip([taken_both], 1)]
    mine = [strip([kept], 0), strip([kept_near], 1)]
    for_them = project([(0, own_pieces)], theirs)
    mine_near = project([(0, own_pieces)], mine)
    for_them, mine_near, kept_far, kept_both = together((for_them, mine_near, kept_far, kept_both))
    kept_both.append(swap(kept_far[-1], near))
    for_them = project([(1, other_pieces)], theirs, for_them)
    from_them = swap(for_them, 0, 1)
    mine_near = project([(1, other_pieces)], mine, mine_near)
    mine_far = project([(0, own_pieces), (1, other_pieces)], [strip(kept_far, 0), strip(kept_both, 1)])

    groups, perms, send, place = route_tables(ctx, heads, rels)
    steps, size = len(perms), len(groups[0])
    send_here = jnp.asarray(send)[me]
    place_here = jnp.asarray(place)[me]
    if strip_width % 128 == 0:
        parts = pl.pallas_call(
            functools.partial(route_kernel, groups, strip_width),
            grid_spec=pltpu.PrefetchScalarGridSpec(
                num_scalar_prefetch=1,
                grid=(1,),
                in_specs=[pl.BlockSpec(x.shape, lambda i, send: (0, 0)) for x in (mine_near, mine_far, from_them)],
                out_specs=[pl.BlockSpec((rows, size * strip_width), lambda i, send: (0, 0))] * steps,
                scratch_shapes=[pltpu.VMEM((steps, rows, size * strip_width), jnp.float32)],
            ),
            out_shape=[of(rows, size * strip_width)] * steps,
            compiler_params=params,
            name="route",
            cost_estimate=cost(0, 6 * rows * steps * size * strip_width),
        )(send_here, mine_near, mine_far, from_them)
    else:
        product = jnp.concatenate([mine_near, mine_far], axis=1) + from_them
        parts = jnp.stack(pieces_of(product, groups, strip_width))
        parts = [lax.dynamic_index_in_dim(parts, send_here[k], 0, False) for k in range(steps)]
    arrived = [lax.ppermute(part, AXES, perm) for part, perm in zip(parts, perms)]
    if strip_width % 128 == 0:
        return pl.pallas_call(
            functools.partial(assemble_kernel, size),
            grid_spec=pltpu.PrefetchScalarGridSpec(
                num_scalar_prefetch=1,
                grid=(1,),
                in_specs=[pl.BlockSpec(x.shape, lambda i, place: (0, 0)) for x in (*arrived, residual)],
                out_specs=pl.BlockSpec(residual.shape, lambda i, place: (0, 0)),
                scratch_shapes=[pltpu.VMEM((ctx, rows, strip_width), jnp.float32)],
            ),
            out_shape=of(*residual.shape),
            compiler_params=params,
            name="assemble",
            cost_estimate=cost(0, 3 * residual.size),
        )(place_here, *arrived, residual)
    blocks = jnp.stack([a[:, b * strip_width : (b + 1) * strip_width] for a in arrived for b in range(size)])
    projected = [lax.dynamic_index_in_dim(blocks, place_here[p], 0, False) for p in range(ctx)]
    return residual + jnp.concatenate(projected, axis=1)


def solution(mesh):
    placed = (
        P("ctx", "head"),
        P("ctx", "head"),
        P("ctx", "head"),
        P("head", None, None),
        P("head", None, None),
        P(None, ("ctx", "head")),
        P("ctx", "head"),
    )
    return jax.shard_map(
        functools.partial(body, mesh.shape["ctx"], mesh.shape["head"]),
        mesh=mesh,
        in_specs=placed,
        out_specs=P("ctx", "head"),
        check_vma=False,
    )
```

```python
import functools

import numpy as np

import jax
import jax.numpy as jnp
from jax import lax
from jax.experimental import pallas as pl
from jax.experimental.pallas import tpu as pltpu
from jax.sharding import PartitionSpec as P

HIGH = lax.Precision.HIGHEST
together = lax.optimization_barrier
AXES = ("ctx", "head")
PAIR = 2
EXTRA = 8
VMEM_LIMIT = 32 * 1024 * 1024


def split(x):
    high = x.astype(jnp.bfloat16)
    return high, (x - high.astype(jnp.float32)).astype(jnp.bfloat16)


def dot3(a, b, dims=(((1,), (0,)), ((), ()))):
    a_high, a_low = split(a)
    b_high, b_low = split(b)
    dot = functools.partial(lax.dot_general, dimension_numbers=dims, preferred_element_type=jnp.float32)
    return dot(a_high, b_high) + (dot(a_high, b_low) + dot(a_low, b_high))


def features(rows, weights):
    scores = jnp.dot(rows, weights, precision=HIGH, preferred_element_type=jnp.float32)
    up = jnp.exp(scores - jnp.max(scores, axis=-1, keepdims=True))
    down = jnp.exp(jnp.min(scores, axis=-1, keepdims=True) - scores)
    up = up / jnp.sum(up, axis=-1, keepdims=True)
    down = down / jnp.sum(down, axis=-1, keepdims=True)
    return jnp.concatenate([up, down], axis=-1)


def key_kernel(first, k_ref, map_ref, v_ref, state_ref, feat_ref):
    heads, head_size, feat_half = map_ref.shape
    size = 2 * feat_half
    row = lax.broadcasted_iota(jnp.int32, (EXTRA, feat_half), 0)
    for i in range(heads):
        columns = slice(i * head_size, (i + 1) * head_size)
        feat = features(k_ref[:, columns], map_ref[i])
        feat_ref[i] = feat
        state_ref[i, :size, :] = dot3(feat, v_ref[:, columns], (((0,), (0,)), ((), ())))
        norm = jnp.sum(feat, axis=0, keepdims=True)
        state_ref[i, size:, :] = jnp.where(row < EXTRA // 2, norm[:, :feat_half], norm[:, feat_half:])


def query_kernel(first, q_ref, map_ref, feat_ref, v_ref, qfeat_ref, numer_ref, denom_ref):
    feat = features(q_ref[...], map_ref[0])
    qfeat_ref[0] = feat
    weights = dot3(feat, feat_ref[0], (((1,), (1,)), ((), ())))
    row = lax.broadcasted_iota(jnp.int32, weights.shape, 0)
    column = lax.broadcasted_iota(jnp.int32, weights.shape, 1)
    weights = jnp.where(column <= row, weights, 0.0)
    numer_ref[0] = dot3(weights, v_ref[...])
    denom_ref[0] = jnp.broadcast_to(jnp.sum(weights, axis=-1, keepdims=True), denom_ref.shape[1:])


def mix_kernel(qfeat_ref, numer_ref, denom_ref, prior_ref, out_ref):
    feat = qfeat_ref[0]
    size = feat.shape[1]
    norm = jnp.concatenate(
        [prior_ref[0, size : size + 1, :], prior_ref[0, size + EXTRA // 2 : size + EXTRA // 2 + 1, :]], axis=1
    )
    denom = denom_ref[0] + jnp.sum(feat * norm, axis=-1, keepdims=True)
    out_ref[...] = (numer_ref[0] + dot3(feat, prior_ref[0, :size, :])) / denom


def project_kernel(count, strips, *refs):
    a_refs, b_refs, w_refs = refs[:count], refs[count : 2 * count], refs[2 * count : (2 + strips) * count]
    rest, out_ref = refs[(2 + strips) * count : -1], refs[-1]
    total = rest[0][...] if rest else None
    for i in range(count):
        a = jnp.concatenate([a_refs[i][...], b_refs[i][...]], axis=0)
        w = jnp.concatenate([ref[...] for ref in w_refs[i * strips : (i + 1) * strips]], axis=1)
        part = dot3(a, w)
        total = part if total is None else total + part
    out_ref[...] = total


def pieces_of(product, groups, width):
    rows = product.shape[0] // 2
    return [
        jnp.concatenate([product[d * rows : (d + 1) * rows, b * width : (b + 1) * width] for b in group], axis=1)
        for d in range(2)
        for group in groups
    ]


def route_kernel(groups, width, send, near_ref, far_ref, other_ref, *refs):
    out_refs, pieces_ref = refs[:-1], refs[-1]
    product = jnp.concatenate([near_ref[...], far_ref[...]], axis=1) + other_ref[...]
    for j, piece in enumerate(pieces_of(product, groups, width)):
        pieces_ref[j] = piece
    for k, out_ref in enumerate(out_refs):
        out_ref[...] = pieces_ref[send[k]]


def assemble_kernel(size, place, *refs):
    arrived, (residual_ref, out_ref, blocks_ref) = refs[:-3], refs[-3:]
    width = blocks_ref.shape[2]
    for k, ref in enumerate(arrived):
        for b in range(size):
            blocks_ref[k * size + b] = ref[:, b * width : (b + 1) * width]
    for p in range(blocks_ref.shape[0]):
        columns = slice(p * width, (p + 1) * width)
        out_ref[:, columns] = residual_ref[:, columns] + blocks_ref[place[p]]


def route_tables(ctx, heads, rels):
    groups = {}
    for column, rel in enumerate(rels):
        groups.setdefault(rel * heads // ctx, []).append(column)
    groups = [groups[key] for key in sorted(groups)]
    size = len(groups[0])
    targets = {}
    for c in range(ctx):
        for h in range(heads):
            found = {}
            for d, step in enumerate((0, PAIR)):
                for g, columns in enumerate(groups):
                    to = (c ^ step) * heads + (c ^ rels[columns[0]]) * heads // ctx
                    found[to] = d * len(groups) + g
            targets[c * heads + h] = found
    classes = {}
    for device in sorted(targets):
        classes.setdefault(tuple(sorted(targets[device])), []).append(device)
    steps = 2 * len(groups)
    perms = [[] for _ in range(steps)]
    send = np.zeros((ctx * heads, steps), np.int32)
    arrives = {}
    for ends, sources in classes.items():
        for i, source in enumerate(sources):
            for k in range(steps):
                to = ends[i ^ k]
                perms[k].append((source, to))
                send[source, k] = targets[source][to]
                arrives[to, source] = k
    place = np.zeros((ctx * heads, ctx), np.int32)
    for c in range(ctx):
        for h in range(heads):
            for p in range(ctx):
                column_ctx, source_h = divmod(h * ctx + p, heads)
                source_c = (c & ~PAIR) | (column_ctx & PAIR)
                k = arrives[c * heads + h, source_c * heads + source_h]
                rel = source_c ^ column_ctx
                group = [g for g in groups if rels.index(rel) in g][0]
                place[c * heads + h, p] = k * size + group.index(rels.index(rel))
    return groups, perms, send, place


def body(ctx, heads, queries, keys, values, query_map, key_map, out_weight, residual):
    rows = queries.shape[0]
    heads_here, head_size, feat_half = query_map.shape
    feat_size = 2 * feat_half
    half = heads_here // 2
    wide = half * head_size
    depth = out_weight.shape[0] // heads
    strip_width = out_weight.shape[1]
    c = lax.axis_index("ctx")
    h = lax.axis_index("head")
    me = c * heads + h
    odd = c & 1

    def swap(x, by_ctx, by_head=0, keep=lambda c: True):
        pairs = [
            (i * heads + j, (i ^ by_ctx) * heads + (j ^ by_head))
            for i in range(ctx)
            for j in range(heads)
            if keep(i)
        ]
        return lax.ppermute(x, AXES, pairs)

    def of(*shape):
        return jax.ShapeDtypeStruct(shape, jnp.float32)

    def cost(products, count, exps=0):
        return pl.CostEstimate(flops=2 * products, bytes_accessed=4 * count, transcendentals=exps)

    params = pltpu.CompilerParams(vmem_limit_bytes=VMEM_LIMIT)
    streaming = pltpu.CompilerParams(vmem_limit_bytes=60 * 1024 * 1024)
    column_block = pl.BlockSpec((rows, head_size), lambda i, first: (0, first[0] * half + i))
    map_block = pl.BlockSpec((1, head_size, feat_half), lambda i, first: (first[0] * half + i, 0, 0))

    def head_block(size, lanes):
        return pl.BlockSpec((1, size, lanes), lambda i, *_: (i, 0, 0))

    def key_part(first):
        columns = pl.BlockSpec((rows, wide), lambda i, first: (0, first[0]))
        maps = pl.BlockSpec((half, head_size, feat_half), lambda i, first: (first[0], 0, 0))
        shapes = [of(half, feat_size + EXTRA, head_size), of(half, rows, feat_size)]
        return pl.pallas_call(
            key_kernel,
            grid_spec=pltpu.PrefetchScalarGridSpec(
                num_scalar_prefetch=1,
                grid=(1,),
                in_specs=[columns, maps, columns],
                out_specs=[pl.BlockSpec(s.shape, lambda i, first: (0, 0, 0)) for s in shapes],
            ),
            out_shape=shapes,
            compiler_params=streaming,
            name="key_part",
            cost_estimate=cost(
                6 * half * rows * head_size * (feat_half + feat_size),
                half * rows * (2 * head_size + 2 * feat_size),
                half * rows * feat_size,
            ),
        )(first, keys, key_map, values)

    def query_part(first, feat):
        return pl.pallas_call(
            query_kernel,
            grid_spec=pltpu.PrefetchScalarGridSpec(
                num_scalar_prefetch=1,
                grid=(half,),
                in_specs=[column_block, map_block, head_block(rows, feat_size), column_block],
                out_specs=[head_block(rows, feat_size), head_block(rows, head_size), head_block(rows, head_size)],
            ),
            out_shape=[of(half, rows, feat_size), of(half, rows, head_size), of(half, rows, head_size)],
            compiler_params=params,
            name="query_part",
            cost_estimate=cost(
                6 * half * rows * (head_size * feat_half + rows * (feat_size + head_size)),
                half * rows * (4 * head_size + 2 * feat_size),
                half * rows * feat_size,
            ),
        )(first, queries, query_map, feat, values)

    def mix(qfeat, numer, denom, prior):
        return pl.pallas_call(
            mix_kernel,
            grid=(half,),
            in_specs=[
                head_block(rows, feat_size),
                head_block(rows, head_size),
                head_block(rows, head_size),
                head_block(feat_size + EXTRA, head_size),
            ],
            out_specs=pl.BlockSpec((rows, head_size), lambda i: (0, i)),
            out_shape=of(rows, wide),
            compiler_params=params,
            name="mix",
            cost_estimate=cost(
                3 * half * rows * feat_size * head_size, half * rows * (3 * head_size + 2 * feat_size)
            ),
        )(qfeat, numer, denom, prior)

    even = range(0, heads, 2)
    blocks = heads // 2
    quarter = 2 * blocks // 4 * wide
    bits = [1 << b for b in reversed(range(ctx.bit_length() - 1)) if 1 << b != PAIR]
    far, near = bits[-2:]
    rels = [0]
    for bit in bits[:-2]:
        rels = rels + [r | bit for r in rels]
    rels = [r | s for s in (0, near, far, far | near) for r in rels]

    def rows_of(weight, flip, halves):
        starts = [(h ^ flip ^ d) * depth + which * wide for which in halves for d in even]
        return jnp.concatenate([lax.dynamic_slice_in_dim(weight, start, wide, 0) for start in starts])

    def widen(x):
        for bit in bits[:-2]:
            x = jnp.concatenate([x, swap(x, bit)], axis=1)
        return x

    def quarters(x):
        return [x[i : i + quarter] for i in range(0, x.shape[0], quarter)]

    own, other = odd.reshape(1), (1 - odd).reshape(1)
    kept_own = widen(rows_of(out_weight, 0, [odd]))
    far_1 = swap(kept_own, far)
    other_state, other_feat = key_part(other)
    out_weight, other_state = together((out_weight, other_state))
    kept_other = widen(rows_of(out_weight, 0, [1 - odd]))
    taken = widen(swap(rows_of(out_weight, 1, [odd, 1 - odd]), 0, 1))
    from_neighbour = swap(other_state, 1)
    own_state, own_feat = key_part(own)

    from_neighbour, own_state, far_1, kept_own, kept_other, taken = together(
        (from_neighbour, own_state, far_1, kept_own, kept_other, taken)
    )
    kept_near = [swap(kept_own, near), swap(kept_other, near)]
    taken_parts = quarters(taken)
    far_2 = swap(jnp.concatenate(taken_parts[:2]), far)
    earlier = jnp.where(odd == 0, own_state, from_neighbour)
    total = own_state + from_neighbour
    before = jnp.zeros_like(total)
    bit = 2
    while 2 * bit < ctx:
        got = swap(total, bit)
        before = before + jnp.where((c & bit) != 0, got, 0.0)
        total = total + got
        bit *= 2
    total, before, far_2, kept_near, taken, own_feat, other_feat = together(
        (total, before, far_2, kept_near, taken, own_feat, other_feat)
    )
    taken_near = swap(taken, near)
    second = (c & PAIR) != 0
    middle = half // 2
    got = swap(jnp.where(second, total[middle:], total[:middle]), bit, keep=lambda i: not i & bit)
    met = swap(got, PAIR, keep=lambda i: i & bit)
    own_query, other_query = query_part(own, own_feat), query_part(other, other_feat)
    got = jnp.concatenate([jnp.where(second, met, got), jnp.where(second, got, met)])
    got, taken_near, own_query, other_query, taken_parts[2] = together(
        (got, taken_near, own_query, other_query, taken_parts[2])
    )
    before = before + got

    other_prior = swap(before + jnp.where(odd == 0, earlier, 0.0), 1)
    own_mixed = mix(*own_query, before + jnp.where(odd == 1, earlier, 0.0))
    head_bits = [1 << b for b in range(1, heads.bit_length() - 1)]

    def spread(own, met, across, last):
        pieces = {(0, 0): own, (PAIR, 0): met, (0, head_bits[0]): across, (PAIR, head_bits[0]): last}
        for bit in head_bits[1:]:
            pieces.update({(d, j | bit): swap(pieces[d, j], 0, bit) for d, j in list(pieces)})
        return [pieces[d, j] for d in (0, PAIR) for j in even]

    met, across = swap(own_mixed, PAIR), swap(own_mixed, 0, head_bits[0])
    far_3 = swap(taken_parts[2], far)
    kept_parts = quarters(kept_other)
    next_part = jnp.concatenate([taken_parts[3], kept_parts[0]])
    other_prior, far_1, far_2, far_3, met, across, next_part = together(
        (other_prior, far_1, far_2, far_3, met, across, next_part)
    )
    own_pieces = spread(own_mixed, met, across, swap(met, 0, head_bits[0]))
    other_mixed = mix(*other_query, other_prior)
    met, across = swap(other_mixed, PAIR), swap(other_mixed, 0, head_bits[0])
    far_4 = swap(next_part, far)
    both_1 = swap(jnp.concatenate([far_1, far_2, far_3]), near)
    met, across, far_4, both_1, kept_parts[1] = together((met, across, far_4, both_1, kept_parts[1]))
    far_5 = swap(kept_parts[1], far)
    both_2 = swap(far_4, near)
    other_pieces = spread(other_mixed, met, across, swap(met, 0, head_bits[0]))

    lanes = kept_own.shape[1]

    def strip(parts, crossed=False):
        places = [(part, i) for part in parts for i in range(part.shape[0] // wide)]
        return places[blocks:] + places[:blocks] if crossed else places

    def part_of(x, i):
        return [(x, j) for j in range(i * quarter // wide, (i + 1) * quarter // wide)]

    def joined(places, crossed=False):
        return places[blocks:] + places[:blocks] if crossed else places

    def project(halves, strips, total=None):
        flat, weights, weight_specs = [[], []], [], []
        for which, pieces in halves:
            flat[0] += pieces[:blocks]
            flat[1] += pieces[blocks:]
            for j in range(blocks):
                for places in strips:
                    part, unit = places[which * blocks + j]
                    weights.append(part)
                    weight_specs.append(pl.BlockSpec((wide, lanes), lambda i, unit=unit: (unit, 0)))
        count = len(flat[0])
        out_block = pl.BlockSpec((2 * rows, len(strips) * lanes), lambda i: (0, 0))
        extra = [] if total is None else [total]
        return pl.pallas_call(
            functools.partial(project_kernel, count, len(strips)),
            grid=(1,),
            in_specs=[pl.BlockSpec((rows, wide), lambda i: (0, 0))] * (2 * count)
            + weight_specs
            + [out_block] * len(extra),
            out_specs=out_block,
            out_shape=of(2 * rows, len(strips) * lanes),
            compiler_params=params,
            name="project",
            cost_estimate=cost(
                3 * 2 * rows * wide * count * len(strips) * lanes, wide * count * (2 * rows + len(strips) * lanes)
            ),
        )(*flat[0], *flat[1], *weights, *extra)

    theirs = [
        strip([taken]),
        strip([taken_near], True),
        strip([far_2, far_3]) + part_of(far_4, 0),
        joined(strip([both_1])[blocks:] + part_of(both_2, 0), True),
    ]
    mine = [strip([kept_own, kept_other]), strip(kept_near, True)]
    for_them = project([(0, own_pieces)], theirs)
    mine_near = project([(0, own_pieces)], mine)
    for_them, mine_near, far_5 = together((for_them, mine_near, far_5))
    both_3 = swap(far_5, near)
    for_them = project([(1, other_pieces)], theirs, for_them)
    from_them = swap(for_them, 0, 1)
    mine_near = project([(1, other_pieces)], mine, mine_near)
    mine_far = [
        strip([far_1]) + part_of(far_4, 1) + strip([far_5]),
        joined(strip([both_1])[:blocks] + part_of(both_2, 1) + strip([both_3]), True),
    ]
    mine_far = project([(0, own_pieces), (1, other_pieces)], mine_far)

    groups, perms, send, place = route_tables(ctx, heads, rels)
    steps, size = len(perms), len(groups[0])
    send_here = jnp.asarray(send)[me]
    place_here = jnp.asarray(place)[me]
    if strip_width % 128 == 0:
        parts = pl.pallas_call(
            functools.partial(route_kernel, groups, strip_width),
            grid_spec=pltpu.PrefetchScalarGridSpec(
                num_scalar_prefetch=1,
                grid=(1,),
                in_specs=[pl.BlockSpec(x.shape, lambda i, send: (0, 0)) for x in (mine_near, mine_far, from_them)],
                out_specs=[pl.BlockSpec((rows, size * strip_width), lambda i, send: (0, 0))] * steps,
                scratch_shapes=[pltpu.VMEM((steps, rows, size * strip_width), jnp.float32)],
            ),
            out_shape=[of(rows, size * strip_width)] * steps,
            compiler_params=params,
            name="route",
            cost_estimate=cost(0, 6 * rows * steps * size * strip_width),
        )(send_here, mine_near, mine_far, from_them)
    else:
        product = jnp.concatenate([mine_near, mine_far], axis=1) + from_them
        parts = jnp.stack(pieces_of(product, groups, strip_width))
        parts = [lax.dynamic_index_in_dim(parts, send_here[k], 0, False) for k in range(steps)]
    arrived = [lax.ppermute(part, AXES, perm) for part, perm in zip(parts, perms)]
    if strip_width % 128 == 0:
        return pl.pallas_call(
            functools.partial(assemble_kernel, size),
            grid_spec=pltpu.PrefetchScalarGridSpec(
                num_scalar_prefetch=1,
                grid=(1,),
                in_specs=[pl.BlockSpec(x.shape, lambda i, place: (0, 0)) for x in (*arrived, residual)],
                out_specs=pl.BlockSpec(residual.shape, lambda i, place: (0, 0)),
                scratch_shapes=[pltpu.VMEM((ctx, rows, strip_width), jnp.float32)],
            ),
            out_shape=of(*residual.shape),
            compiler_params=params,
            name="assemble",
            cost_estimate=cost(0, 3 * residual.size),
        )(place_here, *arrived, residual)
    blocks = jnp.stack([a[:, b * strip_width : (b + 1) * strip_width] for a in arrived for b in range(size)])
    projected = [lax.dynamic_index_in_dim(blocks, place_here[p], 0, False) for p in range(ctx)]
    return residual + jnp.concatenate(projected, axis=1)


def solution(mesh):
    placed = (
        P("ctx", "head"),
        P("ctx", "head"),
        P("ctx", "head"),
        P("head", None, None),
        P("head", None, None),
        P(None, ("ctx", "head")),
        P("ctx", "head"),
    )
    return jax.shard_map(
        functools.partial(body, mesh.shape["ctx"], mesh.shape["head"]),
        mesh=mesh,
        in_specs=placed,
        out_specs=P("ctx", "head"),
        check_vma=False,
    )
```

```python
import functools

import numpy as np

import jax
import jax.numpy as jnp
from jax import lax
from jax.experimental import pallas as pl
from jax.experimental.pallas import tpu as pltpu
from jax.sharding import PartitionSpec as P

HIGH = lax.Precision.HIGHEST
together = lax.optimization_barrier
AXES = ("ctx", "head")
PAIR = 2
EXTRA = 8
VMEM_LIMIT = 32 * 1024 * 1024


def split(x):
    high = x.astype(jnp.bfloat16)
    return high, (x - high.astype(jnp.float32)).astype(jnp.bfloat16)


def dot3(a, b, dims=(((1,), (0,)), ((), ()))):
    a_high, a_low = split(a)
    b_high, b_low = split(b)
    dot = functools.partial(lax.dot_general, dimension_numbers=dims, preferred_element_type=jnp.float32)
    return dot(a_high, b_high) + (dot(a_high, b_low) + dot(a_low, b_high))


def features(rows, weights):
    scores = jnp.dot(rows, weights, precision=HIGH, preferred_element_type=jnp.float32)
    up = jnp.exp(scores - jnp.max(scores, axis=-1, keepdims=True))
    down = jnp.exp(jnp.min(scores, axis=-1, keepdims=True) - scores)
    up = up / jnp.sum(up, axis=-1, keepdims=True)
    down = down / jnp.sum(down, axis=-1, keepdims=True)
    return jnp.concatenate([up, down], axis=-1)


def key_kernel(first, k_ref, map_ref, v_ref, state_ref, feat_ref):
    heads, head_size, feat_half = map_ref.shape
    size = 2 * feat_half
    row = lax.broadcasted_iota(jnp.int32, (EXTRA, feat_half), 0)
    for i in range(heads):
        columns = slice(i * head_size, (i + 1) * head_size)
        feat = features(k_ref[:, columns], map_ref[i])
        feat_ref[i] = feat
        state_ref[i, :size, :] = dot3(feat, v_ref[:, columns], (((0,), (0,)), ((), ())))
        norm = jnp.sum(feat, axis=0, keepdims=True)
        state_ref[i, size:, :] = jnp.where(row < EXTRA // 2, norm[:, :feat_half], norm[:, feat_half:])


def query_kernel(first, q_ref, map_ref, feat_ref, v_ref, qfeat_ref, numer_ref, denom_ref):
    feat = features(q_ref[...], map_ref[0])
    qfeat_ref[0] = feat
    weights = dot3(feat, feat_ref[0], (((1,), (1,)), ((), ())))
    row = lax.broadcasted_iota(jnp.int32, weights.shape, 0)
    column = lax.broadcasted_iota(jnp.int32, weights.shape, 1)
    weights = jnp.where(column <= row, weights, 0.0)
    numer_ref[0] = dot3(weights, v_ref[...])
    denom_ref[0] = jnp.broadcast_to(jnp.sum(weights, axis=-1, keepdims=True), denom_ref.shape[1:])


def mix_kernel(qfeat_ref, numer_ref, denom_ref, prior_ref, out_ref):
    feat = qfeat_ref[0]
    size = feat.shape[1]
    norm = jnp.concatenate(
        [prior_ref[0, size : size + 1, :], prior_ref[0, size + EXTRA // 2 : size + EXTRA // 2 + 1, :]], axis=1
    )
    denom = denom_ref[0] + jnp.sum(feat * norm, axis=-1, keepdims=True)
    out_ref[...] = (numer_ref[0] + dot3(feat, prior_ref[0, :size, :])) / denom


def project_kernel(count, strips, *refs):
    a_refs, b_refs, w_refs = refs[:count], refs[count : 2 * count], refs[2 * count : (2 + strips) * count]
    rest, out_ref = refs[(2 + strips) * count : -1], refs[-1]
    total = rest[0][...] if rest else None
    for i in range(count):
        a = jnp.concatenate([a_refs[i][...], b_refs[i][...]], axis=0)
        w = jnp.concatenate([ref[...] for ref in w_refs[i * strips : (i + 1) * strips]], axis=1)
        part = dot3(a, w)
        total = part if total is None else total + part
    out_ref[...] = total


def pieces_of(product, groups, width):
    rows = product.shape[0] // 2
    return [
        jnp.concatenate([product[d * rows : (d + 1) * rows, b * width : (b + 1) * width] for b in group], axis=1)
        for d in range(2)
        for group in groups
    ]


def route_kernel(groups, width, send, near_ref, far_ref, other_ref, *refs):
    out_refs, pieces_ref = refs[:-1], refs[-1]
    product = jnp.concatenate([near_ref[...], far_ref[...]], axis=1) + other_ref[...]
    for j, piece in enumerate(pieces_of(product, groups, width)):
        pieces_ref[j] = piece
    for k, out_ref in enumerate(out_refs):
        out_ref[...] = pieces_ref[send[k]]


def assemble_kernel(size, place, *refs):
    arrived, (residual_ref, out_ref, blocks_ref) = refs[:-3], refs[-3:]
    width = blocks_ref.shape[2]
    for k, ref in enumerate(arrived):
        for b in range(size):
            blocks_ref[k * size + b] = ref[:, b * width : (b + 1) * width]
    for p in range(blocks_ref.shape[0]):
        columns = slice(p * width, (p + 1) * width)
        out_ref[:, columns] = residual_ref[:, columns] + blocks_ref[place[p]]


def route_tables(ctx, heads, rels):
    groups = {}
    for column, rel in enumerate(rels):
        groups.setdefault(rel * heads // ctx, []).append(column)
    groups = [groups[key] for key in sorted(groups)]
    size = len(groups[0])
    targets = {}
    for c in range(ctx):
        for h in range(heads):
            found = {}
            for d, step in enumerate((0, PAIR)):
                for g, columns in enumerate(groups):
                    to = (c ^ step) * heads + (c ^ rels[columns[0]]) * heads // ctx
                    found[to] = d * len(groups) + g
            targets[c * heads + h] = found
    classes = {}
    for device in sorted(targets):
        classes.setdefault(tuple(sorted(targets[device])), []).append(device)
    steps = 2 * len(groups)
    perms = [[] for _ in range(steps)]
    send = np.zeros((ctx * heads, steps), np.int32)
    arrives = {}
    for ends, sources in classes.items():
        for i, source in enumerate(sources):
            for k in range(steps):
                to = ends[i ^ k]
                perms[k].append((source, to))
                send[source, k] = targets[source][to]
                arrives[to, source] = k
    place = np.zeros((ctx * heads, ctx), np.int32)
    for c in range(ctx):
        for h in range(heads):
            for p in range(ctx):
                column_ctx, source_h = divmod(h * ctx + p, heads)
                source_c = (c & ~PAIR) | (column_ctx & PAIR)
                k = arrives[c * heads + h, source_c * heads + source_h]
                rel = source_c ^ column_ctx
                group = [g for g in groups if rels.index(rel) in g][0]
                place[c * heads + h, p] = k * size + group.index(rels.index(rel))
    return groups, perms, send, place


def body(ctx, heads, queries, keys, values, query_map, key_map, out_weight, residual):
    rows = queries.shape[0]
    heads_here, head_size, feat_half = query_map.shape
    feat_size = 2 * feat_half
    half = heads_here // 2
    wide = half * head_size
    depth = out_weight.shape[0] // heads
    strip_width = out_weight.shape[1]
    c = lax.axis_index("ctx")
    h = lax.axis_index("head")
    me = c * heads + h
    odd = c & 1

    def swap(x, by_ctx, by_head=0, keep=lambda c: True):
        pairs = [
            (i * heads + j, (i ^ by_ctx) * heads + (j ^ by_head))
            for i in range(ctx)
            for j in range(heads)
            if keep(i)
        ]
        return lax.ppermute(x, AXES, pairs)

    def of(*shape):
        return jax.ShapeDtypeStruct(shape, jnp.float32)

    def cost(products, count, exps=0):
        return pl.CostEstimate(flops=2 * products, bytes_accessed=4 * count, transcendentals=exps)

    params = pltpu.CompilerParams(vmem_limit_bytes=VMEM_LIMIT)
    streaming = pltpu.CompilerParams(vmem_limit_bytes=60 * 1024 * 1024)
    column_block = pl.BlockSpec((rows, head_size), lambda i, first: (0, first[0] * half + i))
    map_block = pl.BlockSpec((1, head_size, feat_half), lambda i, first: (first[0] * half + i, 0, 0))

    def head_block(size, lanes):
        return pl.BlockSpec((1, size, lanes), lambda i, *_: (i, 0, 0))

    def key_part(first):
        columns = pl.BlockSpec((rows, wide), lambda i, first: (0, first[0]))
        maps = pl.BlockSpec((half, head_size, feat_half), lambda i, first: (first[0], 0, 0))
        shapes = [of(half, feat_size + EXTRA, head_size), of(half, rows, feat_size)]
        return pl.pallas_call(
            key_kernel,
            grid_spec=pltpu.PrefetchScalarGridSpec(
                num_scalar_prefetch=1,
                grid=(1,),
                in_specs=[columns, maps, columns],
                out_specs=[pl.BlockSpec(s.shape, lambda i, first: (0, 0, 0)) for s in shapes],
            ),
            out_shape=shapes,
            compiler_params=streaming,
            name="key_part",
            cost_estimate=cost(
                6 * half * rows * head_size * (feat_half + feat_size),
                half * rows * (2 * head_size + 2 * feat_size),
                half * rows * feat_size,
            ),
        )(first, keys, key_map, values)

    def query_part(first, feat):
        return pl.pallas_call(
            query_kernel,
            grid_spec=pltpu.PrefetchScalarGridSpec(
                num_scalar_prefetch=1,
                grid=(half,),
                in_specs=[column_block, map_block, head_block(rows, feat_size), column_block],
                out_specs=[head_block(rows, feat_size), head_block(rows, head_size), head_block(rows, head_size)],
            ),
            out_shape=[of(half, rows, feat_size), of(half, rows, head_size), of(half, rows, head_size)],
            compiler_params=params,
            name="query_part",
            cost_estimate=cost(
                6 * half * rows * (head_size * feat_half + rows * (feat_size + head_size)),
                half * rows * (4 * head_size + 2 * feat_size),
                half * rows * feat_size,
            ),
        )(first, queries, query_map, feat, values)

    def mix(qfeat, numer, denom, prior):
        return pl.pallas_call(
            mix_kernel,
            grid=(half,),
            in_specs=[
                head_block(rows, feat_size),
                head_block(rows, head_size),
                head_block(rows, head_size),
                head_block(feat_size + EXTRA, head_size),
            ],
            out_specs=pl.BlockSpec((rows, head_size), lambda i: (0, i)),
            out_shape=of(rows, wide),
            compiler_params=params,
            name="mix",
            cost_estimate=cost(
                3 * half * rows * feat_size * head_size, half * rows * (3 * head_size + 2 * feat_size)
            ),
        )(qfeat, numer, denom, prior)

    even = range(0, heads, 2)
    blocks = heads // 2
    bits = [1 << b for b in reversed(range(ctx.bit_length() - 1)) if 1 << b != PAIR]
    far, near = bits[-2:]
    rels = [0]
    for bit in bits[:-2]:
        rels = rels + [r | bit for r in rels]
    rels = [r | s for s in (0, near, far, far | near) for r in rels]

    def rows_of(weight, flip, halves):
        starts = [(h ^ flip ^ d) * depth + which * wide for which in halves for d in even]
        return jnp.concatenate([lax.dynamic_slice_in_dim(weight, start, wide, 0) for start in starts])

    def widen(x):
        for bit in bits[:-2]:
            x = jnp.concatenate([x, swap(x, bit)], axis=1)
        return x

    def beyond(x):
        pairs = [[i, i | far] for i in range(ctx) if not i & far]
        both = lax.all_gather(x, "ctx", axis_index_groups=pairs)
        return lax.dynamic_index_in_dim(both, jnp.where((c & far) != 0, 0, 1), 0, False)

    own, other = odd.reshape(1), (1 - odd).reshape(1)
    taken = widen(swap(rows_of(out_weight, 1, [odd, 1 - odd]), 0, 1))
    taken_far = beyond(taken)
    other_state, other_feat = key_part(other)
    out_weight, other_state = together((out_weight, other_state))
    kept = widen(rows_of(out_weight, 0, [odd, 1 - odd]))
    from_neighbour = swap(other_state, 1)
    own_state, own_feat = key_part(own)

    from_neighbour, own_state, kept, taken = together((from_neighbour, own_state, kept, taken))
    taken_near = swap(taken, near)
    middle = kept.shape[0] // 2
    kept_far = [beyond(kept[:middle])]
    earlier = jnp.where(odd == 0, own_state, from_neighbour)
    total = own_state + from_neighbour
    before = jnp.zeros_like(total)
    bit = 2
    while 2 * bit < ctx:
        got = swap(total, bit)
        before = before + jnp.where((c & bit) != 0, got, 0.0)
        total = total + got
        bit *= 2
    total, before, taken_near, taken_far, kept, own_feat, other_feat = together(
        (total, before, taken_near, taken_far, kept, own_feat, other_feat)
    )
    kept_near = swap(kept, near)
    kept_far.append(beyond(kept[middle:]))
    second = (c & PAIR) != 0
    got = swap(jnp.where(second, total[half // 2 :], total[: half // 2]), bit, keep=lambda i: not i & bit)
    met = swap(got, PAIR, keep=lambda i: i & bit)
    own_query, other_query = query_part(own, own_feat), query_part(other, other_feat)
    got = jnp.concatenate([jnp.where(second, met, got), jnp.where(second, got, met)])
    got, kept_near, kept_far[0], own_query, other_query = together(
        (got, kept_near, kept_far[0], own_query, other_query)
    )
    before = before + got

    other_prior = swap(before + jnp.where(odd == 0, earlier, 0.0), 1)
    own_mixed = mix(*own_query, before + jnp.where(odd == 1, earlier, 0.0))
    head_bits = [1 << b for b in range(1, heads.bit_length() - 1)]

    def spread(own, met, across, last):
        pieces = {(0, 0): own, (PAIR, 0): met, (0, head_bits[0]): across, (PAIR, head_bits[0]): last}
        for bit in head_bits[1:]:
            pieces.update({(d, j | bit): swap(pieces[d, j], 0, bit) for d, j in list(pieces)})
        return [pieces[d, j] for d in (0, PAIR) for j in even]

    met, across = swap(own_mixed, PAIR), swap(own_mixed, 0, head_bits[0])
    other_prior, met, across, kept_far, taken_far = together((other_prior, met, across, kept_far, taken_far))
    taken_both = swap(taken_far, near)
    own_pieces = spread(own_mixed, met, across, swap(met, 0, head_bits[0]))
    other_mixed = mix(*other_query, other_prior)
    met, across = swap(other_mixed, PAIR), swap(other_mixed, 0, head_bits[0])
    met, across, taken_both, kept_far = together((met, across, taken_both, kept_far))
    kept_both = swap(jnp.concatenate(kept_far), near)
    other_pieces = spread(other_mixed, met, across, swap(met, 0, head_bits[0]))

    lanes = kept.shape[1]

    def strip(parts, crossed=False):
        places = [(part, i) for part in parts for i in range(part.shape[0] // wide)]
        return places[blocks:] + places[:blocks] if crossed else places

    def project(halves, strips, total=None):
        flat, weights, weight_specs = [[], []], [], []
        for which, pieces in halves:
            flat[0] += pieces[:blocks]
            flat[1] += pieces[blocks:]
            for j in range(blocks):
                for places in strips:
                    part, unit = places[which * blocks + j]
                    weights.append(part)
                    weight_specs.append(pl.BlockSpec((wide, lanes), lambda i, unit=unit: (unit, 0)))
        count = len(flat[0])
        out_block = pl.BlockSpec((2 * rows, len(strips) * lanes), lambda i: (0, 0))
        extra = [] if total is None else [total]
        return pl.pallas_call(
            functools.partial(project_kernel, count, len(strips)),
            grid=(1,),
            in_specs=[pl.BlockSpec((rows, wide), lambda i: (0, 0))] * (2 * count)
            + weight_specs
            + [out_block] * len(extra),
            out_specs=out_block,
            out_shape=of(2 * rows, len(strips) * lanes),
            compiler_params=params,
            name="project",
            cost_estimate=cost(
                3 * 2 * rows * wide * count * len(strips) * lanes, wide * count * (2 * rows + len(strips) * lanes)
            ),
        )(*flat[0], *flat[1], *weights, *extra)

    theirs = [strip([taken]), strip([taken_near], True), strip([taken_far]), strip([taken_both], True)]
    mine_near = [strip([kept]), strip([kept_near], True)]
    for_them = project([(0, own_pieces)], theirs)
    near_sum = project([(0, own_pieces)], mine_near)
    for_them, near_sum = together((for_them, near_sum))
    for_them = project([(1, other_pieces)], theirs, for_them)
    from_them = swap(for_them, 0, 1)
    mine_near = project([(1, other_pieces)], mine_near, near_sum)
    mine_far = project([(0, own_pieces), (1, other_pieces)], [strip(kept_far), strip([kept_both], True)])

    groups, perms, send, place = route_tables(ctx, heads, rels)
    steps, size = len(perms), len(groups[0])
    send_here = jnp.asarray(send)[me]
    place_here = jnp.asarray(place)[me]
    if strip_width % 128 == 0:
        parts = pl.pallas_call(
            functools.partial(route_kernel, groups, strip_width),
            grid_spec=pltpu.PrefetchScalarGridSpec(
                num_scalar_prefetch=1,
                grid=(1,),
                in_specs=[pl.BlockSpec(x.shape, lambda i, send: (0, 0)) for x in (mine_near, mine_far, from_them)],
                out_specs=[pl.BlockSpec((rows, size * strip_width), lambda i, send: (0, 0))] * steps,
                scratch_shapes=[pltpu.VMEM((steps, rows, size * strip_width), jnp.float32)],
            ),
            out_shape=[of(rows, size * strip_width)] * steps,
            compiler_params=params,
            name="route",
            cost_estimate=cost(0, 6 * rows * steps * size * strip_width),
        )(send_here, mine_near, mine_far, from_them)
    else:
        product = jnp.concatenate([mine_near, mine_far], axis=1) + from_them
        parts = jnp.stack(pieces_of(product, groups, strip_width))
        parts = [lax.dynamic_index_in_dim(parts, send_here[k], 0, False) for k in range(steps)]
    arrived = [lax.ppermute(part, AXES, perm) for part, perm in zip(parts, perms)]
    if strip_width % 128 == 0:
        return pl.pallas_call(
            functools.partial(assemble_kernel, size),
            grid_spec=pltpu.PrefetchScalarGridSpec(
                num_scalar_prefetch=1,
                grid=(1,),
                in_specs=[pl.BlockSpec(x.shape, lambda i, place: (0, 0)) for x in (*arrived, residual)],
                out_specs=pl.BlockSpec(residual.shape, lambda i, place: (0, 0)),
                scratch_shapes=[pltpu.VMEM((ctx, rows, strip_width), jnp.float32)],
            ),
            out_shape=of(*residual.shape),
            compiler_params=params,
            name="assemble",
            cost_estimate=cost(0, 3 * residual.size),
        )(place_here, *arrived, residual)
    blocks = jnp.stack([a[:, b * strip_width : (b + 1) * strip_width] for a in arrived for b in range(size)])
    projected = [lax.dynamic_index_in_dim(blocks, place_here[p], 0, False) for p in range(ctx)]
    return residual + jnp.concatenate(projected, axis=1)


def solution(mesh):
    placed = (
        P("ctx", "head"),
        P("ctx", "head"),
        P("ctx", "head"),
        P("head", None, None),
        P("head", None, None),
        P(None, ("ctx", "head")),
        P("ctx", "head"),
    )
    return jax.shard_map(
        functools.partial(body, mesh.shape["ctx"], mesh.shape["head"]),
        mesh=mesh,
        in_specs=placed,
        out_specs=P("ctx", "head"),
        check_vma=False,
    )
```

```python
import functools

import numpy as np

import jax
import jax.numpy as jnp
from jax import lax
from jax.experimental import pallas as pl
from jax.experimental.pallas import tpu as pltpu
from jax.sharding import PartitionSpec as P

HIGH = lax.Precision.HIGHEST
together = lax.optimization_barrier
AXES = ("ctx", "head")
PAIR = 2
EXTRA = 8
MIB = 1024 * 1024


def split(x):
    high = x.astype(jnp.bfloat16)
    return high, (x - high.astype(jnp.float32)).astype(jnp.bfloat16)


def dot3(a, b, dims=(((1,), (0,)), ((), ()))):
    a_high, a_low = split(a)
    b_high, b_low = split(b)
    dot = functools.partial(lax.dot_general, dimension_numbers=dims, preferred_element_type=jnp.float32)
    return dot(a_high, b_high) + (dot(a_high, b_low) + dot(a_low, b_high))


def features(rows, weights):
    scores = jnp.dot(rows, weights, precision=HIGH, preferred_element_type=jnp.float32)
    up = jnp.exp(scores - jnp.max(scores, axis=-1, keepdims=True))
    down = jnp.exp(jnp.min(scores, axis=-1, keepdims=True) - scores)
    up = up / jnp.sum(up, axis=-1, keepdims=True)
    down = down / jnp.sum(down, axis=-1, keepdims=True)
    return jnp.concatenate([up, down], axis=-1)


def key_kernel(first, k_ref, map_ref, v_ref, state_ref, feat_ref):
    heads, head_size, feat_half = map_ref.shape
    size = 2 * feat_half
    row = lax.broadcasted_iota(jnp.int32, (EXTRA, feat_half), 0)
    for i in range(heads):
        columns = slice(i * head_size, (i + 1) * head_size)
        feat = features(k_ref[:, columns], map_ref[i])
        feat_ref[i] = feat
        state_ref[i, :size, :] = dot3(feat, v_ref[:, columns], (((0,), (0,)), ((), ())))
        norm = jnp.sum(feat, axis=0, keepdims=True)
        state_ref[i, size:, :] = jnp.where(row < EXTRA // 2, norm[:, :feat_half], norm[:, feat_half:])


def attend(feat, key_feat, values, numer_ref, denom_ref):
    weights = dot3(feat, key_feat, (((1,), (1,)), ((), ())))
    row = lax.broadcasted_iota(jnp.int32, weights.shape, 0)
    column = lax.broadcasted_iota(jnp.int32, weights.shape, 1)
    weights = jnp.where(column <= row, weights, 0.0)
    numer_ref[0] = dot3(weights, values)
    denom_ref[0] = jnp.broadcast_to(jnp.sum(weights, axis=-1, keepdims=True), denom_ref.shape[1:])


def rest_kernel(first, *refs):
    k_ref, k_map_ref, q_ref, q_map_ref, v_ref, other_q_ref, other_q_map_ref, other_v_ref, other_feat_ref = refs[:9]
    state_ref, feat_ref, numer_ref, denom_ref, other_out_ref, other_numer_ref, other_denom_ref = refs[9:]
    heads, head_size, feat_half = k_map_ref.shape
    size = 2 * feat_half
    row = lax.broadcasted_iota(jnp.int32, (EXTRA, feat_half), 0)
    key_feat = features(k_ref[...], k_map_ref[0])
    state_ref[0, :size, :] = dot3(key_feat, v_ref[...], (((0,), (0,)), ((), ())))
    norm = jnp.sum(key_feat, axis=0, keepdims=True)
    state_ref[0, size:, :] = jnp.where(row < EXTRA // 2, norm[:, :feat_half], norm[:, feat_half:])
    feat = features(q_ref[...], q_map_ref[0])
    feat_ref[0] = feat
    attend(feat, key_feat, v_ref[...], numer_ref, denom_ref)
    feat = features(other_q_ref[...], other_q_map_ref[0])
    other_out_ref[0] = feat
    attend(feat, other_feat_ref[0], other_v_ref[...], other_numer_ref, other_denom_ref)


def mix_kernel(qfeat_ref, numer_ref, denom_ref, prior_ref, out_ref):
    feat = qfeat_ref[0]
    size = feat.shape[1]
    norm = jnp.concatenate(
        [prior_ref[0, size : size + 1, :], prior_ref[0, size + EXTRA // 2 : size + EXTRA // 2 + 1, :]], axis=1
    )
    denom = denom_ref[0] + jnp.sum(feat * norm, axis=-1, keepdims=True)
    out_ref[...] = (numer_ref[0] + dot3(feat, prior_ref[0, :size, :])) / denom


def project_kernel(terms, units, *refs):
    rows_refs, refs = refs[: 2 * units], refs[2 * units :]
    count = sum(stop - start for _, start, stop in terms)
    w_refs, rest, out_ref = refs[:count], refs[count:-1], refs[-1]
    out_ref[...] = rest[0][...] if rest else jnp.zeros_like(out_ref)
    lanes = w_refs[0].shape[1]
    for unit, start, stop in terms:
        a = jnp.concatenate([rows_refs[2 * unit][...], rows_refs[2 * unit + 1][...]], axis=0)
        w = jnp.concatenate([ref[...] for ref in w_refs[: stop - start]], axis=1)
        w_refs = w_refs[stop - start :]
        out_ref[:, start * lanes : stop * lanes] += dot3(a, w)


def pieces_of(product, groups, width):
    rows = product.shape[0] // 2
    return [
        jnp.concatenate([product[d * rows : (d + 1) * rows, b * width : (b + 1) * width] for b in group], axis=1)
        for d in range(2)
        for group in groups
    ]


def route_kernel(groups, width, send, mine_ref, other_ref, *refs):
    out_refs, pieces_ref = refs[:-1], refs[-1]
    product = mine_ref[...] + other_ref[...]
    for j, piece in enumerate(pieces_of(product, groups, width)):
        pieces_ref[j] = piece
    for k, out_ref in enumerate(out_refs):
        out_ref[...] = pieces_ref[send[k]]


def assemble_kernel(size, place, *refs):
    arrived, (residual_ref, out_ref, blocks_ref) = refs[:-3], refs[-3:]
    width = blocks_ref.shape[2]
    for k, ref in enumerate(arrived):
        for b in range(size):
            blocks_ref[k * size + b] = ref[:, b * width : (b + 1) * width]
    for p in range(blocks_ref.shape[0]):
        columns = slice(p * width, (p + 1) * width)
        out_ref[:, columns] = residual_ref[:, columns] + blocks_ref[place[p]]


def route_tables(ctx, heads, rels):
    groups = {}
    for column, rel in enumerate(rels):
        groups.setdefault(rel * heads // ctx, []).append(column)
    groups = [groups[key] for key in sorted(groups)]
    size = len(groups[0])
    targets = {}
    for c in range(ctx):
        for h in range(heads):
            found = {}
            for d, step in enumerate((0, PAIR)):
                for g, columns in enumerate(groups):
                    to = (c ^ step) * heads + (c ^ rels[columns[0]]) * heads // ctx
                    found[to] = d * len(groups) + g
            targets[c * heads + h] = found
    classes = {}
    for device in sorted(targets):
        classes.setdefault(tuple(sorted(targets[device])), []).append(device)
    steps = 2 * len(groups)
    perms = [[] for _ in range(steps)]
    send = np.zeros((ctx * heads, steps), np.int32)
    arrives = {}
    for ends, sources in classes.items():
        for i, source in enumerate(sources):
            for k in range(steps):
                to = ends[i ^ k]
                perms[k].append((source, to))
                send[source, k] = targets[source][to]
                arrives[to, source] = k
    place = np.zeros((ctx * heads, ctx), np.int32)
    for c in range(ctx):
        for h in range(heads):
            for p in range(ctx):
                column_ctx, source_h = divmod(h * ctx + p, heads)
                source_c = (c & ~PAIR) | (column_ctx & PAIR)
                k = arrives[c * heads + h, source_c * heads + source_h]
                rel = source_c ^ column_ctx
                group = [g for g in groups if rels.index(rel) in g][0]
                place[c * heads + h, p] = k * size + group.index(rels.index(rel))
    return groups, perms, send, place


def body(ctx, heads, queries, keys, values, query_map, key_map, out_weight, residual):
    rows = queries.shape[0]
    heads_here, head_size, feat_half = query_map.shape
    feat_size = 2 * feat_half
    half = heads_here // 2
    wide = half * head_size
    depth = out_weight.shape[0] // heads
    strip_width = out_weight.shape[1]
    c = lax.axis_index("ctx")
    h = lax.axis_index("head")
    me = c * heads + h
    odd = c & 1

    def swap(x, by_ctx, by_head=0, keep=lambda c: True):
        pairs = [
            (i * heads + j, (i ^ by_ctx) * heads + (j ^ by_head))
            for i in range(ctx)
            for j in range(heads)
            if keep(i)
        ]
        return lax.ppermute(x, AXES, pairs)

    def of(*shape):
        return jax.ShapeDtypeStruct(shape, jnp.float32)

    def cost(products, count, exps=0):
        return pl.CostEstimate(flops=2 * products, bytes_accessed=4 * count, transcendentals=exps)

    def params(mib):
        return pltpu.CompilerParams(vmem_limit_bytes=mib * MIB)

    def head_block(size, lanes):
        return pl.BlockSpec((1, size, lanes), lambda i, *_: (i, 0, 0))

    def key_part(first):
        columns = pl.BlockSpec((rows, wide), lambda i, first: (0, first[0]))
        maps = pl.BlockSpec((half, head_size, feat_half), lambda i, first: (first[0], 0, 0))
        shapes = [of(half, feat_size + EXTRA, head_size), of(half, rows, feat_size)]
        return pl.pallas_call(
            key_kernel,
            grid_spec=pltpu.PrefetchScalarGridSpec(
                num_scalar_prefetch=1,
                grid=(1,),
                in_specs=[columns, maps, columns],
                out_specs=[pl.BlockSpec(s.shape, lambda i, first: (0, 0, 0)) for s in shapes],
            ),
            out_shape=shapes,
            compiler_params=params(60),
            name="key_part",
            cost_estimate=cost(
                6 * half * rows * head_size * (feat_half + feat_size),
                half * rows * (2 * head_size + 2 * feat_size),
                half * rows * feat_size,
            ),
        )(first, keys, key_map, values)

    def rest_part(firsts, other_feat):
        def columns(which):
            return pl.BlockSpec((rows, head_size), lambda i, first: (0, first[which] * half + i))

        def maps(which):
            return pl.BlockSpec((1, head_size, feat_half), lambda i, first: (first[which] * half + i, 0, 0))

        query_shapes = [of(half, rows, feat_size), of(half, rows, head_size), of(half, rows, head_size)]
        shapes = [of(half, feat_size + EXTRA, head_size), *query_shapes, *query_shapes]
        outs = pl.pallas_call(
            rest_kernel,
            grid_spec=pltpu.PrefetchScalarGridSpec(
                num_scalar_prefetch=1,
                grid=(half,),
                in_specs=[columns(0), maps(0), columns(0), maps(0), columns(0)]
                + [columns(1), maps(1), columns(1), head_block(rows, feat_size)],
                out_specs=[head_block(*shape.shape[1:]) for shape in shapes],
            ),
            out_shape=shapes,
            compiler_params=params(40),
            name="rest_part",
            cost_estimate=cost(
                6 * half * rows * (head_size * (3 * feat_half + feat_size) + 2 * rows * (feat_size + head_size)),
                half * rows * (8 * head_size + 4 * feat_size),
                3 * half * rows * feat_size,
            ),
        )(firsts, keys, key_map, queries, query_map, values, queries, query_map, values, other_feat)
        return outs[0], outs[1:4], outs[4:]

    def mix(qfeat, numer, denom, prior):
        return pl.pallas_call(
            mix_kernel,
            grid=(half,),
            in_specs=[
                head_block(rows, feat_size),
                head_block(rows, head_size),
                head_block(rows, head_size),
                head_block(feat_size + EXTRA, head_size),
            ],
            out_specs=pl.BlockSpec((rows, head_size), lambda i: (0, i)),
            out_shape=of(rows, wide),
            compiler_params=params(12),
            name="mix",
            cost_estimate=cost(
                3 * half * rows * feat_size * head_size, half * rows * (3 * head_size + 2 * feat_size)
            ),
        )(qfeat, numer, denom, prior)

    even = range(0, heads, 2)
    blocks = heads // 2
    quarter = 2 * blocks // 4 * wide
    bits = [1 << b for b in reversed(range(ctx.bit_length() - 1)) if 1 << b != PAIR]
    far, near = bits[-2:]
    rels = [0]
    for bit in bits[:-2]:
        rels = rels + [r | bit for r in rels]
    rels = [r | s for s in (0, near, far, far | near) for r in rels]

    def rows_of(weight, flip, some):
        starts = [(h ^ flip ^ d) * depth + which * wide for which, d in some]
        return jnp.concatenate([lax.dynamic_slice_in_dim(weight, start, wide, 0) for start in starts])

    def widen(x):
        for bit in bits[:-2]:
            x = jnp.concatenate([x, swap(x, bit)], axis=1)
        return x

    def quarters(x):
        return [x[i : i + quarter] for i in range(0, x.shape[0], quarter)]

    order = [(which, d) for which in (odd, 1 - odd) for d in even]
    part = len(order) // 4
    own, other = odd.reshape(1), (1 - odd).reshape(1)
    kept_first = widen(rows_of(out_weight, 0, order[:part]))
    far_1 = swap(kept_first, far)
    other_state, other_feat = key_part(other)
    out_weight, other_state = together((out_weight, other_state))
    kept_rest = widen(rows_of(out_weight, 0, order[part:]))
    from_neighbour = swap(other_state, 1)
    own_state, own_query, other_query = rest_part(jnp.concatenate([own, other]), other_feat)
    groups, perms, send, place = route_tables(ctx, heads, rels)
    steps, size = len(perms), len(groups[0])
    send_here = jnp.asarray(send)[me]
    place_here = jnp.asarray(place)[me]

    from_neighbour, own_state, far_1, kept_first, kept_rest, out_weight = together(
        (from_neighbour, own_state, far_1, kept_first, kept_rest, out_weight)
    )
    far_2 = swap(kept_rest[: 2 * quarter], far)
    kept = jnp.concatenate([kept_first, kept_rest])
    kept_near = swap(kept, near)
    taken = widen(swap(rows_of(out_weight, 1, order), 0, 1))
    earlier = jnp.where(odd == 0, own_state, from_neighbour)
    total = own_state + from_neighbour
    before = jnp.zeros_like(total)
    bit = 2
    while 2 * bit < ctx:
        got = swap(total, bit)
        before = before + jnp.where((c & bit) != 0, got, 0.0)
        total = total + got
        bit *= 2
    total, before, far_2, kept_near, taken = together((total, before, far_2, kept_near, taken))
    taken_near = swap(taken, near)
    second = (c & PAIR) != 0
    got = swap(jnp.where(second, total[half // 2 :], total[: half // 2]), bit, keep=lambda i: not i & bit)
    taken_parts = quarters(taken)
    got, taken_parts[0] = together((got, taken_parts[0]))
    met = swap(got, PAIR, keep=lambda i: i & bit)
    far_3 = swap(taken_parts[0], far)
    got = jnp.concatenate([jnp.where(second, met, got), jnp.where(second, got, met)])
    got, far_3, taken_near, taken_parts[1], send_here, place_here = together(
        (got, far_3, taken_near, taken_parts[1], send_here, place_here)
    )
    before = before + got

    other_prior = swap(before + jnp.where(odd == 0, earlier, 0.0), 1)
    own_mixed = mix(*own_query, before + jnp.where(odd == 1, earlier, 0.0))
    head_bits = [1 << b for b in range(1, heads.bit_length() - 1)]

    def spread(own, met, across, last):
        pieces = {(0, 0): own, (PAIR, 0): met, (0, head_bits[0]): across, (PAIR, head_bits[0]): last}
        for bit in head_bits[1:]:
            pieces.update({(d, j | bit): swap(pieces[d, j], 0, bit) for d, j in list(pieces)})
        return [pieces[d, j] for d in (0, PAIR) for j in even]

    met, across = swap(own_mixed, PAIR), swap(own_mixed, 0, head_bits[0])
    far_4 = swap(taken_parts[1], far)
    next_part = taken[2 * quarter :]
    other_prior, far_1, far_2, far_3, far_4, met, across, next_part = together(
        (other_prior, far_1, far_2, far_3, far_4, met, across, next_part)
    )
    own_pieces = spread(own_mixed, met, across, swap(met, 0, head_bits[0]))
    other_mixed = mix(*other_query, other_prior)
    met, across = swap(other_mixed, PAIR), swap(other_mixed, 0, head_bits[0])
    far_5 = swap(next_part, far)
    both_1 = swap(jnp.concatenate([far_1, far_2, far_3, far_4]), near)
    met, across, far_5, both_1, kept_rest = together((met, across, far_5, both_1, kept_rest))
    far_6 = swap(kept_rest[2 * quarter :], far)
    both_2 = swap(far_5, near)
    other_pieces = spread(other_mixed, met, across, swap(met, 0, head_bits[0]))

    lanes = kept.shape[1]

    def strip(parts, crossed=False):
        places = [(x, start * part + i) for x, start, stop in parts for i in range((stop - start) * part)]
        return places[blocks:] + places[:blocks] if crossed else places

    def strips_of(last_far, last_both):
        theirs = [
            strip([(taken, 0, 4)]),
            strip([(taken_near, 0, 4)], True),
            strip([(far_3, 0, 1), (far_4, 0, 1), (far_5, 0, 2)]),
            strip([(both_1, 3, 5), (both_2, 0, 2)], True),
        ]
        mine = [
            strip([(kept, 0, 4)]),
            strip([(kept_near, 0, 4)], True),
            strip([(far_1, 0, 1), (far_2, 0, 2), (last_far, 0, 1)]),
            strip([(both_1, 0, 3), (last_both, 0, 1)], True),
        ]
        return theirs, mine

    def project(pieces, strips, runs, total=None, column=0):
        runs = [(u, start, stop) for q, start, stop in runs for u in range(q * part, (q + 1) * part)]
        used = sorted({u for u, _, _ in runs})
        weights = [strips[s][u] for u, start, stop in runs for s in range(start, stop)]
        shape = (2 * rows, len(strips) * lanes)
        extra = [] if total is None else [total]
        terms = [(used.index(u), start, stop) for u, start, stop in runs]
        return pl.pallas_call(
            functools.partial(project_kernel, terms, len(used)),
            grid=(1,),
            in_specs=[pl.BlockSpec((rows, wide), lambda i: (0, 0))] * (2 * len(used))
            + [pl.BlockSpec((wide, lanes), lambda i, unit=unit: (unit, 0)) for _, unit in weights]
            + [pl.BlockSpec(shape, lambda i: (0, column))] * len(extra),
            out_specs=pl.BlockSpec(shape, lambda i: (0, 0)),
            out_shape=of(*shape),
            compiler_params=params(24),
            name="project",
            cost_estimate=cost(6 * rows * wide * len(weights) * lanes, wide * lanes * len(weights) + 2 * rows * shape[1]),
        )(*[x for u in used for x in pieces[u]], *[x for x, _ in weights], *extra)

    def by_unit(pieces):
        return [(pieces[j], pieces[blocks + j]) for j in range(blocks)]

    theirs, mine = strips_of(None, None)
    pieces = by_unit(own_pieces) + by_unit(other_pieces)
    product = project(pieces, theirs + mine, [(0, 0, 3), (0, 4, 8), (1, 0, 3), (1, 4, 7)])
    product = project(pieces, theirs + mine, [(2, 0, 8)], product)
    product, other_pieces, far_6 = together((product, other_pieces, far_6))
    theirs, mine = strips_of(far_6, swap(far_6, near))
    pieces = by_unit(own_pieces) + by_unit(other_pieces)
    from_them = swap(project(pieces, theirs, [(3, 0, 4), (0, 3, 4), (1, 3, 4)], product, 0), 0, 1)
    product = project(pieces, mine, [(3, 0, 4), (1, 3, 4)], product, 1)

    if strip_width % 128 == 0:
        parts = pl.pallas_call(
            functools.partial(route_kernel, groups, strip_width),
            grid_spec=pltpu.PrefetchScalarGridSpec(
                num_scalar_prefetch=1,
                grid=(1,),
                in_specs=[pl.BlockSpec(x.shape, lambda i, send: (0, 0)) for x in (product, from_them)],
                out_specs=[pl.BlockSpec((rows, size * strip_width), lambda i, send: (0, 0))] * steps,
                scratch_shapes=[pltpu.VMEM((steps, rows, size * strip_width), jnp.float32)],
            ),
            out_shape=[of(rows, size * strip_width)] * steps,
            compiler_params=params(12),
            name="route",
            cost_estimate=cost(0, 6 * rows * steps * size * strip_width),
        )(send_here, product, from_them)
    else:
        parts = jnp.stack(pieces_of(product + from_them, groups, strip_width))
        parts = [lax.dynamic_index_in_dim(parts, send_here[k], 0, False) for k in range(steps)]
    arrived = [lax.ppermute(part, AXES, perm) for part, perm in zip(parts, perms)]
    if strip_width % 128 == 0:
        return pl.pallas_call(
            functools.partial(assemble_kernel, size),
            grid_spec=pltpu.PrefetchScalarGridSpec(
                num_scalar_prefetch=1,
                grid=(1,),
                in_specs=[pl.BlockSpec(x.shape, lambda i, place: (0, 0)) for x in (*arrived, residual)],
                out_specs=pl.BlockSpec(residual.shape, lambda i, place: (0, 0)),
                scratch_shapes=[pltpu.VMEM((ctx, rows, strip_width), jnp.float32)],
            ),
            out_shape=of(*residual.shape),
            compiler_params=params(12),
            name="assemble",
            cost_estimate=cost(0, 3 * residual.size),
        )(place_here, *arrived, residual)
    blocks = jnp.stack([a[:, b * strip_width : (b + 1) * strip_width] for a in arrived for b in range(size)])
    projected = [lax.dynamic_index_in_dim(blocks, place_here[p], 0, False) for p in range(ctx)]
    return residual + jnp.concatenate(projected, axis=1)


def solution(mesh):
    placed = (
        P("ctx", "head"),
        P("ctx", "head"),
        P("ctx", "head"),
        P("head", None, None),
        P("head", None, None),
        P(None, ("ctx", "head")),
        P("ctx", "head"),
    )
    return jax.shard_map(
        functools.partial(body, mesh.shape["ctx"], mesh.shape["head"]),
        mesh=mesh,
        in_specs=placed,
        out_specs=P("ctx", "head"),
        check_vma=False,
    )
```

```python
import functools

import numpy as np

import jax
import jax.numpy as jnp
from jax import lax
from jax.experimental import pallas as pl
from jax.experimental.pallas import tpu as pltpu
from jax.sharding import PartitionSpec as P

HIGH = lax.Precision.HIGHEST
together = lax.optimization_barrier
AXES = ("ctx", "head")
PAIR = 2
EXTRA = 8
MIB = 1024 * 1024


def split(x):
    high = x.astype(jnp.bfloat16)
    return high, (x - high.astype(jnp.float32)).astype(jnp.bfloat16)


def dot3(a, b, dims=(((1,), (0,)), ((), ()))):
    a_high, a_low = split(a)
    b_high, b_low = split(b)
    dot = functools.partial(lax.dot_general, dimension_numbers=dims, preferred_element_type=jnp.float32)
    return dot(a_high, b_high) + (dot(a_high, b_low) + dot(a_low, b_high))


def features(rows, weights):
    scores = jnp.dot(rows, weights, precision=HIGH, preferred_element_type=jnp.float32)
    up = jnp.exp(scores - jnp.max(scores, axis=-1, keepdims=True))
    down = jnp.exp(jnp.min(scores, axis=-1, keepdims=True) - scores)
    up = up / jnp.sum(up, axis=-1, keepdims=True)
    down = down / jnp.sum(down, axis=-1, keepdims=True)
    return jnp.concatenate([up, down], axis=-1)


def arrange_kernel(plan, wide, starts, weight_ref, *refs):
    out_refs, sems = refs[:-1], refs[-1]
    copies = []
    for out_ref, picks in zip(out_refs, plan):
        for i, pick in enumerate(picks):
            source = weight_ref.at[pl.ds(pl.multiple_of(starts[pick], wide), wide), :]
            copies.append(pltpu.make_async_copy(source, out_ref.at[pl.ds(i * wide, wide), :], sems.at[len(copies)]))
            copies[-1].start()
    for copy in copies:
        copy.wait()


def key_kernel(first, k_ref, map_ref, v_ref, state_ref, feat_ref):
    heads, head_size, feat_half = map_ref.shape
    size = 2 * feat_half
    row = lax.broadcasted_iota(jnp.int32, (EXTRA, feat_half), 0)
    for i in range(heads):
        columns = slice(i * head_size, (i + 1) * head_size)
        feat = features(k_ref[:, columns], map_ref[i])
        feat_ref[i] = feat
        state_ref[i, :size, :] = dot3(feat, v_ref[:, columns], (((0,), (0,)), ((), ())))
        norm = jnp.sum(feat, axis=0, keepdims=True)
        state_ref[i, size:, :] = jnp.where(row < EXTRA // 2, norm[:, :feat_half], norm[:, feat_half:])


def attend(feat, key_feat, values, numer_ref, denom_ref):
    weights = dot3(feat, key_feat, (((1,), (1,)), ((), ())))
    row = lax.broadcasted_iota(jnp.int32, weights.shape, 0)
    column = lax.broadcasted_iota(jnp.int32, weights.shape, 1)
    weights = jnp.where(column <= row, weights, 0.0)
    numer_ref[0] = dot3(weights, values)
    denom_ref[0] = jnp.broadcast_to(jnp.sum(weights, axis=-1, keepdims=True), denom_ref.shape[1:])


def rest_kernel(first, *refs):
    k_ref, k_map_ref, q_ref, q_map_ref, v_ref, other_q_ref, other_q_map_ref, other_v_ref, other_feat_ref = refs[:9]
    state_ref, feat_ref, numer_ref, denom_ref, other_out_ref, other_numer_ref, other_denom_ref = refs[9:]
    heads, head_size, feat_half = k_map_ref.shape
    size = 2 * feat_half
    row = lax.broadcasted_iota(jnp.int32, (EXTRA, feat_half), 0)
    key_feat = features(k_ref[...], k_map_ref[0])
    state_ref[0, :size, :] = dot3(key_feat, v_ref[...], (((0,), (0,)), ((), ())))
    norm = jnp.sum(key_feat, axis=0, keepdims=True)
    state_ref[0, size:, :] = jnp.where(row < EXTRA // 2, norm[:, :feat_half], norm[:, feat_half:])
    feat = features(q_ref[...], q_map_ref[0])
    feat_ref[0] = feat
    attend(feat, key_feat, v_ref[...], numer_ref, denom_ref)
    feat = features(other_q_ref[...], other_q_map_ref[0])
    other_out_ref[0] = feat
    attend(feat, other_feat_ref[0], other_v_ref[...], other_numer_ref, other_denom_ref)


def mix_kernel(qfeat_ref, numer_ref, denom_ref, prior_ref, *refs):
    feat = qfeat_ref[0]
    size = feat.shape[1]
    norm = jnp.concatenate(
        [prior_ref[0, size : size + 1, :], prior_ref[0, size + EXTRA // 2 : size + EXTRA // 2 + 1, :]], axis=1
    )
    denom = denom_ref[0] + jnp.sum(feat * norm, axis=-1, keepdims=True)
    mixed = (numer_ref[0] + dot3(feat, prior_ref[0, :size, :])) / denom
    if len(refs) == 1:
        refs[0][...] = mixed
    else:
        below_ref, out_ref, both_ref = refs
        out_ref[...] = mixed
        both_ref[...] = jnp.concatenate([mixed, below_ref[...]], axis=0)


def project_kernel(terms, units, *refs):
    rows_refs, refs = refs[: 2 * units], refs[2 * units :]
    count = sum(stop - start for _, start, stop in terms)
    w_refs, rest, out_ref = refs[:count], refs[count:-1], refs[-1]
    out_ref[...] = rest[0][...] if rest else jnp.zeros_like(out_ref)
    lanes = w_refs[0].shape[1]
    for unit, start, stop in terms:
        a = jnp.concatenate([rows_refs[2 * unit][...], rows_refs[2 * unit + 1][...]], axis=0)
        w = jnp.concatenate([ref[...] for ref in w_refs[: stop - start]], axis=1)
        w_refs = w_refs[stop - start :]
        out_ref[:, start * lanes : stop * lanes] += dot3(a, w)


def pieces_of(product, groups, width):
    rows = product.shape[0] // 2
    return [
        jnp.concatenate([product[d * rows : (d + 1) * rows, b * width : (b + 1) * width] for b in group], axis=1)
        for d in range(2)
        for group in groups
    ]


def route_kernel(groups, width, send, mine_ref, other_ref, *refs):
    out_refs, pieces_ref = refs[:-1], refs[-1]
    product = mine_ref[...] + other_ref[...]
    for j, piece in enumerate(pieces_of(product, groups, width)):
        pieces_ref[j] = piece
    for k, out_ref in enumerate(out_refs):
        out_ref[...] = pieces_ref[send[k]]


def assemble_kernel(size, place, *refs):
    arrived, (residual_ref, out_ref, blocks_ref) = refs[:-3], refs[-3:]
    width = blocks_ref.shape[2]
    for k, ref in enumerate(arrived):
        for b in range(size):
            blocks_ref[k * size + b] = ref[:, b * width : (b + 1) * width]
    for p in range(blocks_ref.shape[0]):
        columns = slice(p * width, (p + 1) * width)
        out_ref[:, columns] = residual_ref[:, columns] + blocks_ref[place[p]]


def route_tables(ctx, heads, rels):
    groups = {}
    for column, rel in enumerate(rels):
        groups.setdefault(rel * heads // ctx, []).append(column)
    groups = [groups[key] for key in sorted(groups)]
    size = len(groups[0])
    targets = {}
    for c in range(ctx):
        for h in range(heads):
            found = {}
            for d, step in enumerate((0, PAIR)):
                for g, columns in enumerate(groups):
                    to = (c ^ step) * heads + (c ^ rels[columns[0]]) * heads // ctx
                    found[to] = d * len(groups) + g
            targets[c * heads + h] = found
    classes = {}
    for device in sorted(targets):
        classes.setdefault(tuple(sorted(targets[device])), []).append(device)
    steps = 2 * len(groups)
    perms = [[] for _ in range(steps)]
    send = np.zeros((ctx * heads, steps), np.int32)
    arrives = {}
    for ends, sources in classes.items():
        for i, source in enumerate(sources):
            for k in range(steps):
                to = ends[i ^ k]
                perms[k].append((source, to))
                send[source, k] = targets[source][to]
                arrives[to, source] = k
    place = np.zeros((ctx * heads, ctx), np.int32)
    for c in range(ctx):
        for h in range(heads):
            for p in range(ctx):
                column_ctx, source_h = divmod(h * ctx + p, heads)
                source_c = (c & ~PAIR) | (column_ctx & PAIR)
                k = arrives[c * heads + h, source_c * heads + source_h]
                rel = source_c ^ column_ctx
                group = [g for g in groups if rels.index(rel) in g][0]
                place[c * heads + h, p] = k * size + group.index(rels.index(rel))
    return groups, perms, send, place


def body(ctx, heads, queries, keys, values, query_map, key_map, out_weight, residual):
    rows = queries.shape[0]
    heads_here, head_size, feat_half = query_map.shape
    feat_size = 2 * feat_half
    half = heads_here // 2
    wide = half * head_size
    depth = out_weight.shape[0] // heads
    strip_width = out_weight.shape[1]
    c = lax.axis_index("ctx")
    h = lax.axis_index("head")
    me = c * heads + h
    odd = c & 1

    def swap(x, by_ctx, by_head=0, keep=lambda c: True):
        pairs = [
            (i * heads + j, (i ^ by_ctx) * heads + (j ^ by_head))
            for i in range(ctx)
            for j in range(heads)
            if keep(i)
        ]
        return lax.ppermute(x, AXES, pairs)

    def of(*shape):
        return jax.ShapeDtypeStruct(shape, jnp.float32)

    def cost(products, count, exps=0):
        return pl.CostEstimate(flops=2 * products, bytes_accessed=4 * count, transcendentals=exps)

    def params(mib):
        return pltpu.CompilerParams(vmem_limit_bytes=mib * MIB)

    def head_block(size, lanes):
        return pl.BlockSpec((1, size, lanes), lambda i, *_: (i, 0, 0))

    def key_part(first):
        columns = pl.BlockSpec((rows, wide), lambda i, first: (0, first[0]))
        maps = pl.BlockSpec((half, head_size, feat_half), lambda i, first: (first[0], 0, 0))
        shapes = [of(half, feat_size + EXTRA, head_size), of(half, rows, feat_size)]
        return pl.pallas_call(
            key_kernel,
            grid_spec=pltpu.PrefetchScalarGridSpec(
                num_scalar_prefetch=1,
                grid=(1,),
                in_specs=[columns, maps, columns],
                out_specs=[pl.BlockSpec(s.shape, lambda i, first: (0, 0, 0)) for s in shapes],
            ),
            out_shape=shapes,
            compiler_params=params(60),
            name="key_part",
            cost_estimate=cost(
                6 * half * rows * head_size * (feat_half + feat_size),
                half * rows * (2 * head_size + 2 * feat_size),
                half * rows * feat_size,
            ),
        )(first, keys, key_map, values)

    def rest_part(firsts, other_feat):
        def columns(which):
            return pl.BlockSpec((rows, head_size), lambda i, first: (0, first[which] * half + i))

        def maps(which):
            return pl.BlockSpec((1, head_size, feat_half), lambda i, first: (first[which] * half + i, 0, 0))

        query_shapes = [of(half, rows, feat_size), of(half, rows, head_size), of(half, rows, head_size)]
        shapes = [of(half, feat_size + EXTRA, head_size), *query_shapes, *query_shapes]
        outs = pl.pallas_call(
            rest_kernel,
            grid_spec=pltpu.PrefetchScalarGridSpec(
                num_scalar_prefetch=1,
                grid=(half,),
                in_specs=[columns(0), maps(0), columns(0), maps(0), columns(0)]
                + [columns(1), maps(1), columns(1), head_block(rows, feat_size)],
                out_specs=[head_block(*shape.shape[1:]) for shape in shapes],
            ),
            out_shape=shapes,
            compiler_params=params(40),
            name="rest_part",
            cost_estimate=cost(
                6 * half * rows * (head_size * (3 * feat_half + feat_size) + 2 * rows * (feat_size + head_size)),
                half * rows * (8 * head_size + 4 * feat_size),
                3 * half * rows * feat_size,
            ),
        )(firsts, keys, key_map, queries, query_map, values, queries, query_map, values, other_feat)
        return outs[0], outs[1:4], outs[4:]

    def mix(qfeat, numer, denom, prior, below=None):
        columns = pl.BlockSpec((rows, head_size), lambda i: (0, i))
        out_specs, shapes = columns, of(rows, wide)
        if below is not None:
            out_specs = [columns, pl.BlockSpec((2 * rows, head_size), lambda i: (0, i))]
            shapes = [shapes, of(2 * rows, wide)]
        return pl.pallas_call(
            mix_kernel,
            grid=(half,),
            in_specs=[
                head_block(rows, feat_size),
                head_block(rows, head_size),
                head_block(rows, head_size),
                head_block(feat_size + EXTRA, head_size),
            ]
            + [columns] * (below is not None),
            out_specs=out_specs,
            out_shape=shapes,
            compiler_params=params(12),
            name="mix",
            cost_estimate=cost(
                3 * half * rows * feat_size * head_size, half * rows * (3 * head_size + 2 * feat_size)
            ),
        )(qfeat, numer, denom, prior, *([] if below is None else [below]))

    even = range(0, heads, 2)
    blocks = heads // 2
    bits = [1 << b for b in reversed(range(ctx.bit_length() - 1)) if 1 << b != PAIR]
    far, near = bits[-2:]
    rels = [0]
    for bit in bits[:-2]:
        rels = rels + [r | bit for r in rels]
    rels = [r | s for s in (0, near, far, far | near) for r in rels]

    def arranged(weight, starts, plan):
        shapes = [of(len(picks) * wide, strip_width) for picks in plan]
        count = sum(len(picks) for picks in plan)
        return pl.pallas_call(
            functools.partial(arrange_kernel, plan, wide),
            grid_spec=pltpu.PrefetchScalarGridSpec(
                num_scalar_prefetch=1,
                grid=(1,),
                in_specs=[pl.BlockSpec(memory_space=pl.ANY)],
                out_specs=[pl.BlockSpec(memory_space=pl.ANY)] * len(plan),
                scratch_shapes=[pltpu.SemaphoreType.DMA((count,))],
            ),
            out_shape=shapes,
            compiler_params=params(12),
            name="arrange",
            cost_estimate=cost(0, 2 * count * wide * strip_width),
        )(starts, weight)

    def widen(x):
        for bit in bits[:-2]:
            x = jnp.concatenate([x, swap(x, bit)], axis=1)
        return x

    order = [(which, d) for which in (odd, 1 - odd) for d in even]
    part = len(order) // 4
    own, other = odd.reshape(1), (1 - odd).reshape(1)
    other_state, other_feat = key_part(other)
    out_weight, other_state = together((out_weight, other_state))
    starts = jnp.stack([(h ^ flip ^ d) * depth + which * wide for flip in (0, 1) for which, d in order])
    count = len(order)
    spans = [(0, part), (part, 3 * part), (3 * part, count), (0, count)]
    plan = [list(range(*span)) for span in spans]
    plan += [list(range(count + start, count + stop)) for start, stop in ((0, 2 * part), (2 * part, count), (0, count))]
    *kept_parts, kept, given_1, given_2, given = arranged(out_weight, starts, plan)
    kept_parts, kept = [widen(x) for x in kept_parts], widen(kept)
    far_1 = swap(kept_parts[0], far)
    from_neighbour = swap(other_state, 1)
    own_state, own_query, other_query = rest_part(jnp.concatenate([own, other]), other_feat)
    groups, perms, send, place = route_tables(ctx, heads, rels)
    steps, size = len(perms), len(groups[0])
    send_here = jnp.asarray(send)[me]
    place_here = jnp.asarray(place)[me]

    from_neighbour, own_state, far_1, kept_parts, kept, given_1, given_2, given = together(
        (from_neighbour, own_state, far_1, kept_parts, kept, given_1, given_2, given)
    )
    far_2 = swap(kept_parts[1], far)
    kept_near = swap(kept, near)
    taken, taken_1, taken_2 = [widen(swap(x, 0, 1)) for x in (given, given_1, given_2)]
    earlier = jnp.where(odd == 0, own_state, from_neighbour)
    total = own_state + from_neighbour
    before = jnp.zeros_like(total)
    bit = 2
    while 2 * bit < ctx:
        got = swap(total, bit)
        before = before + jnp.where((c & bit) != 0, got, 0.0)
        total = total + got
        bit *= 2
    total, before, far_2, kept_near, taken, taken_1, taken_2, send_here, place_here, far_1 = together(
        (total, before, far_2, kept_near, taken, taken_1, taken_2, send_here, place_here, far_1)
    )
    taken_near = swap(taken, near)
    both_1 = swap(far_1, near)
    second = (c & PAIR) != 0
    got = swap(jnp.where(second, total[half // 2 :], total[: half // 2]), bit, keep=lambda i: not i & bit)
    got, kept_parts[2] = together((got, kept_parts[2]))
    met = swap(got, PAIR, keep=lambda i: i & bit)
    far_3 = swap(kept_parts[2], far)
    got = jnp.concatenate([jnp.where(second, met, got), jnp.where(second, got, met)])
    got, far_3, taken_near, both_1, taken_1 = together((got, far_3, taken_near, both_1, taken_1))
    before = before + got

    other_prior = swap(before + jnp.where(odd == 0, earlier, 0.0), 1)
    own_mixed = mix(*own_query, before + jnp.where(odd == 1, earlier, 0.0))
    head_bits = [1 << b for b in range(1, heads.bit_length() - 1)]

    def spread(pieces):
        for bit in head_bits[1:]:
            for (d, j), (x, i) in list(pieces.items()):
                pieces[d, j | bit] = (swap(x[i * rows : (i + 1) * rows], 0, bit), 0)
        return [(pieces[0, j], pieces[PAIR, j]) for j in even]

    met, across = swap(own_mixed, PAIR), swap(own_mixed, 0, head_bits[0])
    far_4 = swap(taken_1, far)
    both_3 = swap(far_3, near)
    other_prior, far_2, far_4, both_3, met, across, taken_2 = together(
        (other_prior, far_2, far_4, both_3, met, across, taken_2)
    )
    other_mixed, both = mix(*other_query, other_prior, met)
    other_met = swap(other_mixed, PAIR)
    both = swap(both, 0, head_bits[0])
    far_5 = swap(taken_2, far)
    both_2 = swap(far_2, near)
    both_4 = swap(far_4, near)
    other_met, both, far_5, both_2, both_4 = together((other_met, both, far_5, both_2, both_4))
    both_5 = swap(far_5, near)
    last = swap(other_met, 0, head_bits[0])
    own_pieces = spread(
        {(0, 0): (own_mixed, 0), (PAIR, 0): (met, 0), (0, head_bits[0]): (across, 0), (PAIR, head_bits[0]): (both, 1)}
    )

    def other_pieces(last):
        pieces = {(0, 0): (other_mixed, 0), (PAIR, 0): (other_met, 0), (0, head_bits[0]): (both, 0)}
        return spread({**pieces, (PAIR, head_bits[0]): (last, 0)})

    lanes = kept.shape[1]

    def strip(parts, crossed=False):
        places = [(x, start * part + i) for x, start, stop in parts for i in range((stop - start) * part)]
        return places[blocks:] + places[:blocks] if crossed else places

    def project(pieces, strips, runs, total=None, column=0):
        runs = [(u, start, stop) for q, start, stop in runs for u in range(q * part, (q + 1) * part)]
        used = sorted({u for u, _, _ in runs})
        weights = [strips[s][u] for u, start, stop in runs for s in range(start, stop)]
        shape = (2 * rows, len(strips) * lanes)
        extra = [] if total is None else [total]
        terms = [(used.index(u), start, stop) for u, start, stop in runs]
        return pl.pallas_call(
            functools.partial(project_kernel, terms, len(used)),
            grid=(1,),
            in_specs=[pl.BlockSpec((rows, wide), lambda i, block=block: (block, 0)) for u in used for _, block in pieces[u]]
            + [pl.BlockSpec((wide, lanes), lambda i, unit=unit: (unit, 0)) for _, unit in weights]
            + [pl.BlockSpec(shape, lambda i: (0, column))] * len(extra),
            out_specs=pl.BlockSpec(shape, lambda i: (0, 0)),
            out_shape=of(*shape),
            compiler_params=params(24),
            name="project",
            cost_estimate=cost(6 * rows * wide * len(weights) * lanes, wide * lanes * len(weights) + 2 * rows * shape[1]),
        )(*[x for u in used for x, _ in pieces[u]], *[x for x, _ in weights], *extra)

    theirs = [
        strip([(taken, 0, 4)]),
        strip([(taken_near, 0, 4)], True),
        strip([(far_4, 0, 2), (far_5, 0, 2)]),
        strip([(both_4, 0, 2), (both_5, 0, 2)], True),
    ]
    mine = [
        strip([(kept, 0, 4)]),
        strip([(kept_near, 0, 4)], True),
        strip([(far_1, 0, 1), (far_2, 0, 2), (far_3, 0, 1)]),
        strip([(both_1, 0, 1), (both_2, 0, 2), (both_3, 0, 1)], True),
    ]
    pieces = own_pieces + other_pieces(last)
    product = project(pieces, theirs + mine, [(0, 0, 3), (0, 4, 8), (1, 0, 3), (1, 4, 8)])
    product = project(pieces, theirs + mine, [(2, 0, 8)], product)
    product, last = together((product, last))
    pieces = own_pieces + other_pieces(last)
    from_them = swap(project(pieces, theirs, [(3, 0, 4), (0, 3, 4), (1, 3, 4)], product, 0), 0, 1)
    product = project(pieces, mine, [(3, 0, 4)], product, 1)

    if strip_width % 128 == 0:
        parts = pl.pallas_call(
            functools.partial(route_kernel, groups, strip_width),
            grid_spec=pltpu.PrefetchScalarGridSpec(
                num_scalar_prefetch=1,
                grid=(1,),
                in_specs=[pl.BlockSpec(x.shape, lambda i, send: (0, 0)) for x in (product, from_them)],
                out_specs=[pl.BlockSpec((rows, size * strip_width), lambda i, send: (0, 0))] * steps,
                scratch_shapes=[pltpu.VMEM((steps, rows, size * strip_width), jnp.float32)],
            ),
            out_shape=[of(rows, size * strip_width)] * steps,
            compiler_params=params(12),
            name="route",
            cost_estimate=cost(0, 6 * rows * steps * size * strip_width),
        )(send_here, product, from_them)
    else:
        parts = jnp.stack(pieces_of(product + from_them, groups, strip_width))
        parts = [lax.dynamic_index_in_dim(parts, send_here[k], 0, False) for k in range(steps)]
    arrived = [lax.ppermute(part, AXES, perm) for part, perm in zip(parts, perms)]
    if strip_width % 128 == 0:
        return pl.pallas_call(
            functools.partial(assemble_kernel, size),
            grid_spec=pltpu.PrefetchScalarGridSpec(
                num_scalar_prefetch=1,
                grid=(1,),
                in_specs=[pl.BlockSpec(x.shape, lambda i, place: (0, 0)) for x in (*arrived, residual)],
                out_specs=pl.BlockSpec(residual.shape, lambda i, place: (0, 0)),
                scratch_shapes=[pltpu.VMEM((ctx, rows, strip_width), jnp.float32)],
            ),
            out_shape=of(*residual.shape),
            compiler_params=params(12),
            name="assemble",
            cost_estimate=cost(0, 3 * residual.size),
        )(place_here, *arrived, residual)
    blocks = jnp.stack([a[:, b * strip_width : (b + 1) * strip_width] for a in arrived for b in range(size)])
    projected = [lax.dynamic_index_in_dim(blocks, place_here[p], 0, False) for p in range(ctx)]
    return residual + jnp.concatenate(projected, axis=1)


def solution(mesh):
    placed = (
        P("ctx", "head"),
        P("ctx", "head"),
        P("ctx", "head"),
        P("head", None, None),
        P("head", None, None),
        P(None, ("ctx", "head")),
        P("ctx", "head"),
    )
    return jax.shard_map(
        functools.partial(body, mesh.shape["ctx"], mesh.shape["head"]),
        mesh=mesh,
        in_specs=placed,
        out_specs=P("ctx", "head"),
        check_vma=False,
    )
```

```python
import functools

import numpy as np

import jax
import jax.numpy as jnp
from jax import lax
from jax.experimental import pallas as pl
from jax.experimental.pallas import tpu as pltpu
from jax.sharding import PartitionSpec as P

HIGH = lax.Precision.HIGHEST
together = lax.optimization_barrier
AXES = ("ctx", "head")
PAIR = 2
EXTRA = 8
MIB = 1024 * 1024


def split(x):
    high = x.astype(jnp.bfloat16)
    return high, (x - high.astype(jnp.float32)).astype(jnp.bfloat16)


def dot3(a, b, dims=(((1,), (0,)), ((), ()))):
    a_high, a_low = split(a)
    b_high, b_low = split(b)
    dot = functools.partial(lax.dot_general, dimension_numbers=dims, preferred_element_type=jnp.float32)
    return dot(a_high, b_high) + (dot(a_high, b_low) + dot(a_low, b_high))


def features(rows, weights):
    scores = jnp.dot(rows, weights, precision=HIGH, preferred_element_type=jnp.float32)
    up = jnp.exp(scores - jnp.max(scores, axis=-1, keepdims=True))
    down = jnp.exp(jnp.min(scores, axis=-1, keepdims=True) - scores)
    up = up / jnp.sum(up, axis=-1, keepdims=True)
    down = down / jnp.sum(down, axis=-1, keepdims=True)
    return jnp.concatenate([up, down], axis=-1)


def arrange_kernel(plan, wide, starts, weight_ref, *refs):
    out_refs, sems = refs[:-1], refs[-1]
    copies = []
    for out_ref, picks in zip(out_refs, plan):
        for i, pick in enumerate(picks):
            source = weight_ref.at[pl.ds(pl.multiple_of(starts[pick], wide), wide), :]
            copies.append(pltpu.make_async_copy(source, out_ref.at[pl.ds(i * wide, wide), :], sems.at[len(copies)]))
            copies[-1].start()
    for copy in copies:
        copy.wait()


def key_kernel(first, k_ref, map_ref, v_ref, state_ref, feat_ref):
    heads, head_size, feat_half = map_ref.shape
    size = 2 * feat_half
    row = lax.broadcasted_iota(jnp.int32, (EXTRA, feat_half), 0)
    for i in range(heads):
        columns = slice(i * head_size, (i + 1) * head_size)
        feat = features(k_ref[:, columns], map_ref[i])
        feat_ref[i] = feat
        state_ref[i, :size, :] = dot3(feat, v_ref[:, columns], (((0,), (0,)), ((), ())))
        norm = jnp.sum(feat, axis=0, keepdims=True)
        state_ref[i, size:, :] = jnp.where(row < EXTRA // 2, norm[:, :feat_half], norm[:, feat_half:])


def attend(feat, key_feat, values, numer_ref, denom_ref):
    weights = dot3(feat, key_feat, (((1,), (1,)), ((), ())))
    row = lax.broadcasted_iota(jnp.int32, weights.shape, 0)
    column = lax.broadcasted_iota(jnp.int32, weights.shape, 1)
    weights = jnp.where(column <= row, weights, 0.0)
    numer_ref[0] = dot3(weights, values)
    denom_ref[0] = jnp.broadcast_to(jnp.sum(weights, axis=-1, keepdims=True), denom_ref.shape[1:])


def rest_kernel(first, *refs):
    k_ref, k_map_ref, q_ref, q_map_ref, v_ref, other_q_ref, other_q_map_ref, other_v_ref, other_feat_ref = refs[:9]
    state_ref, feat_ref, numer_ref, denom_ref, other_out_ref, other_numer_ref, other_denom_ref = refs[9:]
    heads, head_size, feat_half = k_map_ref.shape
    size = 2 * feat_half
    row = lax.broadcasted_iota(jnp.int32, (EXTRA, feat_half), 0)
    key_feat = features(k_ref[...], k_map_ref[0])
    state_ref[0, :size, :] = dot3(key_feat, v_ref[...], (((0,), (0,)), ((), ())))
    norm = jnp.sum(key_feat, axis=0, keepdims=True)
    state_ref[0, size:, :] = jnp.where(row < EXTRA // 2, norm[:, :feat_half], norm[:, feat_half:])
    feat = features(q_ref[...], q_map_ref[0])
    feat_ref[0] = feat
    attend(feat, key_feat, v_ref[...], numer_ref, denom_ref)
    feat = features(other_q_ref[...], other_q_map_ref[0])
    other_out_ref[0] = feat
    attend(feat, other_feat_ref[0], other_v_ref[...], other_numer_ref, other_denom_ref)


def mix_kernel(qfeat_ref, numer_ref, denom_ref, prior_ref, *refs):
    feat = qfeat_ref[0]
    size = feat.shape[1]
    norm = jnp.concatenate(
        [prior_ref[0, size : size + 1, :], prior_ref[0, size + EXTRA // 2 : size + EXTRA // 2 + 1, :]], axis=1
    )
    denom = denom_ref[0] + jnp.sum(feat * norm, axis=-1, keepdims=True)
    mixed = (numer_ref[0] + dot3(feat, prior_ref[0, :size, :])) / denom
    if len(refs) == 1:
        refs[0][...] = mixed
    else:
        below_ref, out_ref, both_ref = refs
        out_ref[...] = mixed
        both_ref[...] = jnp.concatenate([mixed, below_ref[...]], axis=0)


def project_kernel(terms, units, *refs):
    rows_refs, refs = refs[: 2 * units], refs[2 * units :]
    count = sum(stop - start for _, start, stop in terms)
    w_refs, rest, out_ref = refs[:count], refs[count:-1], refs[-1]
    out_ref[...] = rest[0][...] if rest else jnp.zeros_like(out_ref)
    lanes = w_refs[0].shape[1]
    for unit, start, stop in terms:
        a = jnp.concatenate([rows_refs[2 * unit][...], rows_refs[2 * unit + 1][...]], axis=0)
        w = jnp.concatenate([ref[...] for ref in w_refs[: stop - start]], axis=1)
        w_refs = w_refs[stop - start :]
        out_ref[:, start * lanes : stop * lanes] += dot3(a, w)


def pieces_of(product, groups, width):
    rows = product.shape[0] // 2
    return [
        jnp.concatenate([product[d * rows : (d + 1) * rows, b * width : (b + 1) * width] for b in group], axis=1)
        for d in range(2)
        for group in groups
    ]


def route_kernel(groups, width, send, mine_ref, other_ref, *refs):
    out_refs, pieces_ref = refs[:-1], refs[-1]
    product = mine_ref[...] + other_ref[...]
    for j, piece in enumerate(pieces_of(product, groups, width)):
        pieces_ref[j] = piece
    for k, out_ref in enumerate(out_refs):
        out_ref[...] = pieces_ref[send[k]]


def assemble_kernel(size, place, *refs):
    arrived, (residual_ref, out_ref, blocks_ref) = refs[:-3], refs[-3:]
    width = blocks_ref.shape[2]
    for k, ref in enumerate(arrived):
        for b in range(size):
            blocks_ref[k * size + b] = ref[:, b * width : (b + 1) * width]
    for p in range(blocks_ref.shape[0]):
        columns = slice(p * width, (p + 1) * width)
        out_ref[:, columns] = residual_ref[:, columns] + blocks_ref[place[p]]


def route_tables(ctx, heads, rels):
    groups = {}
    for column, rel in enumerate(rels):
        groups.setdefault(rel * heads // ctx, []).append(column)
    groups = [groups[key] for key in sorted(groups)]
    size = len(groups[0])
    targets = {}
    for c in range(ctx):
        for h in range(heads):
            found = {}
            for d, step in enumerate((0, PAIR)):
                for g, columns in enumerate(groups):
                    to = (c ^ step) * heads + (c ^ rels[columns[0]]) * heads // ctx
                    found[to] = d * len(groups) + g
            targets[c * heads + h] = found
    classes = {}
    for device in sorted(targets):
        classes.setdefault(tuple(sorted(targets[device])), []).append(device)
    steps = 2 * len(groups)
    perms = [[] for _ in range(steps)]
    send = np.zeros((ctx * heads, steps), np.int32)
    arrives = {}
    for ends, sources in classes.items():
        for i, source in enumerate(sources):
            for k in range(steps):
                to = ends[i ^ k]
                perms[k].append((source, to))
                send[source, k] = targets[source][to]
                arrives[to, source] = k
    place = np.zeros((ctx * heads, ctx), np.int32)
    for c in range(ctx):
        for h in range(heads):
            for p in range(ctx):
                column_ctx, source_h = divmod(h * ctx + p, heads)
                source_c = (c & ~PAIR) | (column_ctx & PAIR)
                k = arrives[c * heads + h, source_c * heads + source_h]
                rel = source_c ^ column_ctx
                group = [g for g in groups if rels.index(rel) in g][0]
                place[c * heads + h, p] = k * size + group.index(rels.index(rel))
    return groups, perms, send, place


def body(ctx, heads, queries, keys, values, query_map, key_map, out_weight, residual):
    rows = queries.shape[0]
    heads_here, head_size, feat_half = query_map.shape
    feat_size = 2 * feat_half
    half = heads_here // 2
    wide = half * head_size
    depth = out_weight.shape[0] // heads
    strip_width = out_weight.shape[1]
    c = lax.axis_index("ctx")
    h = lax.axis_index("head")
    me = c * heads + h
    odd = c & 1

    def swap(x, by_ctx, by_head=0, keep=lambda source: True):
        pairs = [
            (i * heads + j, (i ^ by_ctx) * heads + (j ^ by_head))
            for i in range(ctx)
            for j in range(heads)
            if keep(i)
        ]
        return lax.ppermute(x, AXES, pairs)

    def of(*shape):
        return jax.ShapeDtypeStruct(shape, jnp.float32)

    def cost(products, count, exps=0):
        return pl.CostEstimate(flops=2 * products, bytes_accessed=4 * count, transcendentals=exps)

    def params(mib):
        return pltpu.CompilerParams(vmem_limit_bytes=mib * MIB)

    def head_block(size, lanes):
        return pl.BlockSpec((1, size, lanes), lambda i, *_: (i, 0, 0))

    def key_part(first):
        columns = pl.BlockSpec((rows, wide), lambda i, first: (0, first[0]))
        maps = pl.BlockSpec((half, head_size, feat_half), lambda i, first: (first[0], 0, 0))
        shapes = [of(half, feat_size + EXTRA, head_size), of(half, rows, feat_size)]
        return pl.pallas_call(
            key_kernel,
            grid_spec=pltpu.PrefetchScalarGridSpec(
                num_scalar_prefetch=1,
                grid=(1,),
                in_specs=[columns, maps, columns],
                out_specs=[pl.BlockSpec(s.shape, lambda i, first: (0, 0, 0)) for s in shapes],
            ),
            out_shape=shapes,
            compiler_params=params(60),
            name="key_part",
            cost_estimate=cost(
                6 * half * rows * head_size * (feat_half + feat_size),
                half * rows * (2 * head_size + 2 * feat_size),
                half * rows * feat_size,
            ),
        )(first, keys, key_map, values)

    def rest_part(firsts, other_feat):
        def columns(which):
            return pl.BlockSpec((rows, head_size), lambda i, first: (0, first[which] * half + i))

        def maps(which):
            return pl.BlockSpec((1, head_size, feat_half), lambda i, first: (first[which] * half + i, 0, 0))

        query_shapes = [of(half, rows, feat_size), of(half, rows, head_size), of(half, rows, head_size)]
        shapes = [of(half, feat_size + EXTRA, head_size), *query_shapes, *query_shapes]
        outs = pl.pallas_call(
            rest_kernel,
            grid_spec=pltpu.PrefetchScalarGridSpec(
                num_scalar_prefetch=1,
                grid=(half,),
                in_specs=[columns(0), maps(0), columns(0), maps(0), columns(0)]
                + [columns(1), maps(1), columns(1), head_block(rows, feat_size)],
                out_specs=[head_block(*shape.shape[1:]) for shape in shapes],
            ),
            out_shape=shapes,
            compiler_params=params(48),
            name="rest_part",
            cost_estimate=cost(
                6 * half * rows * (head_size * (3 * feat_half + feat_size) + 2 * rows * (feat_size + head_size)),
                half * rows * (8 * head_size + 4 * feat_size),
                3 * half * rows * feat_size,
            ),
        )(firsts, keys, key_map, queries, query_map, values, queries, query_map, values, other_feat)
        return outs[0], outs[1:4], outs[4:]

    def mix(qfeat, numer, denom, prior, below=None):
        columns = pl.BlockSpec((rows, head_size), lambda i: (0, i))
        out_specs, shapes = columns, of(rows, wide)
        if below is not None:
            out_specs = [columns, pl.BlockSpec((2 * rows, head_size), lambda i: (0, i))]
            shapes = [shapes, of(2 * rows, wide)]
        return pl.pallas_call(
            mix_kernel,
            grid=(half,),
            in_specs=[
                head_block(rows, feat_size),
                head_block(rows, head_size),
                head_block(rows, head_size),
                head_block(feat_size + EXTRA, head_size),
            ]
            + [columns] * (below is not None),
            out_specs=out_specs,
            out_shape=shapes,
            compiler_params=params(12),
            name="mix",
            cost_estimate=cost(
                3 * half * rows * feat_size * head_size, half * rows * (3 * head_size + 2 * feat_size)
            ),
        )(qfeat, numer, denom, prior, *([] if below is None else [below]))

    even = range(0, heads, 2)
    blocks = heads // 2
    bits = [1 << b for b in reversed(range(ctx.bit_length() - 1)) if 1 << b != PAIR]
    far, near = bits[-2:]
    rels = [0]
    for bit in bits[:-2]:
        rels = rels + [r | bit for r in rels]
    rels = [r | s for s in (0, near, far, far | near) for r in rels]

    def arranged(weight, starts, plan):
        shapes = [of(len(picks) * wide, strip_width) for picks in plan]
        count = sum(len(picks) for picks in plan)
        return pl.pallas_call(
            functools.partial(arrange_kernel, plan, wide),
            grid_spec=pltpu.PrefetchScalarGridSpec(
                num_scalar_prefetch=1,
                grid=(1,),
                in_specs=[pl.BlockSpec(memory_space=pl.ANY)],
                out_specs=[pl.BlockSpec(memory_space=pl.ANY)] * len(plan),
                scratch_shapes=[pltpu.SemaphoreType.DMA((count,))],
            ),
            out_shape=shapes,
            compiler_params=params(16),
            name="arrange",
            cost_estimate=cost(0, 2 * count * wide * strip_width),
        )(starts, weight)

    def widen(x):
        for bit in bits[:-2]:
            x = jnp.concatenate([x, swap(x, bit)], axis=1)
        return x

    order = [(which, d) for which in (odd, 1 - odd) for d in even]
    part = len(order) // 4
    own, other = odd.reshape(1), (1 - odd).reshape(1)
    other_state, other_feat = key_part(other)
    out_weight, other_state = together((out_weight, other_state))
    starts = jnp.stack([(h ^ flip ^ d) * depth + which * wide for flip in (0, 1) for which, d in order])
    count = len(order)
    spans = [(0, part), (part, 3 * part), (3 * part, count), (0, count)]
    plan = [list(range(*span)) for span in spans]
    plan += [list(range(count + start, count + stop)) for start, stop in ((0, 2 * part), (2 * part, count), (0, count))]
    *kept_parts, kept, given_1, given_2, given = arranged(out_weight, starts, plan)
    kept_parts, kept = [widen(x) for x in kept_parts], widen(kept)
    far_1 = swap(kept_parts[0], far)
    from_neighbour = swap(other_state, 1)
    own_state, own_query, other_query = rest_part(jnp.concatenate([own, other]), other_feat)
    groups, perms, send, place = route_tables(ctx, heads, rels)
    steps, size = len(perms), len(groups[0])
    send_here = jnp.asarray(send)[me]
    place_here = jnp.asarray(place)[me]

    from_neighbour, own_state, far_1, kept_parts, kept, given_1, given_2, given = together(
        (from_neighbour, own_state, far_1, kept_parts, kept, given_1, given_2, given)
    )
    far_2 = swap(kept_parts[1], far)
    kept_near = swap(kept, near)
    taken, taken_1, taken_2 = [widen(swap(x, 0, 1)) for x in (given, given_1, given_2)]
    earlier = jnp.where(odd == 0, own_state, from_neighbour)
    total = own_state + from_neighbour
    before = jnp.zeros_like(total)
    bit = 2
    while 2 * bit < ctx:
        got = swap(total, bit)
        before = before + jnp.where((c & bit) != 0, got, 0.0)
        total = total + got
        bit *= 2
    total, before, far_2, kept_near, taken, taken_1, taken_2, far_1 = together(
        (total, before, far_2, kept_near, taken, taken_1, taken_2, far_1)
    )
    taken_near = swap(taken, near)
    both_1 = swap(far_1, near)
    got = swap(total, bit | PAIR, keep=lambda i: i & PAIR and not i & bit)
    got, kept_parts[2] = together((got, kept_parts[2]))
    met = swap(got, PAIR, keep=lambda i: i & bit and not i & PAIR)
    far_3 = swap(kept_parts[2], far)
    met, far_3, taken_near, both_1, taken_1 = together((met, far_3, taken_near, both_1, taken_1))
    before = before + got + met

    other_prior = swap(before + jnp.where(odd == 0, earlier, 0.0), 1)
    own_mixed = mix(*own_query, before + jnp.where(odd == 1, earlier, 0.0))
    head_bits = [1 << b for b in range(1, heads.bit_length() - 1)]

    def spread(pieces):
        for bit in head_bits[1:]:
            for (d, j), (x, i) in list(pieces.items()):
                pieces[d, j | bit] = (swap(x[i * rows : (i + 1) * rows], 0, bit), 0)
        return [(pieces[0, j], pieces[PAIR, j]) for j in even]

    met, across = swap(own_mixed, PAIR), swap(own_mixed, 0, head_bits[0])
    far_4 = swap(taken_1, far)
    both_3 = swap(far_3, near)
    other_prior, far_2, far_4, both_3, met, across, taken_2 = together(
        (other_prior, far_2, far_4, both_3, met, across, taken_2)
    )
    other_mixed, both = mix(*other_query, other_prior, met)
    other_met = swap(other_mixed, PAIR)
    both = swap(both, 0, head_bits[0])
    far_5 = swap(taken_2, far)
    both_2 = swap(far_2, near)
    both_4 = swap(far_4, near)
    other_met, both, far_5, both_2, both_4, send_here, place_here = together(
        (other_met, both, far_5, both_2, both_4, send_here, place_here)
    )
    both_5 = swap(far_5, near)
    last = swap(other_met, 0, head_bits[0])
    own_pieces = spread(
        {(0, 0): (own_mixed, 0), (PAIR, 0): (met, 0), (0, head_bits[0]): (across, 0), (PAIR, head_bits[0]): (both, 1)}
    )

    def other_pieces(last):
        pieces = {(0, 0): (other_mixed, 0), (PAIR, 0): (other_met, 0), (0, head_bits[0]): (both, 0)}
        return spread({**pieces, (PAIR, head_bits[0]): (last, 0)})

    lanes = kept.shape[1]

    def strip(parts, crossed=False):
        places = [(x, start * part + i) for x, start, stop in parts for i in range((stop - start) * part)]
        return places[blocks:] + places[:blocks] if crossed else places

    def project(pieces, strips, runs, total=None, column=0):
        runs = [(u, start, stop) for q, start, stop in runs for u in range(q * part, (q + 1) * part)]
        used = sorted({u for u, _, _ in runs})
        weights = [strips[s][u] for u, start, stop in runs for s in range(start, stop)]
        shape = (2 * rows, len(strips) * lanes)
        extra = [] if total is None else [total]
        terms = [(used.index(u), start, stop) for u, start, stop in runs]
        return pl.pallas_call(
            functools.partial(project_kernel, terms, len(used)),
            grid=(1,),
            in_specs=[pl.BlockSpec((rows, wide), lambda i, block=block: (block, 0)) for u in used for _, block in pieces[u]]
            + [pl.BlockSpec((wide, lanes), lambda i, unit=unit: (unit, 0)) for _, unit in weights]
            + [pl.BlockSpec(shape, lambda i: (0, column))] * len(extra),
            out_specs=pl.BlockSpec(shape, lambda i: (0, 0)),
            out_shape=of(*shape),
            compiler_params=params(24),
            name="project",
            cost_estimate=cost(6 * rows * wide * len(weights) * lanes, wide * lanes * len(weights) + 2 * rows * shape[1]),
        )(*[x for u in used for x, _ in pieces[u]], *[x for x, _ in weights], *extra)

    theirs = [
        strip([(taken, 0, 4)]),
        strip([(taken_near, 0, 4)], True),
        strip([(far_4, 0, 2), (far_5, 0, 2)]),
        strip([(both_4, 0, 2), (both_5, 0, 2)], True),
    ]
    mine = [
        strip([(kept, 0, 4)]),
        strip([(kept_near, 0, 4)], True),
        strip([(far_1, 0, 1), (far_2, 0, 2), (far_3, 0, 1)]),
        strip([(both_1, 0, 1), (both_2, 0, 2), (both_3, 0, 1)], True),
    ]
    pieces = own_pieces + other_pieces(last)
    product = project(pieces, theirs + mine, [(0, 0, 3), (0, 4, 8), (1, 0, 3), (1, 4, 8)])
    product = project(pieces, theirs + mine, [(2, 0, 8)], product)
    product, last = together((product, last))
    pieces = own_pieces + other_pieces(last)
    from_them = swap(project(pieces, theirs, [(3, 0, 4), (0, 3, 4), (1, 3, 4)], product, 0), 0, 1)
    product = project(pieces, mine, [(3, 0, 4)], product, 1)

    if strip_width % 128 == 0:
        parts = pl.pallas_call(
            functools.partial(route_kernel, groups, strip_width),
            grid_spec=pltpu.PrefetchScalarGridSpec(
                num_scalar_prefetch=1,
                grid=(1,),
                in_specs=[pl.BlockSpec(x.shape, lambda i, send: (0, 0)) for x in (product, from_them)],
                out_specs=[pl.BlockSpec((rows, size * strip_width), lambda i, send: (0, 0))] * steps,
                scratch_shapes=[pltpu.VMEM((steps, rows, size * strip_width), jnp.float32)],
            ),
            out_shape=[of(rows, size * strip_width)] * steps,
            compiler_params=params(12),
            name="route",
            cost_estimate=cost(0, 6 * rows * steps * size * strip_width),
        )(send_here, product, from_them)
    else:
        parts = jnp.stack(pieces_of(product + from_them, groups, strip_width))
        parts = [lax.dynamic_index_in_dim(parts, send_here[k], 0, False) for k in range(steps)]
    arrived = [lax.ppermute(part, AXES, perm) for part, perm in zip(parts, perms)]
    if strip_width % 128 == 0:
        return pl.pallas_call(
            functools.partial(assemble_kernel, size),
            grid_spec=pltpu.PrefetchScalarGridSpec(
                num_scalar_prefetch=1,
                grid=(1,),
                in_specs=[pl.BlockSpec(x.shape, lambda i, place: (0, 0)) for x in (*arrived, residual)],
                out_specs=pl.BlockSpec(residual.shape, lambda i, place: (0, 0)),
                scratch_shapes=[pltpu.VMEM((ctx, rows, strip_width), jnp.float32)],
            ),
            out_shape=of(*residual.shape),
            compiler_params=params(12),
            name="assemble",
            cost_estimate=cost(0, 3 * residual.size),
        )(place_here, *arrived, residual)
    blocks = jnp.stack([a[:, b * strip_width : (b + 1) * strip_width] for a in arrived for b in range(size)])
    projected = [lax.dynamic_index_in_dim(blocks, place_here[p], 0, False) for p in range(ctx)]
    return residual + jnp.concatenate(projected, axis=1)


def solution(mesh):
    placed = (
        P("ctx", "head"),
        P("ctx", "head"),
        P("ctx", "head"),
        P("head", None, None),
        P("head", None, None),
        P(None, ("ctx", "head")),
        P("ctx", "head"),
    )
    return jax.shard_map(
        functools.partial(body, mesh.shape["ctx"], mesh.shape["head"]),
        mesh=mesh,
        in_specs=placed,
        out_specs=P("ctx", "head"),
        check_vma=False,
    )
```

```python
import functools

import numpy as np

import jax
import jax.numpy as jnp
from jax import lax
from jax.experimental import pallas as pl
from jax.experimental.pallas import tpu as pltpu
from jax.sharding import PartitionSpec as P

HIGH = lax.Precision.HIGHEST
together = lax.optimization_barrier
AXES = ("ctx", "head")
PAIR = 2
EXTRA = 8
MIB = 1024 * 1024


def split(x):
    high = x.astype(jnp.bfloat16)
    return high, (x - high.astype(jnp.float32)).astype(jnp.bfloat16)


def dot3(a, b, dims=(((1,), (0,)), ((), ()))):
    a_high, a_low = split(a)
    b_high, b_low = split(b)
    dot = functools.partial(lax.dot_general, dimension_numbers=dims, preferred_element_type=jnp.float32)
    return dot(a_high, b_high) + (dot(a_high, b_low) + dot(a_low, b_high))


def features(rows, weights):
    scores = jnp.dot(rows, weights, precision=HIGH, preferred_element_type=jnp.float32)
    up = jnp.exp(scores - jnp.max(scores, axis=-1, keepdims=True))
    down = jnp.exp(jnp.min(scores, axis=-1, keepdims=True) - scores)
    up = up / jnp.sum(up, axis=-1, keepdims=True)
    down = down / jnp.sum(down, axis=-1, keepdims=True)
    return jnp.concatenate([up, down], axis=-1)


def arrange_kernel(plan, wide, starts, weight_ref, *refs):
    out_refs, sems = refs[:-1], refs[-1]
    copies = []
    for out_ref, picks in zip(out_refs, plan):
        for i, pick in enumerate(picks):
            source = weight_ref.at[pl.ds(pl.multiple_of(starts[pick], wide), wide), :]
            copies.append(pltpu.make_async_copy(source, out_ref.at[pl.ds(i * wide, wide), :], sems.at[len(copies)]))
            copies[-1].start()
    for copy in copies:
        copy.wait()


def key_kernel(first, k_ref, map_ref, v_ref, state_ref, feat_ref):
    heads, head_size, feat_half = map_ref.shape
    size = 2 * feat_half
    row = lax.broadcasted_iota(jnp.int32, (EXTRA, feat_half), 0)
    for i in range(heads):
        columns = slice(i * head_size, (i + 1) * head_size)
        feat = features(k_ref[:, columns], map_ref[i])
        feat_ref[i] = feat
        state_ref[i, :size, :] = dot3(feat, v_ref[:, columns], (((0,), (0,)), ((), ())))
        norm = jnp.sum(feat, axis=0, keepdims=True)
        state_ref[i, size:, :] = jnp.where(row < EXTRA // 2, norm[:, :feat_half], norm[:, feat_half:])


def attend(feat, key_feat, values, numer_ref, denom_ref):
    weights = dot3(feat, key_feat, (((1,), (1,)), ((), ())))
    row = lax.broadcasted_iota(jnp.int32, weights.shape, 0)
    column = lax.broadcasted_iota(jnp.int32, weights.shape, 1)
    weights = jnp.where(column <= row, weights, 0.0)
    numer_ref[0] = dot3(weights, values)
    denom_ref[0] = jnp.broadcast_to(jnp.sum(weights, axis=-1, keepdims=True), denom_ref.shape[1:])


def rest_kernel(first, *refs):
    k_ref, k_map_ref, q_ref, q_map_ref, v_ref, other_q_ref, other_q_map_ref, other_v_ref, other_feat_ref = refs[:9]
    state_ref, feat_ref, numer_ref, denom_ref, other_out_ref, other_numer_ref, other_denom_ref = refs[9:]
    heads, head_size, feat_half = k_map_ref.shape
    size = 2 * feat_half
    row = lax.broadcasted_iota(jnp.int32, (EXTRA, feat_half), 0)
    key_feat = features(k_ref[...], k_map_ref[0])
    state_ref[0, :size, :] = dot3(key_feat, v_ref[...], (((0,), (0,)), ((), ())))
    norm = jnp.sum(key_feat, axis=0, keepdims=True)
    state_ref[0, size:, :] = jnp.where(row < EXTRA // 2, norm[:, :feat_half], norm[:, feat_half:])
    feat = features(q_ref[...], q_map_ref[0])
    feat_ref[0] = feat
    attend(feat, key_feat, v_ref[...], numer_ref, denom_ref)
    feat = features(other_q_ref[...], other_q_map_ref[0])
    other_out_ref[0] = feat
    attend(feat, other_feat_ref[0], other_v_ref[...], other_numer_ref, other_denom_ref)


def mix_kernel(qfeat_ref, numer_ref, denom_ref, prior_ref, *refs):
    feat = qfeat_ref[0]
    size = feat.shape[1]
    norm = jnp.concatenate(
        [prior_ref[0, size : size + 1, :], prior_ref[0, size + EXTRA // 2 : size + EXTRA // 2 + 1, :]], axis=1
    )
    denom = denom_ref[0] + jnp.sum(feat * norm, axis=-1, keepdims=True)
    mixed = (numer_ref[0] + dot3(feat, prior_ref[0, :size, :])) / denom
    if len(refs) == 1:
        refs[0][...] = mixed
    else:
        below_ref, out_ref, both_ref = refs
        out_ref[...] = mixed
        both_ref[...] = jnp.concatenate([mixed, below_ref[...]], axis=0)


def project_kernel(terms, units, *refs):
    rows_refs, refs = refs[: 2 * units], refs[2 * units :]
    count = sum(stop - start for _, start, stop in terms)
    w_refs, rest, out_ref = refs[:count], refs[count:-1], refs[-1]
    out_ref[...] = rest[0][...] if rest else jnp.zeros_like(out_ref)
    lanes = w_refs[0].shape[1]
    for unit, start, stop in terms:
        a = jnp.concatenate([rows_refs[2 * unit][...], rows_refs[2 * unit + 1][...]], axis=0)
        w = jnp.concatenate([ref[...] for ref in w_refs[: stop - start]], axis=1)
        w_refs = w_refs[stop - start :]
        out_ref[:, start * lanes : stop * lanes] += dot3(a, w)


def pieces_of(product, groups, width):
    rows = product.shape[0] // 2
    return [
        jnp.concatenate([product[d * rows : (d + 1) * rows, b * width : (b + 1) * width] for b in group], axis=1)
        for d in range(2)
        for group in groups
    ]


def route_kernel(groups, width, send, mine_ref, other_ref, *refs):
    out_refs, pieces_ref = refs[:-1], refs[-1]
    product = mine_ref[...] + other_ref[...]
    for j, piece in enumerate(pieces_of(product, groups, width)):
        pieces_ref[j] = piece
    for k, out_ref in enumerate(out_refs):
        out_ref[...] = pieces_ref[send[k]]


def assemble_kernel(size, place, *refs):
    arrived, (residual_ref, out_ref, blocks_ref) = refs[:-3], refs[-3:]
    width = blocks_ref.shape[2]
    for k, ref in enumerate(arrived):
        for b in range(size):
            blocks_ref[k * size + b] = ref[:, b * width : (b + 1) * width]
    for p in range(blocks_ref.shape[0]):
        columns = slice(p * width, (p + 1) * width)
        out_ref[:, columns] = residual_ref[:, columns] + blocks_ref[place[p]]


def route_tables(ctx, heads, rels):
    groups = {}
    for column, rel in enumerate(rels):
        groups.setdefault(rel * heads // ctx, []).append(column)
    groups = [groups[key] for key in sorted(groups)]
    size = len(groups[0])
    targets = {}
    for c in range(ctx):
        for h in range(heads):
            found = {}
            for d, step in enumerate((0, PAIR)):
                for g, columns in enumerate(groups):
                    to = (c ^ step) * heads + (c ^ rels[columns[0]]) * heads // ctx
                    found[to] = d * len(groups) + g
            targets[c * heads + h] = found
    classes = {}
    for device in sorted(targets):
        classes.setdefault(tuple(sorted(targets[device])), []).append(device)
    steps = 2 * len(groups)
    perms = [[] for _ in range(steps)]
    send = np.zeros((ctx * heads, steps), np.int32)
    arrives = {}
    for ends, sources in classes.items():
        for i, source in enumerate(sources):
            for k in range(steps):
                to = ends[i ^ k]
                perms[k].append((source, to))
                send[source, k] = targets[source][to]
                arrives[to, source] = k
    place = np.zeros((ctx * heads, ctx), np.int32)
    for c in range(ctx):
        for h in range(heads):
            for p in range(ctx):
                column_ctx, source_h = divmod(h * ctx + p, heads)
                source_c = (c & ~PAIR) | (column_ctx & PAIR)
                k = arrives[c * heads + h, source_c * heads + source_h]
                rel = source_c ^ column_ctx
                group = [g for g in groups if rels.index(rel) in g][0]
                place[c * heads + h, p] = k * size + group.index(rels.index(rel))
    return groups, perms, send, place


def body(ctx, heads, queries, keys, values, query_map, key_map, out_weight, residual):
    rows = queries.shape[0]
    heads_here, head_size, feat_half = query_map.shape
    feat_size = 2 * feat_half
    half = heads_here // 2
    wide = half * head_size
    depth = out_weight.shape[0] // heads
    strip_width = out_weight.shape[1]
    c = lax.axis_index("ctx")
    h = lax.axis_index("head")
    me = c * heads + h
    odd = c & 1

    def swap(x, by_ctx, by_head=0, keep=lambda c: True):
        pairs = [
            (i * heads + j, (i ^ by_ctx) * heads + (j ^ by_head))
            for i in range(ctx)
            for j in range(heads)
            if keep(i)
        ]
        return lax.ppermute(x, AXES, pairs)

    def of(*shape):
        return jax.ShapeDtypeStruct(shape, jnp.float32)

    def cost(products, count, exps=0):
        return pl.CostEstimate(flops=2 * products, bytes_accessed=4 * count, transcendentals=exps)

    def params(mib):
        return pltpu.CompilerParams(vmem_limit_bytes=mib * MIB)

    def head_block(size, lanes):
        return pl.BlockSpec((1, size, lanes), lambda i, *_: (i, 0, 0))

    def key_part(first):
        columns = pl.BlockSpec((rows, wide), lambda i, first: (0, first[0]))
        maps = pl.BlockSpec((half, head_size, feat_half), lambda i, first: (first[0], 0, 0))
        shapes = [of(half, feat_size + EXTRA, head_size), of(half, rows, feat_size)]
        return pl.pallas_call(
            key_kernel,
            grid_spec=pltpu.PrefetchScalarGridSpec(
                num_scalar_prefetch=1,
                grid=(1,),
                in_specs=[columns, maps, columns],
                out_specs=[pl.BlockSpec(s.shape, lambda i, first: (0, 0, 0)) for s in shapes],
            ),
            out_shape=shapes,
            compiler_params=params(60),
            name="key_part",
            cost_estimate=cost(
                6 * half * rows * head_size * (feat_half + feat_size),
                half * rows * (2 * head_size + 2 * feat_size),
                half * rows * feat_size,
            ),
        )(first, keys, key_map, values)

    def rest_part(firsts, other_feat):
        def columns(which):
            return pl.BlockSpec((rows, head_size), lambda i, first: (0, first[which] * half + i))

        def maps(which):
            return pl.BlockSpec((1, head_size, feat_half), lambda i, first: (first[which] * half + i, 0, 0))

        query_shapes = [of(half, rows, feat_size), of(half, rows, head_size), of(half, rows, head_size)]
        shapes = [of(half, feat_size + EXTRA, head_size), *query_shapes, *query_shapes]
        outs = pl.pallas_call(
            rest_kernel,
            grid_spec=pltpu.PrefetchScalarGridSpec(
                num_scalar_prefetch=1,
                grid=(half,),
                in_specs=[columns(0), maps(0), columns(0), maps(0), columns(0)]
                + [columns(1), maps(1), columns(1), head_block(rows, feat_size)],
                out_specs=[head_block(*shape.shape[1:]) for shape in shapes],
            ),
            out_shape=shapes,
            compiler_params=params(40),
            name="rest_part",
            cost_estimate=cost(
                6 * half * rows * (head_size * (3 * feat_half + feat_size) + 2 * rows * (feat_size + head_size)),
                half * rows * (8 * head_size + 4 * feat_size),
                3 * half * rows * feat_size,
            ),
        )(firsts, keys, key_map, queries, query_map, values, queries, query_map, values, other_feat)
        return outs[0], outs[1:4], outs[4:]

    def mix(qfeat, numer, denom, prior, below=None):
        columns = pl.BlockSpec((rows, head_size), lambda i: (0, i))
        out_specs, shapes = columns, of(rows, wide)
        if below is not None:
            out_specs = [columns, pl.BlockSpec((2 * rows, head_size), lambda i: (0, i))]
            shapes = [shapes, of(2 * rows, wide)]
        return pl.pallas_call(
            mix_kernel,
            grid=(half,),
            in_specs=[
                head_block(rows, feat_size),
                head_block(rows, head_size),
                head_block(rows, head_size),
                head_block(feat_size + EXTRA, head_size),
            ]
            + [columns] * (below is not None),
            out_specs=out_specs,
            out_shape=shapes,
            compiler_params=params(12),
            name="mix",
            cost_estimate=cost(
                3 * half * rows * feat_size * head_size, half * rows * (3 * head_size + 2 * feat_size)
            ),
        )(qfeat, numer, denom, prior, *([] if below is None else [below]))

    even = range(0, heads, 2)
    blocks = heads // 2
    bits = [1 << b for b in reversed(range(ctx.bit_length() - 1)) if 1 << b != PAIR]
    far, near = bits[-2:]
    rels = [0]
    for bit in bits[:-2]:
        rels = rels + [r | bit for r in rels]
    rels = [r | s for s in (0, near, far, far | near) for r in rels]

    def arranged(weight, starts, plan):
        shapes = [of(len(picks) * wide, strip_width) for picks in plan]
        count = sum(len(picks) for picks in plan)
        return pl.pallas_call(
            functools.partial(arrange_kernel, plan, wide),
            grid_spec=pltpu.PrefetchScalarGridSpec(
                num_scalar_prefetch=1,
                grid=(1,),
                in_specs=[pl.BlockSpec(memory_space=pl.ANY)],
                out_specs=[pl.BlockSpec(memory_space=pl.ANY)] * len(plan),
                scratch_shapes=[pltpu.SemaphoreType.DMA((count,))],
            ),
            out_shape=shapes,
            compiler_params=params(12),
            name="arrange",
            cost_estimate=cost(0, 2 * count * wide * strip_width),
        )(starts, weight)

    def widen(x):
        for bit in bits[:-2]:
            x = jnp.concatenate([x, swap(x, bit)], axis=1)
        return x

    order = [(which, d) for which in (odd, 1 - odd) for d in even]
    part = len(order) // 4
    own, other = odd.reshape(1), (1 - odd).reshape(1)
    other_state, other_feat = key_part(other)
    out_weight, other_state = together((out_weight, other_state))
    starts = jnp.stack([(h ^ flip ^ d) * depth + which * wide for flip in (0, 1) for which, d in order])
    count = len(order)
    (first_part,) = arranged(out_weight, starts, [list(range(part))])
    first_part = widen(first_part)
    far_1 = swap(first_part, far)
    from_neighbour = swap(other_state, 1)
    own_state, own_query, other_query = rest_part(jnp.concatenate([own, other]), other_feat)
    out_weight, own_state = together((out_weight, own_state))
    spans = [(part, 3 * part), (3 * part, count), (0, count)]
    spans += [(count, count + 2 * part), (count + 2 * part, 2 * count), (count, 2 * count)]
    kept_2, kept_3, kept, given_1, given_2, given = arranged(out_weight, starts, [list(range(*span)) for span in spans])
    kept_2, kept_3, kept = [widen(x) for x in (kept_2, kept_3, kept)]
    groups, perms, send, place = route_tables(ctx, heads, rels)
    steps, size = len(perms), len(groups[0])
    send_here = jnp.asarray(send)[me]
    place_here = jnp.asarray(place)[me]

    from_neighbour, own_state, far_1, kept_2, kept, given_1, given_2, given = together(
        (from_neighbour, own_state, far_1, kept_2, kept, given_1, given_2, given)
    )
    far_2 = swap(kept_2, far)
    kept_near = swap(kept, near)
    taken, taken_1, taken_2 = [widen(swap(x, 0, 1)) for x in (given, given_1, given_2)]
    earlier = jnp.where(odd == 0, own_state, from_neighbour)
    total = own_state + from_neighbour
    before = jnp.zeros_like(total)
    bit = 2
    while 2 * bit < ctx:
        got = swap(total, bit)
        before = before + jnp.where((c & bit) != 0, got, 0.0)
        total = total + got
        bit *= 2
    total, before, far_2, kept_near, taken, taken_1, taken_2, far_1 = together(
        (total, before, far_2, kept_near, taken, taken_1, taken_2, far_1)
    )
    taken_near = swap(taken, near)
    both_1 = swap(far_1, near)
    second = (c & PAIR) != 0
    got = swap(jnp.where(second, total[half // 2 :], total[: half // 2]), bit, keep=lambda i: not i & bit)
    got, kept_3 = together((got, kept_3))
    met = swap(got, PAIR, keep=lambda i: i & bit)
    far_3 = swap(kept_3, far)
    got = jnp.concatenate([jnp.where(second, met, got), jnp.where(second, got, met)])
    got, taken_near, both_1, taken_1, far_2 = together((got, taken_near, both_1, taken_1, far_2))
    before = before + got

    other_prior = swap(before + jnp.where(odd == 0, earlier, 0.0), 1)
    own_mixed = mix(*own_query, before + jnp.where(odd == 1, earlier, 0.0))
    head_bits = [1 << b for b in range(1, heads.bit_length() - 1)]

    def spread(pieces):
        for bit in head_bits[1:]:
            for (d, j), (x, i) in list(pieces.items()):
                pieces[d, j | bit] = (swap(x[i * rows : (i + 1) * rows], 0, bit), 0)
        return [(pieces[0, j], pieces[PAIR, j]) for j in even]

    own_mixed, far_3 = together((own_mixed, far_3))
    met, across = swap(own_mixed, PAIR), swap(own_mixed, 0, head_bits[0])
    far_4 = swap(taken_1, far)
    both_2 = swap(far_2, near)
    other_prior, far_3, far_4, both_2, met, across, taken_2 = together(
        (other_prior, far_3, far_4, both_2, met, across, taken_2)
    )
    other_mixed, both = mix(*other_query, other_prior, met)
    other_met = swap(other_mixed, PAIR)
    both = swap(both, 0, head_bits[0])
    far_5 = swap(taken_2, far)
    both_3 = swap(far_3, near)
    both_4 = swap(far_4, near)
    other_met, both, far_5, both_3, both_4, send_here, place_here = together(
        (other_met, both, far_5, both_3, both_4, send_here, place_here)
    )
    both_5 = swap(far_5, near)
    last = swap(other_met, 0, head_bits[0])
    own_pieces = spread(
        {(0, 0): (own_mixed, 0), (PAIR, 0): (met, 0), (0, head_bits[0]): (across, 0), (PAIR, head_bits[0]): (both, 1)}
    )

    def other_pieces(last):
        pieces = {(0, 0): (other_mixed, 0), (PAIR, 0): (other_met, 0), (0, head_bits[0]): (both, 0)}
        return spread({**pieces, (PAIR, head_bits[0]): (last, 0)})

    lanes = kept.shape[1]

    def strip(parts, crossed=False):
        places = [(x, start * part + i) for x, start, stop in parts for i in range((stop - start) * part)]
        return places[blocks:] + places[:blocks] if crossed else places

    def project(pieces, strips, runs, total=None, column=0):
        runs = [(u, start, stop) for q, start, stop in runs for u in range(q * part, (q + 1) * part)]
        used = sorted({u for u, _, _ in runs})
        weights = [strips[s][u] for u, start, stop in runs for s in range(start, stop)]
        shape = (2 * rows, len(strips) * lanes)
        extra = [] if total is None else [total]
        terms = [(used.index(u), start, stop) for u, start, stop in runs]
        return pl.pallas_call(
            functools.partial(project_kernel, terms, len(used)),
            grid=(1,),
            in_specs=[pl.BlockSpec((rows, wide), lambda i, block=block: (block, 0)) for u in used for _, block in pieces[u]]
            + [pl.BlockSpec((wide, lanes), lambda i, unit=unit: (unit, 0)) for _, unit in weights]
            + [pl.BlockSpec(shape, lambda i: (0, column))] * len(extra),
            out_specs=pl.BlockSpec(shape, lambda i: (0, 0)),
            out_shape=of(*shape),
            compiler_params=params(24),
            name="project",
            cost_estimate=cost(6 * rows * wide * len(weights) * lanes, wide * lanes * len(weights) + 2 * rows * shape[1]),
        )(*[x for u in used for x, _ in pieces[u]], *[x for x, _ in weights], *extra)

    theirs = [
        strip([(taken, 0, 4)]),
        strip([(taken_near, 0, 4)], True),
        strip([(far_4, 0, 2), (far_5, 0, 2)]),
        strip([(both_4, 0, 2), (both_5, 0, 2)], True),
    ]
    mine = [
        strip([(kept, 0, 4)]),
        strip([(kept_near, 0, 4)], True),
        strip([(far_1, 0, 1), (far_2, 0, 2), (far_3, 0, 1)]),
        strip([(both_1, 0, 1), (both_2, 0, 2), (both_3, 0, 1)], True),
    ]
    pieces = own_pieces + other_pieces(last)
    product = project(pieces, theirs + mine, [(0, 0, 3), (0, 4, 8), (1, 0, 3), (1, 4, 8)])
    product = project(pieces, theirs + mine, [(2, 0, 8)], product)
    product, last = together((product, last))
    pieces = own_pieces + other_pieces(last)
    from_them = swap(project(pieces, theirs, [(3, 0, 4), (0, 3, 4), (1, 3, 4)], product, 0), 0, 1)
    product = project(pieces, mine, [(3, 0, 4)], product, 1)

    if strip_width % 128 == 0:
        parts = pl.pallas_call(
            functools.partial(route_kernel, groups, strip_width),
            grid_spec=pltpu.PrefetchScalarGridSpec(
                num_scalar_prefetch=1,
                grid=(1,),
                in_specs=[pl.BlockSpec(x.shape, lambda i, send: (0, 0)) for x in (product, from_them)],
                out_specs=[pl.BlockSpec((rows, size * strip_width), lambda i, send: (0, 0))] * steps,
                scratch_shapes=[pltpu.VMEM((steps, rows, size * strip_width), jnp.float32)],
            ),
            out_shape=[of(rows, size * strip_width)] * steps,
            compiler_params=params(12),
            name="route",
            cost_estimate=cost(0, 6 * rows * steps * size * strip_width),
        )(send_here, product, from_them)
    else:
        parts = jnp.stack(pieces_of(product + from_them, groups, strip_width))
        parts = [lax.dynamic_index_in_dim(parts, send_here[k], 0, False) for k in range(steps)]
    arrived = [lax.ppermute(part, AXES, perm) for part, perm in zip(parts, perms)]
    if strip_width % 128 == 0:
        return pl.pallas_call(
            functools.partial(assemble_kernel, size),
            grid_spec=pltpu.PrefetchScalarGridSpec(
                num_scalar_prefetch=1,
                grid=(1,),
                in_specs=[pl.BlockSpec(x.shape, lambda i, place: (0, 0)) for x in (*arrived, residual)],
                out_specs=pl.BlockSpec(residual.shape, lambda i, place: (0, 0)),
                scratch_shapes=[pltpu.VMEM((ctx, rows, strip_width), jnp.float32)],
            ),
            out_shape=of(*residual.shape),
            compiler_params=params(12),
            name="assemble",
            cost_estimate=cost(0, 3 * residual.size),
        )(place_here, *arrived, residual)
    blocks = jnp.stack([a[:, b * strip_width : (b + 1) * strip_width] for a in arrived for b in range(size)])
    projected = [lax.dynamic_index_in_dim(blocks, place_here[p], 0, False) for p in range(ctx)]
    return residual + jnp.concatenate(projected, axis=1)


def solution(mesh):
    placed = (
        P("ctx", "head"),
        P("ctx", "head"),
        P("ctx", "head"),
        P("head", None, None),
        P("head", None, None),
        P(None, ("ctx", "head")),
        P("ctx", "head"),
    )
    return jax.shard_map(
        functools.partial(body, mesh.shape["ctx"], mesh.shape["head"]),
        mesh=mesh,
        in_specs=placed,
        out_specs=P("ctx", "head"),
        check_vma=False,
    )
```

```python
import functools

import numpy as np

import jax
import jax.numpy as jnp
from jax import lax
from jax.experimental import pallas as pl
from jax.experimental.pallas import tpu as pltpu
from jax.sharding import PartitionSpec as P

HIGH = lax.Precision.HIGHEST
together = lax.optimization_barrier
AXES = ("ctx", "head")
PAIR = 2
EXTRA = 8
MIB = 1024 * 1024


def split(x):
    high = x.astype(jnp.bfloat16)
    return high, (x - high.astype(jnp.float32)).astype(jnp.bfloat16)


def dot3(a, b, dims=(((1,), (0,)), ((), ()))):
    a_high, a_low = split(a)
    b_high, b_low = split(b)
    dot = functools.partial(lax.dot_general, dimension_numbers=dims, preferred_element_type=jnp.float32)
    return dot(a_high, b_high) + (dot(a_high, b_low) + dot(a_low, b_high))


def features(rows, weights):
    scores = jnp.dot(rows, weights, precision=HIGH, preferred_element_type=jnp.float32)
    up = jnp.exp(scores - jnp.max(scores, axis=-1, keepdims=True))
    down = jnp.exp(jnp.min(scores, axis=-1, keepdims=True) - scores)
    up = up / jnp.sum(up, axis=-1, keepdims=True)
    down = down / jnp.sum(down, axis=-1, keepdims=True)
    return jnp.concatenate([up, down], axis=-1)


def arrange_kernel(plan, wide, starts, weight_ref, *refs):
    out_refs, sems = refs[:-1], refs[-1]
    copies = []
    for out_ref, picks in zip(out_refs, plan):
        for i, pick in enumerate(picks):
            source = weight_ref.at[pl.ds(pl.multiple_of(starts[pick], wide), wide), :]
            copies.append(pltpu.make_async_copy(source, out_ref.at[pl.ds(i * wide, wide), :], sems.at[len(copies)]))
            copies[-1].start()
    for copy in copies:
        copy.wait()


def key_kernel(first, k_ref, map_ref, v_ref, state_ref, feat_ref):
    heads, head_size, feat_half = map_ref.shape
    size = 2 * feat_half
    row = lax.broadcasted_iota(jnp.int32, (EXTRA, feat_half), 0)
    for i in range(heads):
        columns = slice(i * head_size, (i + 1) * head_size)
        feat = features(k_ref[:, columns], map_ref[i])
        feat_ref[i] = feat
        state_ref[i, :size, :] = dot3(feat, v_ref[:, columns], (((0,), (0,)), ((), ())))
        norm = jnp.sum(feat, axis=0, keepdims=True)
        state_ref[i, size:, :] = jnp.where(row < EXTRA // 2, norm[:, :feat_half], norm[:, feat_half:])


def attend(feat, key_feat, values, numer_ref, denom_ref):
    weights = dot3(feat, key_feat, (((1,), (1,)), ((), ())))
    row = lax.broadcasted_iota(jnp.int32, weights.shape, 0)
    column = lax.broadcasted_iota(jnp.int32, weights.shape, 1)
    weights = jnp.where(column <= row, weights, 0.0)
    numer_ref[0] = dot3(weights, values)
    denom_ref[0] = jnp.broadcast_to(jnp.sum(weights, axis=-1, keepdims=True), denom_ref.shape[1:])


def rest_kernel(firsts, *refs):
    keys_ref, key_map_ref, queries_ref, query_map_ref, values_ref, other_feat_ref = refs[:6]
    state_ref, feat_ref, numer_ref, denom_ref, other_out_ref, other_numer_ref, other_denom_ref = refs[6:13]
    k_ref, k_map_ref, q_ref, q_map_ref, v_ref, sems = refs[13:]
    half, head_size, feat_half = k_map_ref.shape
    wide = half * head_size
    size = 2 * feat_half
    step = pl.program_id(0)

    def columns(which):
        return pl.ds(pl.multiple_of(firsts[which] * wide, wide), wide)

    def heads(which):
        return pl.ds(firsts[which] * half, half)

    copies = [
        (keys_ref.at[:, columns(0)], k_ref),
        (key_map_ref.at[heads(0)], k_map_ref),
        (values_ref.at[:, columns(0)], v_ref.at[0]),
        (queries_ref.at[:, columns(0)], q_ref.at[0]),
        (query_map_ref.at[heads(0)], q_map_ref.at[0]),
        (queries_ref.at[:, columns(1)], q_ref.at[1]),
        (query_map_ref.at[heads(1)], q_map_ref.at[1]),
        (values_ref.at[:, columns(1)], v_ref.at[1]),
    ]
    copies = [pltpu.make_async_copy(source, to, sems.at[i]) for i, (source, to) in enumerate(copies)]

    @pl.when(step == 0)
    def _():
        for copy in copies:
            copy.start()
        for copy in copies[:3]:
            copy.wait()

    here = pl.ds(pl.multiple_of(step * head_size, head_size), head_size)
    row = lax.broadcasted_iota(jnp.int32, (EXTRA, feat_half), 0)
    values = v_ref[0, :, here]
    key_feat = features(k_ref[:, here], k_map_ref[step])
    state_ref[0, :size, :] = dot3(key_feat, values, (((0,), (0,)), ((), ())))
    norm = jnp.sum(key_feat, axis=0, keepdims=True)
    state_ref[0, size:, :] = jnp.where(row < EXTRA // 2, norm[:, :feat_half], norm[:, feat_half:])

    @pl.when(step == 0)
    def _():
        for copy in copies[3:]:
            copy.wait()

    feat = features(q_ref[0, :, here], q_map_ref[0, step])
    feat_ref[0] = feat
    attend(feat, key_feat, values, numer_ref, denom_ref)
    feat = features(q_ref[1, :, here], q_map_ref[1, step])
    other_out_ref[0] = feat
    attend(feat, other_feat_ref[0], v_ref[1, :, here], other_numer_ref, other_denom_ref)


def mix_kernel(qfeat_ref, numer_ref, denom_ref, prior_ref, *refs):
    feat = qfeat_ref[0]
    size = feat.shape[1]
    norm = jnp.concatenate(
        [prior_ref[0, size : size + 1, :], prior_ref[0, size + EXTRA // 2 : size + EXTRA // 2 + 1, :]], axis=1
    )
    denom = denom_ref[0] + jnp.sum(feat * norm, axis=-1, keepdims=True)
    mixed = (numer_ref[0] + dot3(feat, prior_ref[0, :size, :])) / denom
    if len(refs) == 1:
        refs[0][...] = mixed
    else:
        below_ref, out_ref, both_ref = refs
        out_ref[...] = mixed
        both_ref[...] = jnp.concatenate([mixed, below_ref[...]], axis=0)


def project_kernel(terms, units, places, arrays, *refs):
    rows_refs, refs = refs[: 2 * units], refs[2 * units :]
    array_refs, refs = refs[:arrays], refs[arrays:]
    rest, (out_ref, w_ref, sems) = refs[:-3], refs[-3:]
    _, wide, lanes = w_ref.shape
    copies = []
    for i, (array, unit) in enumerate(places):
        source = array_refs[array].at[pl.ds(unit * wide, wide), :]
        copies.append(pltpu.make_async_copy(source, w_ref.at[i], sems.at[i]))
        copies[-1].start()
    out_ref[...] = rest[0][...] if rest else jnp.zeros_like(out_ref)
    done = 0
    for unit, start, stop in terms:
        a = jnp.concatenate([rows_refs[2 * unit][...], rows_refs[2 * unit + 1][...]], axis=0)
        mine = range(done, done + stop - start)
        for i in mine:
            copies[i].wait()
        w = jnp.concatenate([w_ref[i] for i in mine], axis=1)
        done += stop - start
        out_ref[:, start * lanes : stop * lanes] += dot3(a, w)


def pieces_of(product, groups, width):
    rows = product.shape[0] // 2
    return [
        jnp.concatenate([product[d * rows : (d + 1) * rows, b * width : (b + 1) * width] for b in group], axis=1)
        for d in range(2)
        for group in groups
    ]


def route_kernel(groups, width, send, mine_ref, other_ref, *refs):
    out_refs, pieces_ref = refs[:-1], refs[-1]
    product = mine_ref[...] + other_ref[...]
    for j, piece in enumerate(pieces_of(product, groups, width)):
        pieces_ref[j] = piece
    for k, out_ref in enumerate(out_refs):
        out_ref[...] = pieces_ref[send[k]]


def assemble_kernel(size, place, *refs):
    arrived, (residual_ref, out_ref, blocks_ref) = refs[:-3], refs[-3:]
    width = blocks_ref.shape[2]
    for k, ref in enumerate(arrived):
        for b in range(size):
            blocks_ref[k * size + b] = ref[:, b * width : (b + 1) * width]
    for p in range(blocks_ref.shape[0]):
        columns = slice(p * width, (p + 1) * width)
        out_ref[:, columns] = residual_ref[:, columns] + blocks_ref[place[p]]


def route_tables(ctx, heads, rels):
    groups = {}
    for column, rel in enumerate(rels):
        groups.setdefault(rel * heads // ctx, []).append(column)
    groups = [groups[key] for key in sorted(groups)]
    size = len(groups[0])
    targets = {}
    for c in range(ctx):
        for h in range(heads):
            found = {}
            for d, step in enumerate((0, PAIR)):
                for g, columns in enumerate(groups):
                    to = (c ^ step) * heads + (c ^ rels[columns[0]]) * heads // ctx
                    found[to] = d * len(groups) + g
            targets[c * heads + h] = found
    classes = {}
    for device in sorted(targets):
        classes.setdefault(tuple(sorted(targets[device])), []).append(device)
    steps = 2 * len(groups)
    perms = [[] for _ in range(steps)]
    send = np.zeros((ctx * heads, steps), np.int32)
    arrives = {}
    for ends, sources in classes.items():
        for i, source in enumerate(sources):
            for k in range(steps):
                to = ends[i ^ k]
                perms[k].append((source, to))
                send[source, k] = targets[source][to]
                arrives[to, source] = k
    place = np.zeros((ctx * heads, ctx), np.int32)
    for c in range(ctx):
        for h in range(heads):
            for p in range(ctx):
                column_ctx, source_h = divmod(h * ctx + p, heads)
                source_c = (c & ~PAIR) | (column_ctx & PAIR)
                k = arrives[c * heads + h, source_c * heads + source_h]
                rel = source_c ^ column_ctx
                group = [g for g in groups if rels.index(rel) in g][0]
                place[c * heads + h, p] = k * size + group.index(rels.index(rel))
    return groups, perms, send, place


def body(ctx, heads, queries, keys, values, query_map, key_map, out_weight, residual):
    rows = queries.shape[0]
    heads_here, head_size, feat_half = query_map.shape
    feat_size = 2 * feat_half
    half = heads_here // 2
    wide = half * head_size
    depth = out_weight.shape[0] // heads
    strip_width = out_weight.shape[1]
    c = lax.axis_index("ctx")
    h = lax.axis_index("head")
    me = c * heads + h
    odd = c & 1

    def swap(x, by_ctx, by_head=0, keep=lambda c: True):
        pairs = [
            (i * heads + j, (i ^ by_ctx) * heads + (j ^ by_head))
            for i in range(ctx)
            for j in range(heads)
            if keep(i)
        ]
        return lax.ppermute(x, AXES, pairs)

    def of(*shape):
        return jax.ShapeDtypeStruct(shape, jnp.float32)

    def cost(products, count, exps=0):
        return pl.CostEstimate(flops=2 * products, bytes_accessed=4 * count, transcendentals=exps)

    def params(mib):
        return pltpu.CompilerParams(vmem_limit_bytes=mib * MIB)

    in_hbm = pl.BlockSpec(memory_space=pltpu.MemorySpace.HBM)

    def head_block(size, lanes):
        return pl.BlockSpec((1, size, lanes), lambda i, *_: (i, 0, 0))

    def key_part(first):
        columns = pl.BlockSpec((rows, wide), lambda i, first: (0, first[0]))
        maps = pl.BlockSpec((half, head_size, feat_half), lambda i, first: (first[0], 0, 0))
        shapes = [of(half, feat_size + EXTRA, head_size), of(half, rows, feat_size)]
        return pl.pallas_call(
            key_kernel,
            grid_spec=pltpu.PrefetchScalarGridSpec(
                num_scalar_prefetch=1,
                grid=(1,),
                in_specs=[columns, maps, columns],
                out_specs=[pl.BlockSpec(s.shape, lambda i, first: (0, 0, 0)) for s in shapes],
            ),
            out_shape=shapes,
            compiler_params=params(60),
            name="key_part",
            cost_estimate=cost(
                6 * half * rows * head_size * (feat_half + feat_size),
                half * rows * (2 * head_size + 2 * feat_size),
                half * rows * feat_size,
            ),
        )(first, keys, key_map, values)

    def rest_part(firsts, other_feat):
        query_shapes = [of(half, rows, feat_size), of(half, rows, head_size), of(half, rows, head_size)]
        shapes = [of(half, feat_size + EXTRA, head_size), *query_shapes, *query_shapes]
        outs = pl.pallas_call(
            rest_kernel,
            grid_spec=pltpu.PrefetchScalarGridSpec(
                num_scalar_prefetch=1,
                grid=(half,),
                in_specs=[in_hbm] * 5 + [head_block(rows, feat_size)],
                out_specs=[head_block(*shape.shape[1:]) for shape in shapes],
                scratch_shapes=[
                    pltpu.VMEM((rows, wide), jnp.float32),
                    pltpu.VMEM((half, head_size, feat_half), jnp.float32),
                    pltpu.VMEM((2, rows, wide), jnp.float32),
                    pltpu.VMEM((2, half, head_size, feat_half), jnp.float32),
                    pltpu.VMEM((2, rows, wide), jnp.float32),
                    pltpu.SemaphoreType.DMA((8,)),
                ],
            ),
            out_shape=shapes,
            compiler_params=params(24),
            name="rest_part",
            cost_estimate=cost(
                6 * half * rows * (head_size * (3 * feat_half + feat_size) + 2 * rows * (feat_size + head_size)),
                half * rows * (8 * head_size + 4 * feat_size),
                3 * half * rows * feat_size,
            ),
        )(firsts, keys, key_map, queries, query_map, values, other_feat)
        return outs[0], outs[1:4], outs[4:]

    def mix(qfeat, numer, denom, prior, below=None):
        columns = pl.BlockSpec((rows, head_size), lambda i: (0, i))
        out_specs, shapes = columns, of(rows, wide)
        if below is not None:
            out_specs = [columns, pl.BlockSpec((2 * rows, head_size), lambda i: (0, i))]
            shapes = [shapes, of(2 * rows, wide)]
        return pl.pallas_call(
            mix_kernel,
            grid=(half,),
            in_specs=[
                head_block(rows, feat_size),
                head_block(rows, head_size),
                head_block(rows, head_size),
                head_block(feat_size + EXTRA, head_size),
            ]
            + [columns] * (below is not None),
            out_specs=out_specs,
            out_shape=shapes,
            compiler_params=params(12),
            name="mix",
            cost_estimate=cost(
                3 * half * rows * feat_size * head_size, half * rows * (3 * head_size + 2 * feat_size)
            ),
        )(qfeat, numer, denom, prior, *([] if below is None else [below]))

    even = range(0, heads, 2)
    blocks = heads // 2
    bits = [1 << b for b in reversed(range(ctx.bit_length() - 1)) if 1 << b != PAIR]
    far, near = bits[-2:]
    rels = [0]
    for bit in bits[:-2]:
        rels = rels + [r | bit for r in rels]
    rels = [r | s for s in (0, near, far, far | near) for r in rels]

    def arranged(weight, starts, plan):
        shapes = [of(len(picks) * wide, strip_width) for picks in plan]
        count = sum(len(picks) for picks in plan)
        return pl.pallas_call(
            functools.partial(arrange_kernel, plan, wide),
            grid_spec=pltpu.PrefetchScalarGridSpec(
                num_scalar_prefetch=1,
                grid=(1,),
                in_specs=[pl.BlockSpec(memory_space=pl.ANY)],
                out_specs=[pl.BlockSpec(memory_space=pl.ANY)] * len(plan),
                scratch_shapes=[pltpu.SemaphoreType.DMA((count,))],
            ),
            out_shape=shapes,
            compiler_params=params(12),
            name="arrange",
            cost_estimate=cost(0, 2 * count * wide * strip_width),
        )(starts, weight)

    def widen(x):
        for bit in bits[:-2]:
            x = jnp.concatenate([x, swap(x, bit)], axis=1)
        return x

    order = [(which, d) for which in (odd, 1 - odd) for d in even]
    part = len(order) // 4
    own, other = odd.reshape(1), (1 - odd).reshape(1)
    other_state, other_feat = key_part(other)
    out_weight, other_state = together((out_weight, other_state))
    starts = jnp.stack([(h ^ flip ^ d) * depth + which * wide for flip in (0, 1) for which, d in order])
    count = len(order)
    (first_part,) = arranged(out_weight, starts, [list(range(part))])
    first_part = widen(first_part)
    far_1 = swap(first_part, far)
    from_neighbour = swap(other_state, 1)
    own_state, own_query, other_query = rest_part(jnp.concatenate([own, other]), other_feat)
    out_weight, own_state = together((out_weight, own_state))
    spans = [(part, 3 * part), (3 * part, count), (0, count)]
    spans += [(count, count + 2 * part), (count + 2 * part, 2 * count), (count, 2 * count)]
    kept_2, kept_3, kept, given_1, given_2, given = arranged(out_weight, starts, [list(range(*span)) for span in spans])
    kept_2, kept_3, kept = [widen(x) for x in (kept_2, kept_3, kept)]
    groups, perms, send, place = route_tables(ctx, heads, rels)
    steps, size = len(perms), len(groups[0])
    send_here = jnp.asarray(send)[me]
    place_here = jnp.asarray(place)[me]

    from_neighbour, own_state, far_1, kept_2, kept, given_1, given_2, given = together(
        (from_neighbour, own_state, far_1, kept_2, kept, given_1, given_2, given)
    )
    far_2 = swap(kept_2, far)
    kept_near = swap(kept, near)
    taken, taken_1, taken_2 = [widen(swap(x, 0, 1)) for x in (given, given_1, given_2)]
    earlier = jnp.where(odd == 0, own_state, from_neighbour)
    total = own_state + from_neighbour
    before = jnp.zeros_like(total)
    bit = 2
    while 2 * bit < ctx:
        got = swap(total, bit)
        before = before + jnp.where((c & bit) != 0, got, 0.0)
        total = total + got
        bit *= 2
    total, before, far_2, kept_near, taken, taken_1, taken_2, far_1 = together(
        (total, before, far_2, kept_near, taken, taken_1, taken_2, far_1)
    )
    taken_near = swap(taken, near)
    both_1 = swap(far_1, near)
    second = (c & PAIR) != 0
    got = swap(jnp.where(second, total[half // 2 :], total[: half // 2]), bit, keep=lambda i: not i & bit)
    got, kept_3 = together((got, kept_3))
    met = swap(got, PAIR, keep=lambda i: i & bit)
    far_3 = swap(kept_3, far)
    got = jnp.concatenate([jnp.where(second, met, got), jnp.where(second, got, met)])
    got, taken_near, both_1, taken_1, far_2 = together((got, taken_near, both_1, taken_1, far_2))
    before = before + got

    other_prior = swap(before + jnp.where(odd == 0, earlier, 0.0), 1)
    own_mixed = mix(*own_query, before + jnp.where(odd == 1, earlier, 0.0))
    head_bits = [1 << b for b in range(1, heads.bit_length() - 1)]

    def spread(pieces):
        for bit in head_bits[1:]:
            for (d, j), (x, i) in list(pieces.items()):
                pieces[d, j | bit] = (swap(x[i * rows : (i + 1) * rows], 0, bit), 0)
        return [(pieces[0, j], pieces[PAIR, j]) for j in even]

    own_mixed, far_3 = together((own_mixed, far_3))
    met, across = swap(own_mixed, PAIR), swap(own_mixed, 0, head_bits[0])
    far_4 = swap(taken_1, far)
    both_2 = swap(far_2, near)
    other_mixed, both = mix(*other_query, other_prior, met)
    other_mixed, both, across, far_3, far_4, both_2, taken_2 = together(
        (other_mixed, both, across, far_3, far_4, both_2, taken_2)
    )
    other_met = swap(other_mixed, PAIR)
    both = swap(both, 0, head_bits[0])
    far_5 = swap(taken_2, far)
    both_3 = swap(far_3, near)
    both_4 = swap(far_4, near)
    other_met, both, far_5, both_3, both_4, send_here, place_here = together(
        (other_met, both, far_5, both_3, both_4, send_here, place_here)
    )
    both_5 = swap(far_5, near)
    last = swap(other_met, 0, head_bits[0])
    own_pieces = spread(
        {(0, 0): (own_mixed, 0), (PAIR, 0): (met, 0), (0, head_bits[0]): (across, 0), (PAIR, head_bits[0]): (both, 1)}
    )

    def other_pieces(last):
        pieces = {(0, 0): (other_mixed, 0), (PAIR, 0): (other_met, 0), (0, head_bits[0]): (both, 0)}
        return spread({**pieces, (PAIR, head_bits[0]): (last, 0)})

    lanes = kept.shape[1]

    def strip(parts, crossed=False):
        places = [(x, start * part + i) for x, start, stop in parts for i in range((stop - start) * part)]
        return places[blocks:] + places[:blocks] if crossed else places

    def project(pieces, strips, runs, total=None, column=0):
        runs = [(u, start, stop) for q, start, stop in runs for u in range(q * part, (q + 1) * part)]
        used = sorted({u for u, _, _ in runs})
        weights = [strips[s][u] for u, start, stop in runs for s in range(start, stop)]
        arrays = list({id(x): x for x, _ in weights}.values())
        places = [([id(x) for x in arrays].index(id(x)), unit) for x, unit in weights]
        shape = (2 * rows, len(strips) * lanes)
        extra = [] if total is None else [total]
        terms = [(used.index(u), start, stop) for u, start, stop in runs]
        return pl.pallas_call(
            functools.partial(project_kernel, terms, len(used), places, len(arrays)),
            grid=(1,),
            in_specs=[pl.BlockSpec((rows, wide), lambda i, block=block: (block, 0)) for u in used for _, block in pieces[u]]
            + [in_hbm] * len(arrays)
            + [pl.BlockSpec(shape, lambda i: (0, column))] * len(extra),
            out_specs=pl.BlockSpec(shape, lambda i: (0, 0)),
            out_shape=of(*shape),
            scratch_shapes=[
                pltpu.VMEM((len(places), wide, lanes), jnp.float32),
                pltpu.SemaphoreType.DMA((len(places),)),
            ],
            compiler_params=params(24),
            name="project",
            cost_estimate=cost(6 * rows * wide * len(weights) * lanes, wide * lanes * len(weights) + 2 * rows * shape[1]),
        )(*[x for u in used for x, _ in pieces[u]], *arrays, *extra)

    theirs = [
        strip([(taken, 0, 4)]),
        strip([(taken_near, 0, 4)], True),
        strip([(far_4, 0, 2), (far_5, 0, 2)]),
        strip([(both_4, 0, 2), (both_5, 0, 2)], True),
    ]
    mine = [
        strip([(kept, 0, 4)]),
        strip([(kept_near, 0, 4)], True),
        strip([(far_1, 0, 1), (far_2, 0, 2), (far_3, 0, 1)]),
        strip([(both_1, 0, 1), (both_2, 0, 2), (both_3, 0, 1)], True),
    ]
    pieces = own_pieces + other_pieces(last)
    product = project(pieces, theirs + mine, [(0, 0, 3), (0, 4, 8), (1, 0, 3), (1, 4, 8)])
    product = project(pieces, theirs + mine, [(2, 0, 8)], product)
    product, last = together((product, last))
    pieces = own_pieces + other_pieces(last)
    from_them = swap(project(pieces, theirs, [(3, 0, 4), (0, 3, 4), (1, 3, 4)], product, 0), 0, 1)
    product = project(pieces, mine, [(3, 0, 4)], product, 1)

    if strip_width % 128 == 0:
        parts = pl.pallas_call(
            functools.partial(route_kernel, groups, strip_width),
            grid_spec=pltpu.PrefetchScalarGridSpec(
                num_scalar_prefetch=1,
                grid=(1,),
                in_specs=[pl.BlockSpec(x.shape, lambda i, send: (0, 0)) for x in (product, from_them)],
                out_specs=[pl.BlockSpec((rows, size * strip_width), lambda i, send: (0, 0))] * steps,
                scratch_shapes=[pltpu.VMEM((steps, rows, size * strip_width), jnp.float32)],
            ),
            out_shape=[of(rows, size * strip_width)] * steps,
            compiler_params=params(12),
            name="route",
            cost_estimate=cost(0, 6 * rows * steps * size * strip_width),
        )(send_here, product, from_them)
    else:
        parts = jnp.stack(pieces_of(product + from_them, groups, strip_width))
        parts = [lax.dynamic_index_in_dim(parts, send_here[k], 0, False) for k in range(steps)]
    arrived = [lax.ppermute(part, AXES, perm) for part, perm in zip(parts, perms)]
    if strip_width % 128 == 0:
        return pl.pallas_call(
            functools.partial(assemble_kernel, size),
            grid_spec=pltpu.PrefetchScalarGridSpec(
                num_scalar_prefetch=1,
                grid=(1,),
                in_specs=[pl.BlockSpec(x.shape, lambda i, place: (0, 0)) for x in (*arrived, residual)],
                out_specs=pl.BlockSpec(residual.shape, lambda i, place: (0, 0)),
                scratch_shapes=[pltpu.VMEM((ctx, rows, strip_width), jnp.float32)],
            ),
            out_shape=of(*residual.shape),
            compiler_params=params(12),
            name="assemble",
            cost_estimate=cost(0, 3 * residual.size),
        )(place_here, *arrived, residual)
    blocks = jnp.stack([a[:, b * strip_width : (b + 1) * strip_width] for a in arrived for b in range(size)])
    projected = [lax.dynamic_index_in_dim(blocks, place_here[p], 0, False) for p in range(ctx)]
    return residual + jnp.concatenate(projected, axis=1)


def solution(mesh):
    placed = (
        P("ctx", "head"),
        P("ctx", "head"),
        P("ctx", "head"),
        P("head", None, None),
        P("head", None, None),
        P(None, ("ctx", "head")),
        P("ctx", "head"),
    )
    return jax.shard_map(
        functools.partial(body, mesh.shape["ctx"], mesh.shape["head"]),
        mesh=mesh,
        in_specs=placed,
        out_specs=P("ctx", "head"),
        check_vma=False,
    )
```

```python
import functools

import numpy as np

import jax
import jax.numpy as jnp
from jax import lax
from jax.experimental import pallas as pl
from jax.experimental.pallas import tpu as pltpu
from jax.sharding import PartitionSpec as P

HIGH = lax.Precision.HIGHEST
together = lax.optimization_barrier
AXES = ("ctx", "head")
PAIR = 2
EXTRA = 8
MIB = 1024 * 1024


def split(x):
    high = x.astype(jnp.bfloat16)
    return high, (x - high.astype(jnp.float32)).astype(jnp.bfloat16)


def dot3(a, b, dims=(((1,), (0,)), ((), ()))):
    a_high, a_low = split(a)
    b_high, b_low = split(b)
    dot = functools.partial(lax.dot_general, dimension_numbers=dims, preferred_element_type=jnp.float32)
    return dot(a_high, b_high) + (dot(a_high, b_low) + dot(a_low, b_high))


def features(rows, weights):
    scores = jnp.dot(rows, weights, precision=HIGH, preferred_element_type=jnp.float32)
    up = jnp.exp(scores - jnp.max(scores, axis=-1, keepdims=True))
    down = jnp.exp(jnp.min(scores, axis=-1, keepdims=True) - scores)
    up = up / jnp.sum(up, axis=-1, keepdims=True)
    down = down / jnp.sum(down, axis=-1, keepdims=True)
    return jnp.concatenate([up, down], axis=-1)


def arrange_kernel(plan, wide, starts, weight_ref, *refs):
    out_refs, sems = refs[:-1], refs[-1]
    copies = []
    for out_ref, picks in zip(out_refs, plan):
        for i, pick in enumerate(picks):
            source = weight_ref.at[pl.ds(pl.multiple_of(starts[pick], wide), wide), :]
            copies.append(pltpu.make_async_copy(source, out_ref.at[pl.ds(i * wide, wide), :], sems.at[len(copies)]))
            copies[-1].start()
    for copy in copies:
        copy.wait()


def key_kernel(first, k_ref, map_ref, v_ref, state_ref, feat_ref):
    heads, head_size, feat_half = map_ref.shape
    size = 2 * feat_half
    row = lax.broadcasted_iota(jnp.int32, (EXTRA, feat_half), 0)
    for i in range(heads):
        columns = slice(i * head_size, (i + 1) * head_size)
        feat = features(k_ref[:, columns], map_ref[i])
        feat_ref[i] = feat
        state_ref[i, :size, :] = dot3(feat, v_ref[:, columns], (((0,), (0,)), ((), ())))
        norm = jnp.sum(feat, axis=0, keepdims=True)
        state_ref[i, size:, :] = jnp.where(row < EXTRA // 2, norm[:, :feat_half], norm[:, feat_half:])


def attend(feat, key_feat, values, numer_ref, denom_ref):
    weights = dot3(feat, key_feat, (((1,), (1,)), ((), ())))
    row = lax.broadcasted_iota(jnp.int32, weights.shape, 0)
    column = lax.broadcasted_iota(jnp.int32, weights.shape, 1)
    weights = jnp.where(column <= row, weights, 0.0)
    numer_ref[0] = dot3(weights, values)
    denom_ref[0] = jnp.broadcast_to(jnp.sum(weights, axis=-1, keepdims=True), denom_ref.shape[1:])


def rest_kernel(first, *refs):
    k_ref, k_map_ref, q_ref, q_map_ref, v_ref, other_q_ref, other_q_map_ref, other_v_ref, other_feat_ref = refs[:9]
    state_ref, feat_ref, numer_ref, denom_ref, other_out_ref, other_numer_ref, other_denom_ref = refs[9:]
    heads, head_size, feat_half = k_map_ref.shape
    size = 2 * feat_half
    row = lax.broadcasted_iota(jnp.int32, (EXTRA, feat_half), 0)
    key_feat = features(k_ref[...], k_map_ref[0])
    state_ref[0, :size, :] = dot3(key_feat, v_ref[...], (((0,), (0,)), ((), ())))
    norm = jnp.sum(key_feat, axis=0, keepdims=True)
    state_ref[0, size:, :] = jnp.where(row < EXTRA // 2, norm[:, :feat_half], norm[:, feat_half:])
    feat = features(q_ref[...], q_map_ref[0])
    feat_ref[0] = feat
    attend(feat, key_feat, v_ref[...], numer_ref, denom_ref)
    feat = features(other_q_ref[...], other_q_map_ref[0])
    other_out_ref[0] = feat
    attend(feat, other_feat_ref[0], other_v_ref[...], other_numer_ref, other_denom_ref)


def mix_kernel(qfeat_ref, numer_ref, denom_ref, prior_ref, *refs):
    feat = qfeat_ref[0]
    size = feat.shape[1]
    norm = jnp.concatenate(
        [prior_ref[0, size : size + 1, :], prior_ref[0, size + EXTRA // 2 : size + EXTRA // 2 + 1, :]], axis=1
    )
    denom = denom_ref[0] + jnp.sum(feat * norm, axis=-1, keepdims=True)
    mixed = (numer_ref[0] + dot3(feat, prior_ref[0, :size, :])) / denom
    if len(refs) == 1:
        refs[0][...] = mixed
    else:
        below_ref, out_ref, both_ref = refs
        out_ref[...] = mixed
        both_ref[...] = jnp.concatenate([mixed, below_ref[...]], axis=0)


def project_kernel(terms, units, *refs):
    rows_refs, refs = refs[: 2 * units], refs[2 * units :]
    count = sum(stop - start for _, start, stop in terms)
    w_refs, rest, out_ref = refs[:count], refs[count:-1], refs[-1]
    out_ref[...] = rest[0][...] if rest else jnp.zeros_like(out_ref)
    lanes = w_refs[0].shape[1]
    for unit, start, stop in terms:
        a = jnp.concatenate([rows_refs[2 * unit][...], rows_refs[2 * unit + 1][...]], axis=0)
        w = jnp.concatenate([ref[...] for ref in w_refs[: stop - start]], axis=1)
        w_refs = w_refs[stop - start :]
        out_ref[:, start * lanes : stop * lanes] += dot3(a, w)


def pieces_of(product, groups, width):
    rows = product.shape[0] // 2
    return [
        jnp.concatenate([product[d * rows : (d + 1) * rows, b * width : (b + 1) * width] for b in group], axis=1)
        for d in range(2)
        for group in groups
    ]


def route_kernel(groups, width, send, mine_ref, other_ref, *refs):
    out_refs, pieces_ref = refs[:-1], refs[-1]
    product = mine_ref[...] + other_ref[...]
    for j, piece in enumerate(pieces_of(product, groups, width)):
        pieces_ref[j] = piece
    for k, out_ref in enumerate(out_refs):
        out_ref[...] = pieces_ref[send[k]]


def assemble_kernel(size, place, *refs):
    arrived, (residual_ref, out_ref, blocks_ref) = refs[:-3], refs[-3:]
    width = blocks_ref.shape[2]
    for k, ref in enumerate(arrived):
        for b in range(size):
            blocks_ref[k * size + b] = ref[:, b * width : (b + 1) * width]
    for p in range(blocks_ref.shape[0]):
        columns = slice(p * width, (p + 1) * width)
        out_ref[:, columns] = residual_ref[:, columns] + blocks_ref[place[p]]


def route_tables(ctx, heads, rels):
    groups = {}
    for column, rel in enumerate(rels):
        groups.setdefault(rel * heads // ctx, []).append(column)
    groups = [groups[key] for key in sorted(groups)]
    size = len(groups[0])
    targets = {}
    for c in range(ctx):
        for h in range(heads):
            found = {}
            for d, step in enumerate((0, PAIR)):
                for g, columns in enumerate(groups):
                    to = (c ^ step) * heads + (c ^ rels[columns[0]]) * heads // ctx
                    found[to] = d * len(groups) + g
            targets[c * heads + h] = found
    classes = {}
    for device in sorted(targets):
        classes.setdefault(tuple(sorted(targets[device])), []).append(device)
    steps = 2 * len(groups)
    perms = [[] for _ in range(steps)]
    send = np.zeros((ctx * heads, steps), np.int32)
    arrives = {}
    for ends, sources in classes.items():
        for i, source in enumerate(sources):
            for k in range(steps):
                to = ends[i ^ k]
                perms[k].append((source, to))
                send[source, k] = targets[source][to]
                arrives[to, source] = k
    place = np.zeros((ctx * heads, ctx), np.int32)
    for c in range(ctx):
        for h in range(heads):
            for p in range(ctx):
                column_ctx, source_h = divmod(h * ctx + p, heads)
                source_c = (c & ~PAIR) | (column_ctx & PAIR)
                k = arrives[c * heads + h, source_c * heads + source_h]
                rel = source_c ^ column_ctx
                group = [g for g in groups if rels.index(rel) in g][0]
                place[c * heads + h, p] = k * size + group.index(rels.index(rel))
    return groups, perms, send, place


def body(ctx, heads, queries, keys, values, query_map, key_map, out_weight, residual):
    rows = queries.shape[0]
    heads_here, head_size, feat_half = query_map.shape
    feat_size = 2 * feat_half
    half = heads_here // 2
    wide = half * head_size
    depth = out_weight.shape[0] // heads
    strip_width = out_weight.shape[1]
    c = lax.axis_index("ctx")
    h = lax.axis_index("head")
    odd = c & 1

    def swap(x, by_ctx, by_head=0, keep=lambda c: True):
        pairs = [
            (i * heads + j, (i ^ by_ctx) * heads + (j ^ by_head))
            for i in range(ctx)
            for j in range(heads)
            if keep(i)
        ]
        return lax.ppermute(x, AXES, pairs)

    def of(*shape):
        return jax.ShapeDtypeStruct(shape, jnp.float32)

    def cost(products, count, exps=0):
        return pl.CostEstimate(flops=2 * products, bytes_accessed=4 * count, transcendentals=exps)

    def params(mib):
        return pltpu.CompilerParams(vmem_limit_bytes=mib * MIB)

    def head_block(size, lanes):
        return pl.BlockSpec((1, size, lanes), lambda i, *_: (i, 0, 0))

    def key_part(first):
        columns = pl.BlockSpec((rows, wide), lambda i, first: (0, first[0]))
        maps = pl.BlockSpec((half, head_size, feat_half), lambda i, first: (first[0], 0, 0))
        shapes = [of(half, feat_size + EXTRA, head_size), of(half, rows, feat_size)]
        return pl.pallas_call(
            key_kernel,
            grid_spec=pltpu.PrefetchScalarGridSpec(
                num_scalar_prefetch=1,
                grid=(1,),
                in_specs=[columns, maps, columns],
                out_specs=[pl.BlockSpec(s.shape, lambda i, first: (0, 0, 0)) for s in shapes],
            ),
            out_shape=shapes,
            compiler_params=params(60),
            name="key_part",
            cost_estimate=cost(
                6 * half * rows * head_size * (feat_half + feat_size),
                half * rows * (2 * head_size + 2 * feat_size),
                half * rows * feat_size,
            ),
        )(first, keys, key_map, values)

    def rest_part(firsts, other_feat):
        def columns(which):
            return pl.BlockSpec((rows, head_size), lambda i, first: (0, first[which] * half + i))

        def maps(which):
            return pl.BlockSpec((1, head_size, feat_half), lambda i, first: (first[which] * half + i, 0, 0))

        query_shapes = [of(half, rows, feat_size), of(half, rows, head_size), of(half, rows, head_size)]
        shapes = [of(half, feat_size + EXTRA, head_size), *query_shapes, *query_shapes]
        outs = pl.pallas_call(
            rest_kernel,
            grid_spec=pltpu.PrefetchScalarGridSpec(
                num_scalar_prefetch=1,
                grid=(half,),
                in_specs=[columns(0), maps(0), columns(0), maps(0), columns(0)]
                + [columns(1), maps(1), columns(1), head_block(rows, feat_size)],
                out_specs=[head_block(*shape.shape[1:]) for shape in shapes],
            ),
            out_shape=shapes,
            compiler_params=params(48),
            name="rest_part",
            cost_estimate=cost(
                6 * half * rows * (head_size * (3 * feat_half + feat_size) + 2 * rows * (feat_size + head_size)),
                half * rows * (8 * head_size + 4 * feat_size),
                3 * half * rows * feat_size,
            ),
        )(firsts, keys, key_map, queries, query_map, values, queries, query_map, values, other_feat)
        return outs[0], outs[1:4], outs[4:]

    def mix(qfeat, numer, denom, prior, below=None):
        columns = pl.BlockSpec((rows, head_size), lambda i: (0, i))
        out_specs, shapes = columns, of(rows, wide)
        if below is not None:
            out_specs = [columns, pl.BlockSpec((2 * rows, head_size), lambda i: (0, i))]
            shapes = [shapes, of(2 * rows, wide)]
        return pl.pallas_call(
            mix_kernel,
            grid=(half,),
            in_specs=[
                head_block(rows, feat_size),
                head_block(rows, head_size),
                head_block(rows, head_size),
                head_block(feat_size + EXTRA, head_size),
            ]
            + [columns] * (below is not None),
            out_specs=out_specs,
            out_shape=shapes,
            compiler_params=params(12),
            name="mix",
            cost_estimate=cost(
                3 * half * rows * feat_size * head_size, half * rows * (3 * head_size + 2 * feat_size)
            ),
        )(qfeat, numer, denom, prior, *([] if below is None else [below]))

    even = range(0, heads, 2)
    blocks = heads // 2
    bits = [1 << b for b in reversed(range(ctx.bit_length() - 1)) if 1 << b != PAIR]
    far, near = bits[-2:]
    rels = [0]
    for bit in bits[:-2]:
        rels = rels + [r | bit for r in rels]
    rels = [r | s for s in (0, near, far, far | near) for r in rels]

    def arranged(weight, starts, plan):
        shapes = [of(len(picks) * wide, strip_width) for picks in plan]
        count = sum(len(picks) for picks in plan)
        return pl.pallas_call(
            functools.partial(arrange_kernel, plan, wide),
            grid_spec=pltpu.PrefetchScalarGridSpec(
                num_scalar_prefetch=1,
                grid=(1,),
                in_specs=[pl.BlockSpec(memory_space=pl.ANY)],
                out_specs=[pl.BlockSpec(memory_space=pl.ANY)] * len(plan),
                scratch_shapes=[pltpu.SemaphoreType.DMA((count,))],
            ),
            out_shape=shapes,
            compiler_params=params(12),
            name="arrange",
            cost_estimate=cost(0, 2 * count * wide * strip_width),
        )(starts, weight)

    def widen(x):
        for bit in bits[:-2]:
            x = jnp.concatenate([x, swap(x, bit)], axis=1)
        return x

    order = [(which, d) for which in (0, 1) for d in even]
    part = len(order) // 4
    firsts = odd ^ np.array([0, 1], np.int32)
    other = odd ^ np.array([1], np.int32)
    other_state, other_feat = key_part(other)
    out_weight, other_state = together((out_weight, other_state))
    count = len(order)
    head_masks = np.array([flip ^ d for flip in (0, 1) for _, d in order], np.int32)
    half_masks = np.array([which for _ in (0, 1) for which, _ in order], np.int32)
    starts = (h ^ head_masks) * depth + (odd ^ half_masks) * wide
    (first_part,) = arranged(out_weight, starts, [list(range(part))])
    first_part = widen(first_part)
    far_1 = swap(first_part, far)
    from_neighbour = swap(other_state, 1)
    own_state, own_query, other_query = rest_part(firsts, other_feat)
    out_weight, own_state = together((out_weight, own_state))
    spans = [(part, 3 * part), (3 * part, count), (0, count)]
    spans += [(count, count + 2 * part), (count + 2 * part, 2 * count), (count, 2 * count)]
    kept_2, kept_3, kept, given_1, given_2, given = arranged(out_weight, starts, [list(range(*span)) for span in spans])
    kept_2, kept_3, kept = [widen(x) for x in (kept_2, kept_3, kept)]
    groups, perms, send, place = route_tables(ctx, heads, rels)
    steps, size = len(perms), len(groups[0])
    send_here, place_here = [
        lax.dynamic_slice(
            x.reshape(ctx, heads, -1), (c, h, 0), (1, 1, x.shape[1]), allow_negative_indices=False
        ).reshape(-1)
        for x in (send, place)
    ]

    from_neighbour, own_state, far_1, kept_2, kept, given_1, given_2, given = together(
        (from_neighbour, own_state, far_1, kept_2, kept, given_1, given_2, given)
    )
    far_2 = swap(kept_2, far)
    kept_near = swap(kept, near)
    taken, taken_1, taken_2 = [widen(swap(x, 0, 1)) for x in (given, given_1, given_2)]
    earlier = jnp.where(odd == 0, own_state, from_neighbour)
    total = own_state + from_neighbour
    before = jnp.zeros_like(total)
    bit = 2
    while 2 * bit < ctx:
        got = swap(total, bit)
        before = before + jnp.where((c & bit) != 0, got, 0.0)
        total = total + got
        bit *= 2
    total, before, far_2, kept_near, taken, taken_1, taken_2, far_1 = together(
        (total, before, far_2, kept_near, taken, taken_1, taken_2, far_1)
    )
    taken_near = swap(taken, near)
    both_1 = swap(far_1, near)
    second = (c & PAIR) != 0
    got = swap(jnp.where(second, total[half // 2 :], total[: half // 2]), bit, keep=lambda i: not i & bit)
    got, kept_3 = together((got, kept_3))
    met = swap(got, PAIR, keep=lambda i: i & bit)
    far_3 = swap(kept_3, far)
    got = jnp.concatenate([jnp.where(second, met, got), jnp.where(second, got, met)])
    got, taken_near, both_1, taken_1, far_2 = together((got, taken_near, both_1, taken_1, far_2))
    before = before + got

    other_prior = swap(before + jnp.where(odd == 0, earlier, 0.0), 1)
    own_mixed = mix(*own_query, before + jnp.where(odd == 1, earlier, 0.0))
    head_bits = [1 << b for b in range(1, heads.bit_length() - 1)]

    def spread(pieces):
        for bit in head_bits[1:]:
            for (d, j), (x, i) in list(pieces.items()):
                pieces[d, j | bit] = (swap(x[i * rows : (i + 1) * rows], 0, bit), 0)
        return [(pieces[0, j], pieces[PAIR, j]) for j in even]

    own_mixed, far_3 = together((own_mixed, far_3))
    met, across = swap(own_mixed, PAIR), swap(own_mixed, 0, head_bits[0])
    far_4 = swap(taken_1, far)
    both_2 = swap(far_2, near)
    other_mixed, both = mix(*other_query, other_prior, met)
    other_mixed, both, across, far_3, far_4, both_2, taken_2 = together(
        (other_mixed, both, across, far_3, far_4, both_2, taken_2)
    )
    other_met = swap(other_mixed, PAIR)
    both = swap(both, 0, head_bits[0])
    far_5 = swap(taken_2, far)
    both_3 = swap(far_3, near)
    both_4 = swap(far_4, near)
    other_met, both, far_5, both_3, both_4, send_here, place_here = together(
        (other_met, both, far_5, both_3, both_4, send_here, place_here)
    )
    both_5 = swap(far_5, near)
    last = swap(other_met, 0, head_bits[0])
    own_pieces = spread(
        {(0, 0): (own_mixed, 0), (PAIR, 0): (met, 0), (0, head_bits[0]): (across, 0), (PAIR, head_bits[0]): (both, 1)}
    )

    def other_pieces(last):
        pieces = {(0, 0): (other_mixed, 0), (PAIR, 0): (other_met, 0), (0, head_bits[0]): (both, 0)}
        return spread({**pieces, (PAIR, head_bits[0]): (last, 0)})

    lanes = kept.shape[1]

    def strip(parts, crossed=False):
        places = [(x, start * part + i) for x, start, stop in parts for i in range((stop - start) * part)]
        return places[blocks:] + places[:blocks] if crossed else places

    def project(pieces, strips, runs, total=None, column=0):
        runs = [(u, start, stop) for q, start, stop in runs for u in range(q * part, (q + 1) * part)]
        used = sorted({u for u, _, _ in runs})
        weights = [strips[s][u] for u, start, stop in runs for s in range(start, stop)]
        shape = (2 * rows, len(strips) * lanes)
        extra = [] if total is None else [total]
        terms = [(used.index(u), start, stop) for u, start, stop in runs]
        return pl.pallas_call(
            functools.partial(project_kernel, terms, len(used)),
            grid=(1,),
            in_specs=[pl.BlockSpec((rows, wide), lambda i, block=block: (block, 0)) for u in used for _, block in pieces[u]]
            + [pl.BlockSpec((wide, lanes), lambda i, unit=unit: (unit, 0)) for _, unit in weights]
            + [pl.BlockSpec(shape, lambda i: (0, column))] * len(extra),
            out_specs=pl.BlockSpec(shape, lambda i: (0, 0)),
            out_shape=of(*shape),
            compiler_params=params(24),
            name="project",
            cost_estimate=cost(6 * rows * wide * len(weights) * lanes, wide * lanes * len(weights) + 2 * rows * shape[1]),
        )(*[x for u in used for x, _ in pieces[u]], *[x for x, _ in weights], *extra)

    theirs = [
        strip([(taken, 0, 4)]),
        strip([(taken_near, 0, 4)], True),
        strip([(far_4, 0, 2), (far_5, 0, 2)]),
        strip([(both_4, 0, 2), (both_5, 0, 2)], True),
    ]
    mine = [
        strip([(kept, 0, 4)]),
        strip([(kept_near, 0, 4)], True),
        strip([(far_1, 0, 1), (far_2, 0, 2), (far_3, 0, 1)]),
        strip([(both_1, 0, 1), (both_2, 0, 2), (both_3, 0, 1)], True),
    ]
    pieces = own_pieces + other_pieces(last)
    product = project(pieces, theirs + mine, [(0, 0, 3), (0, 4, 8), (1, 0, 3), (1, 4, 8)])
    product = project(pieces, theirs + mine, [(2, 0, 8)], product)
    product, last = together((product, last))
    pieces = own_pieces + other_pieces(last)
    from_them = swap(project(pieces, theirs, [(3, 0, 4), (0, 3, 4), (1, 3, 4)], product, 0), 0, 1)
    product = project(pieces, mine, [(3, 0, 4)], product, 1)

    if strip_width % 128 == 0:
        parts = pl.pallas_call(
            functools.partial(route_kernel, groups, strip_width),
            grid_spec=pltpu.PrefetchScalarGridSpec(
                num_scalar_prefetch=1,
                grid=(1,),
                in_specs=[pl.BlockSpec(x.shape, lambda i, send: (0, 0)) for x in (product, from_them)],
                out_specs=[pl.BlockSpec((rows, size * strip_width), lambda i, send: (0, 0))] * steps,
                scratch_shapes=[pltpu.VMEM((steps, rows, size * strip_width), jnp.float32)],
            ),
            out_shape=[of(rows, size * strip_width)] * steps,
            compiler_params=params(12),
            name="route",
            cost_estimate=cost(0, 6 * rows * steps * size * strip_width),
        )(send_here, product, from_them)
    else:
        parts = jnp.stack(pieces_of(product + from_them, groups, strip_width))
        parts = [lax.dynamic_index_in_dim(parts, send_here[k], 0, False) for k in range(steps)]
    arrived = [lax.ppermute(part, AXES, perm) for part, perm in zip(parts, perms)]
    if strip_width % 128 == 0:
        return pl.pallas_call(
            functools.partial(assemble_kernel, size),
            grid_spec=pltpu.PrefetchScalarGridSpec(
                num_scalar_prefetch=1,
                grid=(1,),
                in_specs=[pl.BlockSpec(x.shape, lambda i, place: (0, 0)) for x in (*arrived, residual)],
                out_specs=pl.BlockSpec(residual.shape, lambda i, place: (0, 0)),
                scratch_shapes=[pltpu.VMEM((ctx, rows, strip_width), jnp.float32)],
            ),
            out_shape=of(*residual.shape),
            compiler_params=params(12),
            name="assemble",
            cost_estimate=cost(0, 3 * residual.size),
        )(place_here, *arrived, residual)
    blocks = jnp.stack([a[:, b * strip_width : (b + 1) * strip_width] for a in arrived for b in range(size)])
    projected = [lax.dynamic_index_in_dim(blocks, place_here[p], 0, False) for p in range(ctx)]
    return residual + jnp.concatenate(projected, axis=1)


def solution(mesh):
    placed = (
        P("ctx", "head"),
        P("ctx", "head"),
        P("ctx", "head"),
        P("head", None, None),
        P("head", None, None),
        P(None, ("ctx", "head")),
        P("ctx", "head"),
    )
    return jax.shard_map(
        functools.partial(body, mesh.shape["ctx"], mesh.shape["head"]),
        mesh=mesh,
        in_specs=placed,
        out_specs=P("ctx", "head"),
        check_vma=False,
    )
```

```python
import functools

import numpy as np

import jax
import jax.numpy as jnp
from jax import lax
from jax.experimental import pallas as pl
from jax.experimental.pallas import tpu as pltpu
from jax.sharding import PartitionSpec as P

HIGH = lax.Precision.HIGHEST
together = lax.optimization_barrier
AXES = ("ctx", "head")
PAIR = 2
EXTRA = 8
MIB = 1024 * 1024


def split(x):
    high = x.astype(jnp.bfloat16)
    return high, (x - high.astype(jnp.float32)).astype(jnp.bfloat16)


def dot3(a, b, dims=(((1,), (0,)), ((), ()))):
    a_high, a_low = split(a)
    b_high, b_low = split(b)
    dot = functools.partial(lax.dot_general, dimension_numbers=dims, preferred_element_type=jnp.float32)
    return dot(a_high, b_high) + (dot(a_high, b_low) + dot(a_low, b_high))


def features(rows, weights):
    scores = jnp.dot(rows, weights, precision=HIGH, preferred_element_type=jnp.float32)
    up = jnp.exp(scores - jnp.max(scores, axis=-1, keepdims=True))
    down = jnp.exp(jnp.min(scores, axis=-1, keepdims=True) - scores)
    up = up / jnp.sum(up, axis=-1, keepdims=True)
    down = down / jnp.sum(down, axis=-1, keepdims=True)
    return jnp.concatenate([up, down], axis=-1)


def arrange_kernel(plan, wide, starts, weight_ref, *refs):
    out_refs, sems = refs[:-1], refs[-1]
    copies = []
    for out_ref, picks in zip(out_refs, plan):
        for i, pick in enumerate(picks):
            source = weight_ref.at[pl.ds(pl.multiple_of(starts[pick], wide), wide), :]
            copies.append(pltpu.make_async_copy(source, out_ref.at[pl.ds(i * wide, wide), :], sems.at[len(copies)]))
            copies[-1].start()
    for copy in copies:
        copy.wait()


def key_kernel(first, k_ref, map_ref, v_ref, state_ref, feat_ref):
    heads, head_size, feat_half = map_ref.shape
    size = 2 * feat_half
    row = lax.broadcasted_iota(jnp.int32, (EXTRA, feat_half), 0)
    for i in range(heads):
        columns = slice(i * head_size, (i + 1) * head_size)
        feat = features(k_ref[:, columns], map_ref[i])
        feat_ref[i] = feat
        state_ref[i, :size, :] = dot3(feat, v_ref[:, columns], (((0,), (0,)), ((), ())))
        norm = jnp.sum(feat, axis=0, keepdims=True)
        state_ref[i, size:, :] = jnp.where(row < EXTRA // 2, norm[:, :feat_half], norm[:, feat_half:])


def attend(feat, key_feat, values, numer_ref, denom_ref):
    weights = dot3(feat, key_feat, (((1,), (1,)), ((), ())))
    row = lax.broadcasted_iota(jnp.int32, weights.shape, 0)
    column = lax.broadcasted_iota(jnp.int32, weights.shape, 1)
    weights = jnp.where(column <= row, weights, 0.0)
    numer_ref[0] = dot3(weights, values)
    denom_ref[0] = jnp.broadcast_to(jnp.sum(weights, axis=-1, keepdims=True), denom_ref.shape[1:])


def own_kernel(first, k_ref, k_map_ref, q_ref, q_map_ref, v_ref, state_ref, feat_ref, numer_ref, denom_ref):
    feat_half = k_map_ref.shape[2]
    size = 2 * feat_half
    row = lax.broadcasted_iota(jnp.int32, (EXTRA, feat_half), 0)
    key_feat = features(k_ref[...], k_map_ref[0])
    state_ref[0, :size, :] = dot3(key_feat, v_ref[...], (((0,), (0,)), ((), ())))
    norm = jnp.sum(key_feat, axis=0, keepdims=True)
    state_ref[0, size:, :] = jnp.where(row < EXTRA // 2, norm[:, :feat_half], norm[:, feat_half:])
    feat = features(q_ref[...], q_map_ref[0])
    feat_ref[0] = feat
    attend(feat, key_feat, v_ref[...], numer_ref, denom_ref)


def query_kernel(first, q_ref, q_map_ref, v_ref, key_feat_ref, feat_ref, numer_ref, denom_ref):
    feat = features(q_ref[...], q_map_ref[0])
    feat_ref[0] = feat
    attend(feat, key_feat_ref[0], v_ref[...], numer_ref, denom_ref)


def mix_kernel(qfeat_ref, numer_ref, denom_ref, prior_ref, *refs):
    feat = qfeat_ref[0]
    size = feat.shape[1]
    norm = jnp.concatenate(
        [prior_ref[0, size : size + 1, :], prior_ref[0, size + EXTRA // 2 : size + EXTRA // 2 + 1, :]], axis=1
    )
    denom = denom_ref[0] + jnp.sum(feat * norm, axis=-1, keepdims=True)
    mixed = (numer_ref[0] + dot3(feat, prior_ref[0, :size, :])) / denom
    if len(refs) == 1:
        refs[0][...] = mixed
    else:
        below_ref, out_ref, both_ref = refs
        out_ref[...] = mixed
        both_ref[...] = jnp.concatenate([mixed, below_ref[...]], axis=0)


def project_kernel(terms, units, *refs):
    rows_refs, refs = refs[: 2 * units], refs[2 * units :]
    count = sum(stop - start for _, start, stop in terms)
    w_refs, rest, out_ref = refs[:count], refs[count:-1], refs[-1]
    out_ref[...] = rest[0][...] if rest else jnp.zeros_like(out_ref)
    lanes = w_refs[0].shape[1]
    for unit, start, stop in terms:
        a = jnp.concatenate([rows_refs[2 * unit][...], rows_refs[2 * unit + 1][...]], axis=0)
        w = jnp.concatenate([ref[...] for ref in w_refs[: stop - start]], axis=1)
        w_refs = w_refs[stop - start :]
        out_ref[:, start * lanes : stop * lanes] += dot3(a, w)


def pieces_of(product, groups, width):
    rows = product.shape[0] // 2
    return [
        jnp.concatenate([product[d * rows : (d + 1) * rows, b * width : (b + 1) * width] for b in group], axis=1)
        for d in range(2)
        for group in groups
    ]


def route_kernel(groups, width, send, mine_ref, other_ref, *refs):
    out_refs, pieces_ref = refs[:-1], refs[-1]
    product = mine_ref[...] + other_ref[...]
    for j, piece in enumerate(pieces_of(product, groups, width)):
        pieces_ref[j] = piece
    for k, out_ref in enumerate(out_refs):
        out_ref[...] = pieces_ref[send[k]]


def assemble_kernel(size, place, *refs):
    arrived, (residual_ref, out_ref, blocks_ref) = refs[:-3], refs[-3:]
    width = blocks_ref.shape[2]
    for k, ref in enumerate(arrived):
        for b in range(size):
            blocks_ref[k * size + b] = ref[:, b * width : (b + 1) * width]
    for p in range(blocks_ref.shape[0]):
        columns = slice(p * width, (p + 1) * width)
        out_ref[:, columns] = residual_ref[:, columns] + blocks_ref[place[p]]


def route_tables(ctx, heads, rels):
    groups = {}
    for column, rel in enumerate(rels):
        groups.setdefault(rel * heads // ctx, []).append(column)
    groups = [groups[key] for key in sorted(groups)]
    size = len(groups[0])
    targets = {}
    for c in range(ctx):
        for h in range(heads):
            found = {}
            for d, step in enumerate((0, PAIR)):
                for g, columns in enumerate(groups):
                    to = (c ^ step) * heads + (c ^ rels[columns[0]]) * heads // ctx
                    found[to] = d * len(groups) + g
            targets[c * heads + h] = found
    classes = {}
    for device in sorted(targets):
        classes.setdefault(tuple(sorted(targets[device])), []).append(device)
    steps = 2 * len(groups)
    perms = [[] for _ in range(steps)]
    send = np.zeros((ctx * heads, steps), np.int32)
    arrives = {}
    for ends, sources in classes.items():
        for i, source in enumerate(sources):
            for k in range(steps):
                to = ends[i ^ k]
                perms[k].append((source, to))
                send[source, k] = targets[source][to]
                arrives[to, source] = k
    place = np.zeros((ctx * heads, ctx), np.int32)
    for c in range(ctx):
        for h in range(heads):
            for p in range(ctx):
                column_ctx, source_h = divmod(h * ctx + p, heads)
                source_c = (c & ~PAIR) | (column_ctx & PAIR)
                k = arrives[c * heads + h, source_c * heads + source_h]
                rel = source_c ^ column_ctx
                group = [g for g in groups if rels.index(rel) in g][0]
                place[c * heads + h, p] = k * size + group.index(rels.index(rel))
    return groups, perms, send, place


def body(ctx, heads, queries, keys, values, query_map, key_map, out_weight, residual):
    rows = queries.shape[0]
    heads_here, head_size, feat_half = query_map.shape
    feat_size = 2 * feat_half
    half = heads_here // 2
    wide = half * head_size
    depth = out_weight.shape[0] // heads
    strip_width = out_weight.shape[1]
    c = lax.axis_index("ctx")
    h = lax.axis_index("head")
    odd = c & 1

    def swap(x, by_ctx, by_head=0, keep=lambda c: True):
        pairs = [
            (i * heads + j, (i ^ by_ctx) * heads + (j ^ by_head))
            for i in range(ctx)
            for j in range(heads)
            if keep(i)
        ]
        return lax.ppermute(x, AXES, pairs)

    def of(*shape):
        return jax.ShapeDtypeStruct(shape, jnp.float32)

    def cost(products, count, exps=0):
        return pl.CostEstimate(flops=2 * products, bytes_accessed=4 * count, transcendentals=exps)

    def params(mib):
        return pltpu.CompilerParams(vmem_limit_bytes=mib * MIB)

    def head_block(size, lanes):
        return pl.BlockSpec((1, size, lanes), lambda i, *_: (i, 0, 0))

    def key_part(first):
        columns = pl.BlockSpec((rows, wide), lambda i, first: (0, first[0]))
        maps = pl.BlockSpec((half, head_size, feat_half), lambda i, first: (first[0], 0, 0))
        shapes = [of(half, feat_size + EXTRA, head_size), of(half, rows, feat_size)]
        return pl.pallas_call(
            key_kernel,
            grid_spec=pltpu.PrefetchScalarGridSpec(
                num_scalar_prefetch=1,
                grid=(1,),
                in_specs=[columns, maps, columns],
                out_specs=[pl.BlockSpec(s.shape, lambda i, first: (0, 0, 0)) for s in shapes],
            ),
            out_shape=shapes,
            compiler_params=params(60),
            name="key_part",
            cost_estimate=cost(
                6 * half * rows * head_size * (feat_half + feat_size),
                half * rows * (2 * head_size + 2 * feat_size),
                half * rows * feat_size,
            ),
        )(first, keys, key_map, values)

    columns = pl.BlockSpec((rows, head_size), lambda i, first: (0, first[0] * half + i))
    maps = pl.BlockSpec((1, head_size, feat_half), lambda i, first: (first[0] * half + i, 0, 0))
    query_shapes = [of(half, rows, feat_size), of(half, rows, head_size), of(half, rows, head_size)]
    query_specs = [head_block(*shape.shape[1:]) for shape in query_shapes]

    def own_part(first):
        outs = pl.pallas_call(
            own_kernel,
            grid_spec=pltpu.PrefetchScalarGridSpec(
                num_scalar_prefetch=1,
                grid=(half,),
                in_specs=[columns, maps, columns, maps, columns],
                out_specs=[head_block(feat_size + EXTRA, head_size), *query_specs],
            ),
            out_shape=[of(half, feat_size + EXTRA, head_size), *query_shapes],
            compiler_params=params(48),
            name="own_part",
            cost_estimate=cost(
                6 * half * rows * (head_size * (2 * feat_half + feat_size) + rows * (feat_size + head_size)),
                half * rows * (5 * head_size + 3 * feat_size),
                2 * half * rows * feat_size,
            ),
        )(first, keys, key_map, queries, query_map, values)
        return outs[0], outs[1:]

    def query_part(first, key_feat):
        return pl.pallas_call(
            query_kernel,
            grid_spec=pltpu.PrefetchScalarGridSpec(
                num_scalar_prefetch=1,
                grid=(half,),
                in_specs=[columns, maps, columns, head_block(rows, feat_size)],
                out_specs=query_specs,
            ),
            out_shape=query_shapes,
            compiler_params=params(32),
            name="query_part",
            cost_estimate=cost(
                6 * half * rows * (head_size * feat_half + rows * (feat_size + head_size)),
                half * rows * (4 * head_size + 2 * feat_size),
                half * rows * feat_size,
            ),
        )(first, queries, query_map, values, key_feat)

    def mix(qfeat, numer, denom, prior, below=None):
        columns = pl.BlockSpec((rows, head_size), lambda i: (0, i))
        out_specs, shapes = columns, of(rows, wide)
        if below is not None:
            out_specs = [columns, pl.BlockSpec((2 * rows, head_size), lambda i: (0, i))]
            shapes = [shapes, of(2 * rows, wide)]
        return pl.pallas_call(
            mix_kernel,
            grid=(half,),
            in_specs=[
                head_block(rows, feat_size),
                head_block(rows, head_size),
                head_block(rows, head_size),
                head_block(feat_size + EXTRA, head_size),
            ]
            + [columns] * (below is not None),
            out_specs=out_specs,
            out_shape=shapes,
            compiler_params=params(12),
            name="mix",
            cost_estimate=cost(
                3 * half * rows * feat_size * head_size, half * rows * (3 * head_size + 2 * feat_size)
            ),
        )(qfeat, numer, denom, prior, *([] if below is None else [below]))

    even = range(0, heads, 2)
    blocks = heads // 2
    bits = [1 << b for b in reversed(range(ctx.bit_length() - 1)) if 1 << b != PAIR]
    far, near = bits[-2:]
    rels = [0]
    for bit in bits[:-2]:
        rels = rels + [r | bit for r in rels]
    rels = [r | s for s in (0, near, far, far | near) for r in rels]

    def arranged(weight, starts, plan):
        shapes = [of(len(picks) * wide, strip_width) for picks in plan]
        count = sum(len(picks) for picks in plan)
        return pl.pallas_call(
            functools.partial(arrange_kernel, plan, wide),
            grid_spec=pltpu.PrefetchScalarGridSpec(
                num_scalar_prefetch=1,
                grid=(1,),
                in_specs=[pl.BlockSpec(memory_space=pl.ANY)],
                out_specs=[pl.BlockSpec(memory_space=pl.ANY)] * len(plan),
                scratch_shapes=[pltpu.SemaphoreType.DMA((count,))],
            ),
            out_shape=shapes,
            compiler_params=params(12),
            name="arrange",
            cost_estimate=cost(0, 2 * count * wide * strip_width),
        )(starts, weight)

    def widen(x):
        for bit in bits[:-2]:
            x = jnp.concatenate([x, swap(x, bit)], axis=1)
        return x

    order = [(which, d) for which in (0, 1) for d in even]
    part = len(order) // 4
    own = odd ^ np.array([0], np.int32)
    other = odd ^ np.array([1], np.int32)
    other_state, other_feat = key_part(other)
    flags = {1 << b: (c & 1 << b) != 0 for b in range(ctx.bit_length() - 1)}
    out_weight, other_state, flags = together((out_weight, other_state, flags))
    count = len(order)
    head_masks = np.array([flip ^ d for flip in (0, 1) for _, d in order], np.int32)
    half_masks = np.array([which for _ in (0, 1) for which, _ in order], np.int32)
    starts = (h ^ head_masks) * depth + (odd ^ half_masks) * wide
    (first_part,) = arranged(out_weight, starts, [list(range(part))])
    first_part = widen(first_part)
    far_1 = swap(first_part, far)
    from_neighbour = swap(other_state, 1)
    own_state, own_query = own_part(own)
    out_weight, own_state = together((out_weight, own_state))
    spans = [(part, 3 * part), (3 * part, count), (0, count)]
    spans += [(count, count + 2 * part), (count + 2 * part, 2 * count), (count, 2 * count)]
    kept_2, kept_3, kept, given_1, given_2, given = arranged(out_weight, starts, [list(range(*span)) for span in spans])
    kept_2, kept_3, kept = [widen(x) for x in (kept_2, kept_3, kept)]
    groups, perms, send, place = route_tables(ctx, heads, rels)
    steps, size = len(perms), len(groups[0])
    send_here, place_here = [
        lax.dynamic_slice(
            x.reshape(ctx, heads, -1), (c, h, 0), (1, 1, x.shape[1]), allow_negative_indices=False
        ).reshape(-1)
        for x in (send, place)
    ]

    from_neighbour, own_state, far_1, kept_2, kept, given_1, given_2, given = together(
        (from_neighbour, own_state, far_1, kept_2, kept, given_1, given_2, given)
    )
    far_2 = swap(kept_2, far)
    kept_near = swap(kept, near)
    taken, taken_1, taken_2 = [widen(swap(x, 0, 1)) for x in (given, given_1, given_2)]
    earlier = jnp.where(flags[1], from_neighbour, own_state)
    total = own_state + from_neighbour
    parts = []
    bit = 2
    while 2 * bit < ctx:
        if parts:
            total = total + parts[-1]
        parts.append(swap(total, bit))
        bit *= 2
    total, parts, far_2, kept_near, taken, taken_1, taken_2, far_1 = together(
        (total, parts, far_2, kept_near, taken, taken_1, taken_2, far_1)
    )
    taken_near = swap(taken, near)
    both_1 = swap(far_1, near)
    second = flags[PAIR]
    sent = sum(jnp.where(second, x[half // 2 :], x[: half // 2]) for x in (total, *parts[-1:]))
    got = swap(sent, bit, keep=lambda i: not i & bit)
    got, kept_3 = together((got, kept_3))
    met = swap(got, PAIR, keep=lambda i: i & bit)
    far_3 = swap(kept_3, far)
    got = jnp.concatenate([jnp.where(second, met, got), jnp.where(second, got, met)])
    got, taken_near, both_1, taken_1, far_2, other_feat = together(
        (got, taken_near, both_1, taken_1, far_2, other_feat)
    )
    before = got
    for b, part_sum in enumerate(parts):
        before = before + jnp.where(flags[2 << b], part_sum, 0.0)

    other_prior = swap(before + jnp.where(flags[1], 0.0, earlier), 1)
    own_mixed = mix(*own_query, before + jnp.where(flags[1], earlier, 0.0))
    head_bits = [1 << b for b in range(1, heads.bit_length() - 1)]

    def spread(pieces):
        for bit in head_bits[1:]:
            for (d, j), (x, i) in list(pieces.items()):
                pieces[d, j | bit] = (swap(x[i * rows : (i + 1) * rows], 0, bit), 0)
        return [(pieces[0, j], pieces[PAIR, j]) for j in even]

    own_mixed, far_3 = together((own_mixed, far_3))
    met, across = swap(own_mixed, PAIR), swap(own_mixed, 0, head_bits[0])
    far_4 = swap(taken_1, far)
    both_2 = swap(far_2, near)
    other_mixed, both = mix(*query_part(other, other_feat), other_prior, met)
    other_mixed, both, across, far_3, far_4, both_2, taken_2 = together(
        (other_mixed, both, across, far_3, far_4, both_2, taken_2)
    )
    other_met = swap(other_mixed, PAIR)
    both = swap(both, 0, head_bits[0])
    far_5 = swap(taken_2, far)
    both_3 = swap(far_3, near)
    both_4 = swap(far_4, near)
    other_met, both, far_5, both_3, both_4, send_here, place_here = together(
        (other_met, both, far_5, both_3, both_4, send_here, place_here)
    )
    both_5 = swap(far_5, near)
    last = swap(other_met, 0, head_bits[0])
    own_pieces = spread(
        {(0, 0): (own_mixed, 0), (PAIR, 0): (met, 0), (0, head_bits[0]): (across, 0), (PAIR, head_bits[0]): (both, 1)}
    )

    def other_pieces(last):
        pieces = {(0, 0): (other_mixed, 0), (PAIR, 0): (other_met, 0), (0, head_bits[0]): (both, 0)}
        return spread({**pieces, (PAIR, head_bits[0]): (last, 0)})

    lanes = kept.shape[1]

    def strip(parts, crossed=False):
        places = [(x, start * part + i) for x, start, stop in parts for i in range((stop - start) * part)]
        return places[blocks:] + places[:blocks] if crossed else places

    def project(pieces, strips, runs, total=None, column=0):
        runs = [(u, start, stop) for q, start, stop in runs for u in range(q * part, (q + 1) * part)]
        used = sorted({u for u, _, _ in runs})
        weights = [strips[s][u] for u, start, stop in runs for s in range(start, stop)]
        shape = (2 * rows, len(strips) * lanes)
        extra = [] if total is None else [total]
        terms = [(used.index(u), start, stop) for u, start, stop in runs]
        return pl.pallas_call(
            functools.partial(project_kernel, terms, len(used)),
            grid=(1,),
            in_specs=[pl.BlockSpec((rows, wide), lambda i, block=block: (block, 0)) for u in used for _, block in pieces[u]]
            + [pl.BlockSpec((wide, lanes), lambda i, unit=unit: (unit, 0)) for _, unit in weights]
            + [pl.BlockSpec(shape, lambda i: (0, column))] * len(extra),
            out_specs=pl.BlockSpec(shape, lambda i: (0, 0)),
            out_shape=of(*shape),
            compiler_params=params(24),
            name="project",
            cost_estimate=cost(6 * rows * wide * len(weights) * lanes, wide * lanes * len(weights) + 2 * rows * shape[1]),
        )(*[x for u in used for x, _ in pieces[u]], *[x for x, _ in weights], *extra)

    theirs = [
        strip([(taken, 0, 4)]),
        strip([(taken_near, 0, 4)], True),
        strip([(far_4, 0, 2), (far_5, 0, 2)]),
        strip([(both_4, 0, 2), (both_5, 0, 2)], True),
    ]
    mine = [
        strip([(kept, 0, 4)]),
        strip([(kept_near, 0, 4)], True),
        strip([(far_1, 0, 1), (far_2, 0, 2), (far_3, 0, 1)]),
        strip([(both_1, 0, 1), (both_2, 0, 2), (both_3, 0, 1)], True),
    ]
    pieces = own_pieces + other_pieces(last)
    product = project(pieces, theirs + mine, [(0, 0, 3), (0, 4, 8), (1, 0, 3), (1, 4, 8)])
    product = project(pieces, theirs + mine, [(2, 0, 8)], product)
    product, last = together((product, last))
    pieces = own_pieces + other_pieces(last)
    from_them = swap(project(pieces, theirs, [(3, 0, 4), (0, 3, 4), (1, 3, 4)], product, 0), 0, 1)
    product = project(pieces, mine, [(3, 0, 4)], product, 1)

    if strip_width % 128 == 0:
        parts = pl.pallas_call(
            functools.partial(route_kernel, groups, strip_width),
            grid_spec=pltpu.PrefetchScalarGridSpec(
                num_scalar_prefetch=1,
                grid=(1,),
                in_specs=[pl.BlockSpec(x.shape, lambda i, send: (0, 0)) for x in (product, from_them)],
                out_specs=[pl.BlockSpec((rows, size * strip_width), lambda i, send: (0, 0))] * steps,
                scratch_shapes=[pltpu.VMEM((steps, rows, size * strip_width), jnp.float32)],
            ),
            out_shape=[of(rows, size * strip_width)] * steps,
            compiler_params=params(12),
            name="route",
            cost_estimate=cost(0, 6 * rows * steps * size * strip_width),
        )(send_here, product, from_them)
    else:
        parts = jnp.stack(pieces_of(product + from_them, groups, strip_width))
        parts = [lax.dynamic_index_in_dim(parts, send_here[k], 0, False) for k in range(steps)]
    arrived = [lax.ppermute(part, AXES, perm) for part, perm in zip(parts, perms)]
    if strip_width % 128 == 0:
        return pl.pallas_call(
            functools.partial(assemble_kernel, size),
            grid_spec=pltpu.PrefetchScalarGridSpec(
                num_scalar_prefetch=1,
                grid=(1,),
                in_specs=[pl.BlockSpec(x.shape, lambda i, place: (0, 0)) for x in (*arrived, residual)],
                out_specs=pl.BlockSpec(residual.shape, lambda i, place: (0, 0)),
                scratch_shapes=[pltpu.VMEM((ctx, rows, strip_width), jnp.float32)],
            ),
            out_shape=of(*residual.shape),
            compiler_params=params(12),
            name="assemble",
            cost_estimate=cost(0, 3 * residual.size),
        )(place_here, *arrived, residual)
    blocks = jnp.stack([a[:, b * strip_width : (b + 1) * strip_width] for a in arrived for b in range(size)])
    projected = [lax.dynamic_index_in_dim(blocks, place_here[p], 0, False) for p in range(ctx)]
    return residual + jnp.concatenate(projected, axis=1)


def solution(mesh):
    placed = (
        P("ctx", "head"),
        P("ctx", "head"),
        P("ctx", "head"),
        P("head", None, None),
        P("head", None, None),
        P(None, ("ctx", "head")),
        P("ctx", "head"),
    )
    return jax.shard_map(
        functools.partial(body, mesh.shape["ctx"], mesh.shape["head"]),
        mesh=mesh,
        in_specs=placed,
        out_specs=P("ctx", "head"),
        check_vma=False,
    )
```

```python
import functools

import numpy as np

import jax
import jax.numpy as jnp
from jax import lax
from jax.experimental import pallas as pl
from jax.experimental.pallas import tpu as pltpu
from jax.sharding import PartitionSpec as P

HIGH = lax.Precision.HIGHEST
together = lax.optimization_barrier
AXES = ("ctx", "head")
PAIR = 2
EXTRA = 8
MIB = 1024 * 1024


def split(x):
    high = x.astype(jnp.bfloat16)
    return high, (x - high.astype(jnp.float32)).astype(jnp.bfloat16)


def dot3(a, b, dims=(((1,), (0,)), ((), ()))):
    a_high, a_low = split(a)
    b_high, b_low = split(b)
    dot = functools.partial(lax.dot_general, dimension_numbers=dims, preferred_element_type=jnp.float32)
    return dot(a_high, b_high) + (dot(a_high, b_low) + dot(a_low, b_high))


def features(rows, weights):
    scores = jnp.dot(rows, weights, precision=HIGH, preferred_element_type=jnp.float32)
    up = jnp.exp(scores - jnp.max(scores, axis=-1, keepdims=True))
    down = jnp.exp(jnp.min(scores, axis=-1, keepdims=True) - scores)
    up = up / jnp.sum(up, axis=-1, keepdims=True)
    down = down / jnp.sum(down, axis=-1, keepdims=True)
    return jnp.concatenate([up, down], axis=-1)


def arrange_kernel(plan, wide, starts, weight_ref, *refs):
    out_refs, sems = refs[:-1], refs[-1]
    copies = []
    for out_ref, picks in zip(out_refs, plan):
        for i, pick in enumerate(picks):
            source = weight_ref.at[pl.ds(pl.multiple_of(starts[pick], wide), wide), :]
            copies.append(pltpu.make_async_copy(source, out_ref.at[pl.ds(i * wide, wide), :], sems.at[len(copies)]))
            copies[-1].start()
    for copy in copies:
        copy.wait()


def key_kernel(first, k_ref, map_ref, v_ref, state_ref, feat_ref):
    heads, head_size, feat_half = map_ref.shape
    size = 2 * feat_half
    row = lax.broadcasted_iota(jnp.int32, (EXTRA, feat_half), 0)
    for i in range(heads):
        columns = slice(i * head_size, (i + 1) * head_size)
        feat = features(k_ref[:, columns], map_ref[i])
        feat_ref[i] = feat
        state_ref[i, :size, :] = dot3(feat, v_ref[:, columns], (((0,), (0,)), ((), ())))
        norm = jnp.sum(feat, axis=0, keepdims=True)
        state_ref[i, size:, :] = jnp.where(row < EXTRA // 2, norm[:, :feat_half], norm[:, feat_half:])


def attend(feat, key_feat, values, numer_ref, denom_ref):
    weights = dot3(feat, key_feat, (((1,), (1,)), ((), ())))
    row = lax.broadcasted_iota(jnp.int32, weights.shape, 0)
    column = lax.broadcasted_iota(jnp.int32, weights.shape, 1)
    weights = jnp.where(column <= row, weights, 0.0)
    numer_ref[0] = dot3(weights, values)
    denom_ref[0] = jnp.broadcast_to(jnp.sum(weights, axis=-1, keepdims=True), denom_ref.shape[1:])


def own_kernel(first, k_ref, k_map_ref, q_ref, q_map_ref, v_ref, state_ref, feat_ref, numer_ref, denom_ref):
    feat_half = k_map_ref.shape[2]
    size = 2 * feat_half
    row = lax.broadcasted_iota(jnp.int32, (EXTRA, feat_half), 0)
    key_feat = features(k_ref[...], k_map_ref[0])
    state_ref[0, :size, :] = dot3(key_feat, v_ref[...], (((0,), (0,)), ((), ())))
    norm = jnp.sum(key_feat, axis=0, keepdims=True)
    state_ref[0, size:, :] = jnp.where(row < EXTRA // 2, norm[:, :feat_half], norm[:, feat_half:])
    feat = features(q_ref[...], q_map_ref[0])
    feat_ref[0] = feat
    attend(feat, key_feat, v_ref[...], numer_ref, denom_ref)


def query_kernel(first, q_ref, q_map_ref, v_ref, key_feat_ref, feat_ref, numer_ref, denom_ref):
    feat = features(q_ref[...], q_map_ref[0])
    feat_ref[0] = feat
    attend(feat, key_feat_ref[0], v_ref[...], numer_ref, denom_ref)


def mix_kernel(qfeat_ref, numer_ref, denom_ref, prior_ref, *refs):
    feat = qfeat_ref[0]
    size = feat.shape[1]
    norm = jnp.concatenate(
        [prior_ref[0, size : size + 1, :], prior_ref[0, size + EXTRA // 2 : size + EXTRA // 2 + 1, :]], axis=1
    )
    denom = denom_ref[0] + jnp.sum(feat * norm, axis=-1, keepdims=True)
    mixed = (numer_ref[0] + dot3(feat, prior_ref[0, :size, :])) / denom
    if len(refs) == 1:
        refs[0][...] = mixed
    else:
        below_ref, out_ref, both_ref = refs
        out_ref[...] = mixed
        both_ref[...] = jnp.concatenate([mixed, below_ref[...]], axis=0)


def project_kernel(terms, units, *refs):
    rows_refs, refs = refs[: 2 * units], refs[2 * units :]
    count = sum(stop - start for _, start, stop in terms)
    w_refs, rest, out_ref = refs[:count], refs[count:-1], refs[-1]
    out_ref[...] = rest[0][...] if rest else jnp.zeros_like(out_ref)
    lanes = w_refs[0].shape[1]
    for unit, start, stop in terms:
        a = jnp.concatenate([rows_refs[2 * unit][...], rows_refs[2 * unit + 1][...]], axis=0)
        w = jnp.concatenate([ref[...] for ref in w_refs[: stop - start]], axis=1)
        w_refs = w_refs[stop - start :]
        out_ref[:, start * lanes : stop * lanes] += dot3(a, w)


def pieces_of(product, groups, width):
    rows = product.shape[0] // 2
    return [
        jnp.concatenate([product[d * rows : (d + 1) * rows, b * width : (b + 1) * width] for b in group], axis=1)
        for d in range(2)
        for group in groups
    ]


def route_kernel(groups, width, send, mine_ref, other_ref, *refs):
    out_refs, pieces_ref = refs[:-1], refs[-1]
    product = mine_ref[...] + other_ref[...]
    for j, piece in enumerate(pieces_of(product, groups, width)):
        pieces_ref[j] = piece
    for k, out_ref in enumerate(out_refs):
        out_ref[...] = pieces_ref[send[k]]


def assemble_kernel(size, place, *refs):
    arrived, (residual_ref, out_ref, blocks_ref) = refs[:-3], refs[-3:]
    width = blocks_ref.shape[2]
    for k, ref in enumerate(arrived):
        for b in range(size):
            blocks_ref[k * size + b] = ref[:, b * width : (b + 1) * width]
    for p in range(blocks_ref.shape[0]):
        columns = slice(p * width, (p + 1) * width)
        out_ref[:, columns] = residual_ref[:, columns] + blocks_ref[place[p]]


def route_tables(ctx, heads, rels):
    groups = {}
    for column, rel in enumerate(rels):
        groups.setdefault(rel * heads // ctx, []).append(column)
    groups = [groups[key] for key in sorted(groups)]
    size = len(groups[0])
    targets = {}
    for c in range(ctx):
        for h in range(heads):
            found = {}
            for d, step in enumerate((0, PAIR)):
                for g, columns in enumerate(groups):
                    to = (c ^ step) * heads + (c ^ rels[columns[0]]) * heads // ctx
                    found[to] = d * len(groups) + g
            targets[c * heads + h] = found
    classes = {}
    for device in sorted(targets):
        classes.setdefault(tuple(sorted(targets[device])), []).append(device)
    steps = 2 * len(groups)
    perms = [[] for _ in range(steps)]
    send = np.zeros((ctx * heads, steps), np.int32)
    arrives = {}
    for ends, sources in classes.items():
        for i, source in enumerate(sources):
            for k in range(steps):
                to = ends[i ^ k]
                perms[k].append((source, to))
                send[source, k] = targets[source][to]
                arrives[to, source] = k
    place = np.zeros((ctx * heads, ctx), np.int32)
    for c in range(ctx):
        for h in range(heads):
            for p in range(ctx):
                column_ctx, source_h = divmod(h * ctx + p, heads)
                source_c = (c & ~PAIR) | (column_ctx & PAIR)
                k = arrives[c * heads + h, source_c * heads + source_h]
                rel = source_c ^ column_ctx
                group = [g for g in groups if rels.index(rel) in g][0]
                place[c * heads + h, p] = k * size + group.index(rels.index(rel))
    return groups, perms, send, place


def body(ctx, heads, queries, keys, values, query_map, key_map, out_weight, residual):
    rows = queries.shape[0]
    heads_here, head_size, feat_half = query_map.shape
    feat_size = 2 * feat_half
    half = heads_here // 2
    wide = half * head_size
    depth = out_weight.shape[0] // heads
    strip_width = out_weight.shape[1]
    c = lax.axis_index("ctx")
    h = lax.axis_index("head")
    odd = c & 1

    def swap(x, by_ctx, by_head=0, keep=lambda c: True):
        pairs = [
            (i * heads + j, (i ^ by_ctx) * heads + (j ^ by_head))
            for i in range(ctx)
            for j in range(heads)
            if keep(i)
        ]
        return lax.ppermute(x, AXES, pairs)

    def of(*shape):
        return jax.ShapeDtypeStruct(shape, jnp.float32)

    def cost(products, count, exps=0):
        return pl.CostEstimate(flops=2 * products, bytes_accessed=4 * count, transcendentals=exps)

    def params(mib):
        return pltpu.CompilerParams(vmem_limit_bytes=mib * MIB)

    def head_block(size, lanes):
        return pl.BlockSpec((1, size, lanes), lambda i, *_: (i, 0, 0))

    def key_part(first):
        columns = pl.BlockSpec((rows, wide), lambda i, first: (0, first[0]))
        maps = pl.BlockSpec((half, head_size, feat_half), lambda i, first: (first[0], 0, 0))
        shapes = [of(half, feat_size + EXTRA, head_size), of(half, rows, feat_size)]
        return pl.pallas_call(
            key_kernel,
            grid_spec=pltpu.PrefetchScalarGridSpec(
                num_scalar_prefetch=1,
                grid=(1,),
                in_specs=[columns, maps, columns],
                out_specs=[pl.BlockSpec(s.shape, lambda i, first: (0, 0, 0)) for s in shapes],
            ),
            out_shape=shapes,
            compiler_params=params(60),
            name="key_part",
            cost_estimate=cost(
                6 * half * rows * head_size * (feat_half + feat_size),
                half * rows * (2 * head_size + 2 * feat_size),
                half * rows * feat_size,
            ),
        )(first, keys, key_map, values)

    columns = pl.BlockSpec((rows, head_size), lambda i, first: (0, first[0] * half + i))
    maps = pl.BlockSpec((1, head_size, feat_half), lambda i, first: (first[0] * half + i, 0, 0))
    query_shapes = [of(half, rows, feat_size), of(half, rows, head_size), of(half, rows, head_size)]
    query_specs = [head_block(*shape.shape[1:]) for shape in query_shapes]

    def own_part(first):
        outs = pl.pallas_call(
            own_kernel,
            grid_spec=pltpu.PrefetchScalarGridSpec(
                num_scalar_prefetch=1,
                grid=(half,),
                in_specs=[columns, maps, columns, maps, columns],
                out_specs=[head_block(feat_size + EXTRA, head_size), *query_specs],
            ),
            out_shape=[of(half, feat_size + EXTRA, head_size), *query_shapes],
            compiler_params=params(48),
            name="own_part",
            cost_estimate=cost(
                6 * half * rows * (head_size * (2 * feat_half + feat_size) + rows * (feat_size + head_size)),
                half * rows * (5 * head_size + 3 * feat_size),
                2 * half * rows * feat_size,
            ),
        )(first, keys, key_map, queries, query_map, values)
        return outs[0], outs[1:]

    def query_part(first, key_feat):
        return pl.pallas_call(
            query_kernel,
            grid_spec=pltpu.PrefetchScalarGridSpec(
                num_scalar_prefetch=1,
                grid=(half,),
                in_specs=[columns, maps, columns, head_block(rows, feat_size)],
                out_specs=query_specs,
            ),
            out_shape=query_shapes,
            compiler_params=params(32),
            name="query_part",
            cost_estimate=cost(
                6 * half * rows * (head_size * feat_half + rows * (feat_size + head_size)),
                half * rows * (4 * head_size + 2 * feat_size),
                half * rows * feat_size,
            ),
        )(first, queries, query_map, values, key_feat)

    def mix(qfeat, numer, denom, prior, below=None):
        columns = pl.BlockSpec((rows, head_size), lambda i: (0, i))
        out_specs, shapes = columns, of(rows, wide)
        if below is not None:
            out_specs = [columns, pl.BlockSpec((2 * rows, head_size), lambda i: (0, i))]
            shapes = [shapes, of(2 * rows, wide)]
        return pl.pallas_call(
            mix_kernel,
            grid=(half,),
            in_specs=[
                head_block(rows, feat_size),
                head_block(rows, head_size),
                head_block(rows, head_size),
                head_block(feat_size + EXTRA, head_size),
            ]
            + [columns] * (below is not None),
            out_specs=out_specs,
            out_shape=shapes,
            compiler_params=params(12),
            name="mix",
            cost_estimate=cost(
                3 * half * rows * feat_size * head_size, half * rows * (3 * head_size + 2 * feat_size)
            ),
        )(qfeat, numer, denom, prior, *([] if below is None else [below]))

    even = range(0, heads, 2)
    blocks = heads // 2
    bits = [1 << b for b in reversed(range(ctx.bit_length() - 1)) if 1 << b != PAIR]
    far, near = bits[-2:]
    rels = [0]
    for bit in bits[:-2]:
        rels = rels + [r | bit for r in rels]
    rels = [r | s for s in (0, near, far, far | near) for r in rels]

    def arranged(weight, starts, plan):
        shapes = [of(len(picks) * wide, strip_width) for picks in plan]
        count = sum(len(picks) for picks in plan)
        return pl.pallas_call(
            functools.partial(arrange_kernel, plan, wide),
            grid_spec=pltpu.PrefetchScalarGridSpec(
                num_scalar_prefetch=1,
                grid=(1,),
                in_specs=[pl.BlockSpec(memory_space=pl.ANY)],
                out_specs=[pl.BlockSpec(memory_space=pl.ANY)] * len(plan),
                scratch_shapes=[pltpu.SemaphoreType.DMA((count,))],
            ),
            out_shape=shapes,
            compiler_params=params(12),
            name="arrange",
            cost_estimate=cost(0, 2 * count * wide * strip_width),
        )(starts, weight)

    def widen(x):
        for bit in bits[:-2]:
            x = jnp.concatenate([x, swap(x, bit)], axis=1)
        return x

    order = [(which, d) for which in (0, 1) for d in even]
    part = len(order) // 4
    own = odd ^ np.array([0], np.int32)
    other = odd ^ np.array([1], np.int32)
    other_state, other_feat = key_part(other)
    flags = {1 << b: (c & 1 << b) != 0 for b in range(ctx.bit_length() - 1)}
    out_weight, other_state, flags = together((out_weight, other_state, flags))
    count = len(order)
    head_masks = np.array([flip ^ d for flip in (0, 1) for _, d in order], np.int32)
    half_masks = np.array([which for _ in (0, 1) for which, _ in order], np.int32)
    starts = (h ^ head_masks) * depth + (odd ^ half_masks) * wide
    (first_part,) = arranged(out_weight, starts, [list(range(part))])
    first_part = widen(first_part)
    far_1 = swap(first_part, far)
    from_neighbour = swap(other_state, 1)
    own_state, own_query = own_part(own)
    out_weight, own_state = together((out_weight, own_state))
    spans = [(part, 3 * part), (3 * part, count), (0, count)]
    spans += [(count, count + 2 * part), (count + 2 * part, 2 * count), (count, 2 * count)]
    kept_2, kept_3, kept, given_1, given_2, given = arranged(out_weight, starts, [list(range(*span)) for span in spans])
    kept_2, kept_3, kept = [widen(x) for x in (kept_2, kept_3, kept)]
    groups, perms, send, place = route_tables(ctx, heads, rels)
    steps, size = len(perms), len(groups[0])
    send_here, place_here = [
        lax.dynamic_slice(
            x.reshape(ctx, heads, -1), (c, h, 0), (1, 1, x.shape[1]), allow_negative_indices=False
        ).reshape(-1)
        for x in (send, place)
    ]

    from_neighbour, own_state, far_1, kept_2, kept, given_1, given_2, given = together(
        (from_neighbour, own_state, far_1, kept_2, kept, given_1, given_2, given)
    )
    far_2 = swap(kept_2, far)
    kept_near = swap(kept, near)
    taken, taken_1, taken_2 = [widen(swap(x, 0, 1)) for x in (given, given_1, given_2)]
    earlier = jnp.where(flags[1], from_neighbour, own_state)
    total = own_state + from_neighbour
    parts = []
    bit = 2
    while 2 * bit < ctx:
        if parts:
            total = total + parts[-1]
        parts.append(swap(total, bit))
        bit *= 2
    total, parts, far_2, kept_near, taken, taken_1, taken_2, far_1 = together(
        (total, parts, far_2, kept_near, taken, taken_1, taken_2, far_1)
    )
    taken_near = swap(taken, near)
    second = flags[PAIR]
    sent = sum(jnp.where(second, x[half // 2 :], x[: half // 2]) for x in (total, *parts[-1:]))
    got = swap(sent, bit, keep=lambda i: not i & bit)
    got, kept_3 = together((got, kept_3))
    met = swap(got, PAIR, keep=lambda i: i & bit)
    far_3 = swap(kept_3, far)
    got = jnp.concatenate([jnp.where(second, met, got), jnp.where(second, got, met)])
    got, taken_near, taken_1, far_2, other_feat = together((got, taken_near, taken_1, far_2, other_feat))
    before = got
    for b, part_sum in enumerate(parts):
        before = before + jnp.where(flags[2 << b], part_sum, 0.0)

    other_prior = swap(before + jnp.where(flags[1], 0.0, earlier), 1)
    own_mixed = mix(*own_query, before + jnp.where(flags[1], earlier, 0.0))
    head_bits = [1 << b for b in range(1, heads.bit_length() - 1)]

    def spread(pieces):
        for bit in head_bits[1:]:
            for (d, j), (x, i) in list(pieces.items()):
                pieces[d, j | bit] = (swap(x[i * rows : (i + 1) * rows], 0, bit), 0)
        return [(pieces[0, j], pieces[PAIR, j]) for j in even]

    own_mixed, far_3 = together((own_mixed, far_3))
    met, across = swap(own_mixed, PAIR), swap(own_mixed, 0, head_bits[0])
    far_4 = swap(taken_1, far)
    both_2 = swap(far_2, near)
    other_mixed, both = mix(*query_part(other, other_feat), other_prior, met)
    outer = jnp.concatenate([far_1, far_3])
    other_mixed, both, across, outer, far_4, both_2, taken_2 = together(
        (other_mixed, both, across, outer, far_4, both_2, taken_2)
    )
    other_met = swap(other_mixed, PAIR)
    both = swap(both, 0, head_bits[0])
    far_5 = swap(taken_2, far)
    both_1 = swap(outer, near)
    both_4 = swap(far_4, near)
    other_met, both, far_5, both_1, both_4, send_here, place_here = together(
        (other_met, both, far_5, both_1, both_4, send_here, place_here)
    )
    both_5 = swap(far_5, near)
    last = swap(other_met, 0, head_bits[0])
    own_pieces = spread(
        {(0, 0): (own_mixed, 0), (PAIR, 0): (met, 0), (0, head_bits[0]): (across, 0), (PAIR, head_bits[0]): (both, 1)}
    )

    def other_pieces(last):
        pieces = {(0, 0): (other_mixed, 0), (PAIR, 0): (other_met, 0), (0, head_bits[0]): (both, 0)}
        return spread({**pieces, (PAIR, head_bits[0]): (last, 0)})

    lanes = kept.shape[1]

    def strip(parts, crossed=False):
        places = [(x, start * part + i) for x, start, stop in parts for i in range((stop - start) * part)]
        return places[blocks:] + places[:blocks] if crossed else places

    def project(pieces, strips, runs, total=None, column=0):
        runs = [(u, start, stop) for q, start, stop in runs for u in range(q * part, (q + 1) * part)]
        used = sorted({u for u, _, _ in runs})
        weights = [strips[s][u] for u, start, stop in runs for s in range(start, stop)]
        shape = (2 * rows, len(strips) * lanes)
        extra = [] if total is None else [total]
        terms = [(used.index(u), start, stop) for u, start, stop in runs]
        return pl.pallas_call(
            functools.partial(project_kernel, terms, len(used)),
            grid=(1,),
            in_specs=[pl.BlockSpec((rows, wide), lambda i, block=block: (block, 0)) for u in used for _, block in pieces[u]]
            + [pl.BlockSpec((wide, lanes), lambda i, unit=unit: (unit, 0)) for _, unit in weights]
            + [pl.BlockSpec(shape, lambda i: (0, column))] * len(extra),
            out_specs=pl.BlockSpec(shape, lambda i: (0, 0)),
            out_shape=of(*shape),
            compiler_params=params(24),
            name="project",
            cost_estimate=cost(6 * rows * wide * len(weights) * lanes, wide * lanes * len(weights) + 2 * rows * shape[1]),
        )(*[x for u in used for x, _ in pieces[u]], *[x for x, _ in weights], *extra)

    theirs = [
        strip([(taken, 0, 4)]),
        strip([(taken_near, 0, 4)], True),
        strip([(far_4, 0, 2), (far_5, 0, 2)]),
        strip([(both_4, 0, 2), (both_5, 0, 2)], True),
    ]
    mine = [
        strip([(kept, 0, 4)]),
        strip([(kept_near, 0, 4)], True),
        strip([(far_1, 0, 1), (far_2, 0, 2), (far_3, 0, 1)]),
        strip([(both_1, 0, 1), (both_2, 0, 2), (both_1, 1, 2)], True),
    ]
    pieces = own_pieces + other_pieces(last)
    product = project(pieces, theirs + mine, [(0, 0, 3), (0, 4, 8), (1, 0, 3), (1, 4, 8)])
    product = project(pieces, theirs + mine, [(2, 0, 8)], product)
    product, last = together((product, last))
    pieces = own_pieces + other_pieces(last)
    from_them = swap(project(pieces, theirs, [(3, 0, 4), (0, 3, 4), (1, 3, 4)], product, 0), 0, 1)
    product = project(pieces, mine, [(3, 0, 4)], product, 1)

    if strip_width % 128 == 0:
        parts = pl.pallas_call(
            functools.partial(route_kernel, groups, strip_width),
            grid_spec=pltpu.PrefetchScalarGridSpec(
                num_scalar_prefetch=1,
                grid=(1,),
                in_specs=[pl.BlockSpec(x.shape, lambda i, send: (0, 0)) for x in (product, from_them)],
                out_specs=[pl.BlockSpec((rows, size * strip_width), lambda i, send: (0, 0))] * steps,
                scratch_shapes=[pltpu.VMEM((steps, rows, size * strip_width), jnp.float32)],
            ),
            out_shape=[of(rows, size * strip_width)] * steps,
            compiler_params=params(12),
            name="route",
            cost_estimate=cost(0, 6 * rows * steps * size * strip_width),
        )(send_here, product, from_them)
    else:
        parts = jnp.stack(pieces_of(product + from_them, groups, strip_width))
        parts = [lax.dynamic_index_in_dim(parts, send_here[k], 0, False) for k in range(steps)]
    arrived = [lax.ppermute(part, AXES, perm) for part, perm in zip(parts, perms)]
    if strip_width % 128 == 0:
        return pl.pallas_call(
            functools.partial(assemble_kernel, size),
            grid_spec=pltpu.PrefetchScalarGridSpec(
                num_scalar_prefetch=1,
                grid=(blocks,),
                in_specs=[
                    pl.BlockSpec((rows // blocks, x.shape[1]), lambda i, place: (i, 0)) for x in (*arrived, residual)
                ],
                out_specs=pl.BlockSpec((rows // blocks, residual.shape[1]), lambda i, place: (i, 0)),
                scratch_shapes=[pltpu.VMEM((ctx, rows // blocks, strip_width), jnp.float32)],
            ),
            out_shape=of(*residual.shape),
            compiler_params=params(12),
            name="assemble",
            cost_estimate=cost(0, 3 * residual.size),
        )(place_here, *arrived, residual)
    blocks = jnp.stack([a[:, b * strip_width : (b + 1) * strip_width] for a in arrived for b in range(size)])
    projected = [lax.dynamic_index_in_dim(blocks, place_here[p], 0, False) for p in range(ctx)]
    return residual + jnp.concatenate(projected, axis=1)


def solution(mesh):
    placed = (
        P("ctx", "head"),
        P("ctx", "head"),
        P("ctx", "head"),
        P("head", None, None),
        P("head", None, None),
        P(None, ("ctx", "head")),
        P("ctx", "head"),
    )
    return jax.shard_map(
        functools.partial(body, mesh.shape["ctx"], mesh.shape["head"]),
        mesh=mesh,
        in_specs=placed,
        out_specs=P("ctx", "head"),
        check_vma=False,
    )
```

```python
import functools

import numpy as np

import jax
import jax.numpy as jnp
from jax import lax
from jax.experimental import pallas as pl
from jax.experimental.pallas import tpu as pltpu
from jax.sharding import PartitionSpec as P

HIGH = lax.Precision.HIGHEST
together = lax.optimization_barrier
AXES = ("ctx", "head")
PAIR = 2
EXTRA = 8
MIB = 1024 * 1024


def split(x):
    high = x.astype(jnp.bfloat16)
    return high, (x - high.astype(jnp.float32)).astype(jnp.bfloat16)


def dot3(a, b, dims=(((1,), (0,)), ((), ()))):
    a_high, a_low = split(a)
    b_high, b_low = split(b)
    dot = functools.partial(lax.dot_general, dimension_numbers=dims, preferred_element_type=jnp.float32)
    return dot(a_high, b_high) + (dot(a_high, b_low) + dot(a_low, b_high))


def features(rows, weights):
    scores = jnp.dot(rows, weights, precision=HIGH, preferred_element_type=jnp.float32)
    up = jnp.exp(scores - jnp.max(scores, axis=-1, keepdims=True))
    down = jnp.exp(jnp.min(scores, axis=-1, keepdims=True) - scores)
    up = up / jnp.sum(up, axis=-1, keepdims=True)
    down = down / jnp.sum(down, axis=-1, keepdims=True)
    return jnp.concatenate([up, down], axis=-1)


def arrange_kernel(plan, wide, starts, weight_ref, *refs):
    out_refs, sems = refs[:-1], refs[-1]
    copies = []
    for out_ref, picks in zip(out_refs, plan):
        for i, pick in enumerate(picks):
            source = weight_ref.at[pl.ds(pl.multiple_of(starts[pick], wide), wide), :]
            copies.append(pltpu.make_async_copy(source, out_ref.at[pl.ds(i * wide, wide), :], sems.at[len(copies)]))
            copies[-1].start()
    for copy in copies:
        copy.wait()


def key_kernel(first, k_ref, map_ref, v_ref, state_ref, feat_ref):
    heads, head_size, feat_half = map_ref.shape
    size = 2 * feat_half
    row = lax.broadcasted_iota(jnp.int32, (EXTRA, feat_half), 0)
    for i in range(heads):
        columns = slice(i * head_size, (i + 1) * head_size)
        feat = features(k_ref[:, columns], map_ref[i])
        feat_ref[i] = feat
        state_ref[i, :size, :] = dot3(feat, v_ref[:, columns], (((0,), (0,)), ((), ())))
        norm = jnp.sum(feat, axis=0, keepdims=True)
        state_ref[i, size:, :] = jnp.where(row < EXTRA // 2, norm[:, :feat_half], norm[:, feat_half:])


def attend(feat, key_feat, values, numer_ref, denom_ref):
    weights = dot3(feat, key_feat, (((1,), (1,)), ((), ())))
    row = lax.broadcasted_iota(jnp.int32, weights.shape, 0)
    column = lax.broadcasted_iota(jnp.int32, weights.shape, 1)
    weights = jnp.where(column <= row, weights, 0.0)
    numer_ref[0] = dot3(weights, values)
    denom_ref[0] = jnp.broadcast_to(jnp.sum(weights, axis=-1, keepdims=True), denom_ref.shape[1:])


def own_kernel(first, k_ref, k_map_ref, q_ref, q_map_ref, v_ref, state_ref, feat_ref, numer_ref, denom_ref):
    feat_half = k_map_ref.shape[2]
    size = 2 * feat_half
    row = lax.broadcasted_iota(jnp.int32, (EXTRA, feat_half), 0)
    key_feat = features(k_ref[...], k_map_ref[0])
    state_ref[0, :size, :] = dot3(key_feat, v_ref[...], (((0,), (0,)), ((), ())))
    norm = jnp.sum(key_feat, axis=0, keepdims=True)
    state_ref[0, size:, :] = jnp.where(row < EXTRA // 2, norm[:, :feat_half], norm[:, feat_half:])
    feat = features(q_ref[...], q_map_ref[0])
    feat_ref[0] = feat
    attend(feat, key_feat, v_ref[...], numer_ref, denom_ref)


def query_kernel(first, q_ref, q_map_ref, v_ref, key_feat_ref, feat_ref, numer_ref, denom_ref):
    feat = features(q_ref[...], q_map_ref[0])
    feat_ref[0] = feat
    attend(feat, key_feat_ref[0], v_ref[...], numer_ref, denom_ref)


def mix_kernel(qfeat_ref, numer_ref, denom_ref, prior_ref, *refs):
    feat = qfeat_ref[0]
    size = feat.shape[1]
    norm = jnp.concatenate(
        [prior_ref[0, size : size + 1, :], prior_ref[0, size + EXTRA // 2 : size + EXTRA // 2 + 1, :]], axis=1
    )
    denom = denom_ref[0] + jnp.sum(feat * norm, axis=-1, keepdims=True)
    mixed = (numer_ref[0] + dot3(feat, prior_ref[0, :size, :])) / denom
    if len(refs) == 1:
        refs[0][...] = mixed
    else:
        below_ref, out_ref, both_ref = refs
        out_ref[...] = mixed
        both_ref[...] = jnp.concatenate([mixed, below_ref[...]], axis=0)


def project_kernel(terms, units, *refs):
    rows_refs, refs = refs[: 2 * units], refs[2 * units :]
    count = sum(stop - start for _, start, stop in terms)
    w_refs, rest, out_ref = refs[:count], refs[count:-1], refs[-1]
    out_ref[...] = rest[0][...] if rest else jnp.zeros_like(out_ref)
    lanes = w_refs[0].shape[1]
    for unit, start, stop in terms:
        a = jnp.concatenate([rows_refs[2 * unit][...], rows_refs[2 * unit + 1][...]], axis=0)
        w = jnp.concatenate([ref[...] for ref in w_refs[: stop - start]], axis=1)
        w_refs = w_refs[stop - start :]
        out_ref[:, start * lanes : stop * lanes] += dot3(a, w)


def pieces_of(product, groups, width):
    rows = product.shape[0] // 2
    return [
        jnp.concatenate([product[d * rows : (d + 1) * rows, b * width : (b + 1) * width] for b in group], axis=1)
        for d in range(2)
        for group in groups
    ]


def route_kernel(groups, width, send, mine_ref, other_ref, *refs):
    out_refs, pieces_ref = refs[:-1], refs[-1]
    product = mine_ref[...] + other_ref[...]
    for j, piece in enumerate(pieces_of(product, groups, width)):
        pieces_ref[j] = piece
    for k, out_ref in enumerate(out_refs):
        out_ref[...] = pieces_ref[send[k]]


def assemble_kernel(size, place, *refs):
    arrived, (residual_ref, out_ref, blocks_ref) = refs[:-3], refs[-3:]
    width = blocks_ref.shape[2]
    for k, ref in enumerate(arrived):
        for b in range(size):
            blocks_ref[k * size + b] = ref[:, b * width : (b + 1) * width]
    for p in range(blocks_ref.shape[0]):
        columns = slice(p * width, (p + 1) * width)
        out_ref[:, columns] = residual_ref[:, columns] + blocks_ref[place[p]]


def route_tables(ctx, heads, rels):
    groups = {}
    for column, rel in enumerate(rels):
        groups.setdefault(rel * heads // ctx, []).append(column)
    groups = [groups[key] for key in sorted(groups)]
    size = len(groups[0])
    targets = {}
    for c in range(ctx):
        for h in range(heads):
            found = {}
            for d, step in enumerate((0, PAIR)):
                for g, columns in enumerate(groups):
                    to = (c ^ step) * heads + (c ^ rels[columns[0]]) * heads // ctx
                    found[to] = d * len(groups) + g
            targets[c * heads + h] = found
    classes = {}

    def turn(device):
        c, h = divmod(device, heads)
        return c, h & 1, (h >> 1) ^ (h & 1)

    for device in sorted(targets, key=turn):
        classes.setdefault(tuple(sorted(targets[device])), []).append(device)
    steps = 2 * len(groups)
    perms = [[] for _ in range(steps)]
    send = np.zeros((ctx * heads, steps), np.int32)
    arrives = {}
    for ends, sources in classes.items():
        for i, source in enumerate(sources):
            for k in range(steps):
                to = ends[i ^ k]
                perms[k].append((source, to))
                send[source, k] = targets[source][to]
                arrives[to, source] = k
    place = np.zeros((ctx * heads, ctx), np.int32)
    for c in range(ctx):
        for h in range(heads):
            for p in range(ctx):
                column_ctx, source_h = divmod(h * ctx + p, heads)
                source_c = (c & ~PAIR) | (column_ctx & PAIR)
                k = arrives[c * heads + h, source_c * heads + source_h]
                rel = source_c ^ column_ctx
                group = [g for g in groups if rels.index(rel) in g][0]
                place[c * heads + h, p] = k * size + group.index(rels.index(rel))
    return groups, perms, send, place


def body(ctx, heads, queries, keys, values, query_map, key_map, out_weight, residual):
    rows = queries.shape[0]
    heads_here, head_size, feat_half = query_map.shape
    feat_size = 2 * feat_half
    half = heads_here // 2
    wide = half * head_size
    depth = out_weight.shape[0] // heads
    strip_width = out_weight.shape[1]
    c = lax.axis_index("ctx")
    h = lax.axis_index("head")
    odd = c & 1

    def swap(x, by_ctx, by_head=0, keep=lambda c: True):
        pairs = [
            (i * heads + j, (i ^ by_ctx) * heads + (j ^ by_head))
            for i in range(ctx)
            for j in range(heads)
            if keep(i)
        ]
        return lax.ppermute(x, AXES, pairs)

    def of(*shape):
        return jax.ShapeDtypeStruct(shape, jnp.float32)

    def cost(products, count, exps=0):
        return pl.CostEstimate(flops=2 * products, bytes_accessed=4 * count, transcendentals=exps)

    def params(mib):
        return pltpu.CompilerParams(vmem_limit_bytes=mib * MIB)

    def head_block(size, lanes):
        return pl.BlockSpec((1, size, lanes), lambda i, *_: (i, 0, 0))

    def key_part(first):
        columns = pl.BlockSpec((rows, wide), lambda i, first: (0, first[0]))
        maps = pl.BlockSpec((half, head_size, feat_half), lambda i, first: (first[0], 0, 0))
        shapes = [of(half, feat_size + EXTRA, head_size), of(half, rows, feat_size)]
        return pl.pallas_call(
            key_kernel,
            grid_spec=pltpu.PrefetchScalarGridSpec(
                num_scalar_prefetch=1,
                grid=(1,),
                in_specs=[columns, maps, columns],
                out_specs=[pl.BlockSpec(s.shape, lambda i, first: (0, 0, 0)) for s in shapes],
            ),
            out_shape=shapes,
            compiler_params=params(60),
            name="key_part",
            cost_estimate=cost(
                6 * half * rows * head_size * (feat_half + feat_size),
                half * rows * (2 * head_size + 2 * feat_size),
                half * rows * feat_size,
            ),
        )(first, keys, key_map, values)

    columns = pl.BlockSpec((rows, head_size), lambda i, first: (0, first[0] * half + i))
    maps = pl.BlockSpec((1, head_size, feat_half), lambda i, first: (first[0] * half + i, 0, 0))
    query_shapes = [of(half, rows, feat_size), of(half, rows, head_size), of(half, rows, head_size)]
    query_specs = [head_block(*shape.shape[1:]) for shape in query_shapes]

    def own_part(first):
        outs = pl.pallas_call(
            own_kernel,
            grid_spec=pltpu.PrefetchScalarGridSpec(
                num_scalar_prefetch=1,
                grid=(half,),
                in_specs=[columns, maps, columns, maps, columns],
                out_specs=[head_block(feat_size + EXTRA, head_size), *query_specs],
            ),
            out_shape=[of(half, feat_size + EXTRA, head_size), *query_shapes],
            compiler_params=params(48),
            name="own_part",
            cost_estimate=cost(
                6 * half * rows * (head_size * (2 * feat_half + feat_size) + rows * (feat_size + head_size)),
                half * rows * (5 * head_size + 3 * feat_size),
                2 * half * rows * feat_size,
            ),
        )(first, keys, key_map, queries, query_map, values)
        return outs[0], outs[1:]

    def query_part(first, key_feat):
        return pl.pallas_call(
            query_kernel,
            grid_spec=pltpu.PrefetchScalarGridSpec(
                num_scalar_prefetch=1,
                grid=(half,),
                in_specs=[columns, maps, columns, head_block(rows, feat_size)],
                out_specs=query_specs,
            ),
            out_shape=query_shapes,
            compiler_params=params(32),
            name="query_part",
            cost_estimate=cost(
                6 * half * rows * (head_size * feat_half + rows * (feat_size + head_size)),
                half * rows * (4 * head_size + 2 * feat_size),
                half * rows * feat_size,
            ),
        )(first, queries, query_map, values, key_feat)

    def mix(qfeat, numer, denom, prior, below=None):
        columns = pl.BlockSpec((rows, head_size), lambda i: (0, i))
        out_specs, shapes = columns, of(rows, wide)
        if below is not None:
            out_specs = [columns, pl.BlockSpec((2 * rows, head_size), lambda i: (0, i))]
            shapes = [shapes, of(2 * rows, wide)]
        return pl.pallas_call(
            mix_kernel,
            grid=(half,),
            in_specs=[
                head_block(rows, feat_size),
                head_block(rows, head_size),
                head_block(rows, head_size),
                head_block(feat_size + EXTRA, head_size),
            ]
            + [columns] * (below is not None),
            out_specs=out_specs,
            out_shape=shapes,
            compiler_params=params(12),
            name="mix",
            cost_estimate=cost(
                3 * half * rows * feat_size * head_size, half * rows * (3 * head_size + 2 * feat_size)
            ),
        )(qfeat, numer, denom, prior, *([] if below is None else [below]))

    even = range(0, heads, 2)
    blocks = heads // 2
    bits = [1 << b for b in reversed(range(ctx.bit_length() - 1)) if 1 << b != PAIR]
    far, near = bits[-2:]
    rels = [0]
    for bit in bits[:-2]:
        rels = rels + [r | bit for r in rels]
    rels = [r | s for s in (0, near, far, far | near) for r in rels]

    def arranged(weight, starts, plan):
        shapes = [of(len(picks) * wide, strip_width) for picks in plan]
        count = sum(len(picks) for picks in plan)
        return pl.pallas_call(
            functools.partial(arrange_kernel, plan, wide),
            grid_spec=pltpu.PrefetchScalarGridSpec(
                num_scalar_prefetch=1,
                grid=(1,),
                in_specs=[pl.BlockSpec(memory_space=pl.ANY)],
                out_specs=[pl.BlockSpec(memory_space=pl.ANY)] * len(plan),
                scratch_shapes=[pltpu.SemaphoreType.DMA((count,))],
            ),
            out_shape=shapes,
            compiler_params=params(12),
            name="arrange",
            cost_estimate=cost(0, 2 * count * wide * strip_width),
        )(starts, weight)

    def widen(x):
        for bit in bits[:-2]:
            x = jnp.concatenate([x, swap(x, bit)], axis=1)
        return x

    order = [(which, d) for which in (0, 1) for d in even]
    part = len(order) // 4
    own = odd ^ np.array([0], np.int32)
    other = odd ^ np.array([1], np.int32)
    other_state, other_feat = key_part(other)
    flags = {1 << b: (c & 1 << b) != 0 for b in range(ctx.bit_length() - 1)}
    out_weight, other_state, flags = together((out_weight, other_state, flags))
    count = len(order)
    head_masks = np.array([flip ^ d for flip in (0, 1) for _, d in order], np.int32)
    half_masks = np.array([which for _ in (0, 1) for which, _ in order], np.int32)
    starts = (h ^ head_masks) * depth + (odd ^ half_masks) * wide
    (first_part,) = arranged(out_weight, starts, [list(range(part))])
    first_part = widen(first_part)
    far_1 = swap(first_part, far)
    from_neighbour = swap(other_state, 1)
    own_state, own_query = own_part(own)
    out_weight, own_state = together((out_weight, own_state))
    spans = [(part, 3 * part), (3 * part, count), (0, count)]
    spans += [(count, count + 2 * part), (count + 2 * part, 2 * count), (count, 2 * count)]
    kept_2, kept_3, kept, given_1, given_2, given = arranged(out_weight, starts, [list(range(*span)) for span in spans])
    kept_2, kept_3, kept = [widen(x) for x in (kept_2, kept_3, kept)]
    groups, perms, send, place = route_tables(ctx, heads, rels)
    steps, size = len(perms), len(groups[0])
    send_here, place_here = [
        lax.dynamic_slice(
            x.reshape(ctx, heads, -1), (c, h, 0), (1, 1, x.shape[1]), allow_negative_indices=False
        ).reshape(-1)
        for x in (send, place)
    ]

    from_neighbour, own_state, far_1, kept_2, kept, given_1, given_2, given = together(
        (from_neighbour, own_state, far_1, kept_2, kept, given_1, given_2, given)
    )
    far_2 = swap(kept_2, far)
    kept_near = swap(kept, near)
    taken, taken_1, taken_2 = [widen(swap(x, 0, 1)) for x in (given, given_1, given_2)]
    earlier = jnp.where(flags[1], from_neighbour, own_state)
    total = own_state + from_neighbour
    parts = []
    bit = 2
    while 2 * bit < ctx:
        if parts:
            total = total + parts[-1]
        parts.append(swap(total, bit))
        bit *= 2
    total, parts, far_2, kept_near, taken, taken_1, taken_2, far_1 = together(
        (total, parts, far_2, kept_near, taken, taken_1, taken_2, far_1)
    )
    taken_near = swap(taken, near)
    both_1 = swap(far_1, near)
    second = flags[PAIR]
    sent = sum(jnp.where(second, x[half // 2 :], x[: half // 2]) for x in (total, *parts[-1:]))
    got = swap(sent, bit, keep=lambda i: not i & bit)
    got, kept_3 = together((got, kept_3))
    met = swap(got, PAIR, keep=lambda i: i & bit)
    far_3 = swap(kept_3, far)
    got = jnp.concatenate([jnp.where(second, met, got), jnp.where(second, got, met)])
    got, taken_near, both_1, taken_1, far_2, other_feat = together(
        (got, taken_near, both_1, taken_1, far_2, other_feat)
    )
    before = got
    for b, part_sum in enumerate(parts):
        before = before + jnp.where(flags[2 << b], part_sum, 0.0)

    other_prior = swap(before + jnp.where(flags[1], 0.0, earlier), 1)
    own_mixed = mix(*own_query, before + jnp.where(flags[1], earlier, 0.0))
    head_bits = [1 << b for b in range(1, heads.bit_length() - 1)]

    def spread(pieces):
        for bit in head_bits[1:]:
            for (d, j), (x, i) in list(pieces.items()):
                pieces[d, j | bit] = (swap(x[i * rows : (i + 1) * rows], 0, bit), 0)
        return [(pieces[0, j], pieces[PAIR, j]) for j in even]

    own_mixed, far_3 = together((own_mixed, far_3))
    met, across = swap(own_mixed, PAIR), swap(own_mixed, 0, head_bits[0])
    far_4 = swap(taken_1, far)
    both_2 = swap(far_2, near)
    other_mixed, both = mix(*query_part(other, other_feat), other_prior, met)
    other_mixed, both, across, far_3, far_4, both_2, taken_2 = together(
        (other_mixed, both, across, far_3, far_4, both_2, taken_2)
    )
    other_met = swap(other_mixed, PAIR)
    both = swap(both, 0, head_bits[0])
    far_5 = swap(taken_2, far)
    both_3 = swap(far_3, near)
    both_4 = swap(far_4, near)
    other_met, both, far_5, both_3, both_4, send_here, place_here = together(
        (other_met, both, far_5, both_3, both_4, send_here, place_here)
    )
    both_5 = swap(far_5, near)
    last = swap(other_met, 0, head_bits[0])
    own_pieces = spread(
        {(0, 0): (own_mixed, 0), (PAIR, 0): (met, 0), (0, head_bits[0]): (across, 0), (PAIR, head_bits[0]): (both, 1)}
    )

    def other_pieces(last):
        pieces = {(0, 0): (other_mixed, 0), (PAIR, 0): (other_met, 0), (0, head_bits[0]): (both, 0)}
        return spread({**pieces, (PAIR, head_bits[0]): (last, 0)})

    lanes = kept.shape[1]

    def strip(parts, crossed=False):
        places = [(x, start * part + i) for x, start, stop in parts for i in range((stop - start) * part)]
        return places[blocks:] + places[:blocks] if crossed else places

    def project(pieces, strips, runs, total=None, column=0):
        runs = [(u, start, stop) for q, start, stop in runs for u in range(q * part, (q + 1) * part)]
        used = sorted({u for u, _, _ in runs})
        weights = [strips[s][u] for u, start, stop in runs for s in range(start, stop)]
        shape = (2 * rows, len(strips) * lanes)
        extra = [] if total is None else [total]
        terms = [(used.index(u), start, stop) for u, start, stop in runs]
        return pl.pallas_call(
            functools.partial(project_kernel, terms, len(used)),
            grid=(1,),
            in_specs=[pl.BlockSpec((rows, wide), lambda i, block=block: (block, 0)) for u in used for _, block in pieces[u]]
            + [pl.BlockSpec((wide, lanes), lambda i, unit=unit: (unit, 0)) for _, unit in weights]
            + [pl.BlockSpec(shape, lambda i: (0, column))] * len(extra),
            out_specs=pl.BlockSpec(shape, lambda i: (0, 0)),
            out_shape=of(*shape),
            compiler_params=params(24),
            name="project",
            cost_estimate=cost(6 * rows * wide * len(weights) * lanes, wide * lanes * len(weights) + 2 * rows * shape[1]),
        )(*[x for u in used for x, _ in pieces[u]], *[x for x, _ in weights], *extra)

    theirs = [
        strip([(taken, 0, 4)]),
        strip([(taken_near, 0, 4)], True),
        strip([(far_4, 0, 2), (far_5, 0, 2)]),
        strip([(both_4, 0, 2), (both_5, 0, 2)], True),
    ]
    mine = [
        strip([(kept, 0, 4)]),
        strip([(kept_near, 0, 4)], True),
        strip([(far_1, 0, 1), (far_2, 0, 2), (far_3, 0, 1)]),
        strip([(both_1, 0, 1), (both_2, 0, 2), (both_3, 0, 1)], True),
    ]
    pieces = own_pieces + other_pieces(last)
    product = project(pieces, theirs + mine, [(0, 0, 3), (0, 4, 8), (1, 0, 3), (1, 4, 8)])
    product = project(pieces, theirs + mine, [(2, 0, 8)], product)
    product, last = together((product, last))
    pieces = own_pieces + other_pieces(last)
    from_them = swap(project(pieces, theirs, [(3, 0, 4), (0, 3, 4), (1, 3, 4)], product, 0), 0, 1)
    product = project(pieces, mine, [(3, 0, 4)], product, 1)

    if strip_width % 128 == 0:
        parts = pl.pallas_call(
            functools.partial(route_kernel, groups, strip_width),
            grid_spec=pltpu.PrefetchScalarGridSpec(
                num_scalar_prefetch=1,
                grid=(1,),
                in_specs=[pl.BlockSpec(x.shape, lambda i, send: (0, 0)) for x in (product, from_them)],
                out_specs=[pl.BlockSpec((rows, size * strip_width), lambda i, send: (0, 0))] * steps,
                scratch_shapes=[pltpu.VMEM((steps, rows, size * strip_width), jnp.float32)],
            ),
            out_shape=[of(rows, size * strip_width)] * steps,
            compiler_params=params(12),
            name="route",
            cost_estimate=cost(0, 6 * rows * steps * size * strip_width),
        )(send_here, product, from_them)
    else:
        parts = jnp.stack(pieces_of(product + from_them, groups, strip_width))
        parts = [lax.dynamic_index_in_dim(parts, send_here[k], 0, False) for k in range(steps)]
    arrived = [lax.ppermute(part, AXES, perm) for part, perm in zip(parts, perms)]
    if strip_width % 128 == 0:
        return pl.pallas_call(
            functools.partial(assemble_kernel, size),
            grid_spec=pltpu.PrefetchScalarGridSpec(
                num_scalar_prefetch=1,
                grid=(1,),
                in_specs=[pl.BlockSpec(x.shape, lambda i, place: (0, 0)) for x in (*arrived, residual)],
                out_specs=pl.BlockSpec(residual.shape, lambda i, place: (0, 0)),
                scratch_shapes=[pltpu.VMEM((ctx, rows, strip_width), jnp.float32)],
            ),
            out_shape=of(*residual.shape),
            compiler_params=params(12),
            name="assemble",
            cost_estimate=cost(0, 3 * residual.size),
        )(place_here, *arrived, residual)
    blocks = jnp.stack([a[:, b * strip_width : (b + 1) * strip_width] for a in arrived for b in range(size)])
    projected = [lax.dynamic_index_in_dim(blocks, place_here[p], 0, False) for p in range(ctx)]
    return residual + jnp.concatenate(projected, axis=1)


def solution(mesh):
    placed = (
        P("ctx", "head"),
        P("ctx", "head"),
        P("ctx", "head"),
        P("head", None, None),
        P("head", None, None),
        P(None, ("ctx", "head")),
        P("ctx", "head"),
    )
    return jax.shard_map(
        functools.partial(body, mesh.shape["ctx"], mesh.shape["head"]),
        mesh=mesh,
        in_specs=placed,
        out_specs=P("ctx", "head"),
        check_vma=False,
    )
```

```python
import functools

import numpy as np

import jax
import jax.numpy as jnp
from jax import lax
from jax.experimental import pallas as pl
from jax.experimental.pallas import tpu as pltpu
from jax.sharding import PartitionSpec as P

HIGH = lax.Precision.HIGHEST
together = lax.optimization_barrier
AXES = ("ctx", "head")
PAIR = 2
EXTRA = 8
MIB = 1024 * 1024


def split(x):
    high = x.astype(jnp.bfloat16)
    return high, (x - high.astype(jnp.float32)).astype(jnp.bfloat16)


def dot3(a, b, dims=(((1,), (0,)), ((), ()))):
    a_high, a_low = split(a)
    b_high, b_low = split(b)
    dot = functools.partial(lax.dot_general, dimension_numbers=dims, preferred_element_type=jnp.float32)
    return dot(a_high, b_high) + (dot(a_high, b_low) + dot(a_low, b_high))


def features(rows, weights):
    scores = jnp.dot(rows, weights, precision=HIGH, preferred_element_type=jnp.float32)
    up = jnp.exp(scores - jnp.max(scores, axis=-1, keepdims=True))
    down = jnp.exp(jnp.min(scores, axis=-1, keepdims=True) - scores)
    up = up / jnp.sum(up, axis=-1, keepdims=True)
    down = down / jnp.sum(down, axis=-1, keepdims=True)
    return jnp.concatenate([up, down], axis=-1)


def arrange_kernel(plan, wide, starts, weight_ref, *refs):
    out_refs, sems = refs[:-1], refs[-1]
    copies = []
    for out_ref, picks in zip(out_refs, plan):
        for i, pick in enumerate(picks):
            source = weight_ref.at[pl.ds(pl.multiple_of(starts[pick], wide), wide), :]
            copies.append(pltpu.make_async_copy(source, out_ref.at[pl.ds(i * wide, wide), :], sems.at[len(copies)]))
            copies[-1].start()
    for copy in copies:
        copy.wait()


def key_kernel(first, k_ref, map_ref, v_ref, state_ref, feat_ref):
    heads, head_size, feat_half = map_ref.shape
    size = 2 * feat_half
    row = lax.broadcasted_iota(jnp.int32, (EXTRA, feat_half), 0)
    for i in range(heads):
        columns = slice(i * head_size, (i + 1) * head_size)
        feat = features(k_ref[:, columns], map_ref[i])
        feat_ref[i] = feat
        state_ref[i, :size, :] = dot3(feat, v_ref[:, columns], (((0,), (0,)), ((), ())))
        norm = jnp.sum(feat, axis=0, keepdims=True)
        state_ref[i, size:, :] = jnp.where(row < EXTRA // 2, norm[:, :feat_half], norm[:, feat_half:])


def attend(feat, key_feat, values, numer_ref, denom_ref):
    weights = dot3(feat, key_feat, (((1,), (1,)), ((), ())))
    row = lax.broadcasted_iota(jnp.int32, weights.shape, 0)
    column = lax.broadcasted_iota(jnp.int32, weights.shape, 1)
    weights = jnp.where(column <= row, weights, 0.0)
    numer_ref[0] = dot3(weights, values)
    denom_ref[0] = jnp.broadcast_to(jnp.sum(weights, axis=-1, keepdims=True), denom_ref.shape[1:])


def own_kernel(first, k_ref, k_map_ref, q_ref, q_map_ref, v_ref, state_ref, feat_ref, numer_ref, denom_ref):
    feat_half = k_map_ref.shape[2]
    size = 2 * feat_half
    row = lax.broadcasted_iota(jnp.int32, (EXTRA, feat_half), 0)
    key_feat = features(k_ref[...], k_map_ref[0])
    state_ref[0, :size, :] = dot3(key_feat, v_ref[...], (((0,), (0,)), ((), ())))
    norm = jnp.sum(key_feat, axis=0, keepdims=True)
    state_ref[0, size:, :] = jnp.where(row < EXTRA // 2, norm[:, :feat_half], norm[:, feat_half:])
    feat = features(q_ref[...], q_map_ref[0])
    feat_ref[0] = feat
    attend(feat, key_feat, v_ref[...], numer_ref, denom_ref)


def query_kernel(first, q_ref, q_map_ref, v_ref, key_feat_ref, feat_ref, numer_ref, denom_ref):
    feat = features(q_ref[...], q_map_ref[0])
    feat_ref[0] = feat
    attend(feat, key_feat_ref[0], v_ref[...], numer_ref, denom_ref)


def mix_kernel(qfeat_ref, numer_ref, denom_ref, prior_ref, *refs):
    feat = qfeat_ref[0]
    size = feat.shape[1]
    norm = jnp.concatenate(
        [prior_ref[0, size : size + 1, :], prior_ref[0, size + EXTRA // 2 : size + EXTRA // 2 + 1, :]], axis=1
    )
    denom = denom_ref[0] + jnp.sum(feat * norm, axis=-1, keepdims=True)
    mixed = (numer_ref[0] + dot3(feat, prior_ref[0, :size, :])) / denom
    if len(refs) == 1:
        refs[0][...] = mixed
    else:
        below_ref, out_ref, both_ref = refs
        out_ref[...] = mixed
        both_ref[...] = jnp.concatenate([mixed, below_ref[...]], axis=0)


def project_kernel(terms, units, *refs):
    rows_refs, refs = refs[: 2 * units], refs[2 * units :]
    count = sum(stop - start for _, start, stop in terms)
    w_refs, rest, out_ref = refs[:count], refs[count:-1], refs[-1]
    out_ref[...] = rest[0][...] if rest else jnp.zeros_like(out_ref)
    lanes = w_refs[0].shape[1]
    for unit, start, stop in terms:
        a = jnp.concatenate([rows_refs[2 * unit][...], rows_refs[2 * unit + 1][...]], axis=0)
        w = jnp.concatenate([ref[...] for ref in w_refs[: stop - start]], axis=1)
        w_refs = w_refs[stop - start :]
        out_ref[:, start * lanes : stop * lanes] += dot3(a, w)


def pieces_of(product, groups, width):
    rows = product.shape[0] // 2
    return [
        jnp.concatenate([product[d * rows : (d + 1) * rows, b * width : (b + 1) * width] for b in group], axis=1)
        for d in range(2)
        for group in groups
    ]


def route_kernel(groups, width, send, mine_ref, other_ref, *refs):
    out_refs, pieces_ref = refs[:-1], refs[-1]
    product = mine_ref[...] + other_ref[...]
    for j, piece in enumerate(pieces_of(product, groups, width)):
        pieces_ref[j] = piece
    for k, out_ref in enumerate(out_refs):
        out_ref[...] = pieces_ref[send[k]]


def assemble_kernel(size, place, *refs):
    arrived, (residual_ref, out_ref, blocks_ref) = refs[:-3], refs[-3:]
    width = blocks_ref.shape[2]
    for k, ref in enumerate(arrived):
        for b in range(size):
            blocks_ref[k * size + b] = ref[:, b * width : (b + 1) * width]
    for p in range(blocks_ref.shape[0]):
        columns = slice(p * width, (p + 1) * width)
        out_ref[:, columns] = residual_ref[:, columns] + blocks_ref[place[p]]


def route_tables(ctx, heads, rels):
    groups = {}
    for column, rel in enumerate(rels):
        groups.setdefault(rel * heads // ctx, []).append(column)
    groups = [groups[key] for key in sorted(groups)]
    size = len(groups[0])
    targets = {}
    for c in range(ctx):
        for h in range(heads):
            found = {}
            for d, step in enumerate((0, PAIR)):
                for g, columns in enumerate(groups):
                    to = (c ^ step) * heads + (c ^ rels[columns[0]]) * heads // ctx
                    found[to] = d * len(groups) + g
            targets[c * heads + h] = found
    classes = {}

    def turn(device):
        c, h = divmod(device, heads)
        return c, h & 1, (h >> 1) ^ (h & 1)

    for device in sorted(targets, key=turn):
        classes.setdefault(tuple(sorted(targets[device])), []).append(device)
    steps = 2 * len(groups)
    perms = [[] for _ in range(steps)]
    send = np.zeros((ctx * heads, steps), np.int32)
    arrives = {}
    for ends, sources in classes.items():
        for i, source in enumerate(sources):
            for k in range(steps):
                to = ends[i ^ k]
                perms[k].append((source, to))
                send[source, k] = targets[source][to]
                arrives[to, source] = k
    place = np.zeros((ctx * heads, ctx), np.int32)
    for c in range(ctx):
        for h in range(heads):
            for p in range(ctx):
                column_ctx, source_h = divmod(h * ctx + p, heads)
                source_c = (c & ~PAIR) | (column_ctx & PAIR)
                k = arrives[c * heads + h, source_c * heads + source_h]
                rel = source_c ^ column_ctx
                group = [g for g in groups if rels.index(rel) in g][0]
                place[c * heads + h, p] = k * size + group.index(rels.index(rel))
    return groups, perms, send, place


def body(ctx, heads, queries, keys, values, query_map, key_map, out_weight, residual):
    rows = queries.shape[0]
    heads_here, head_size, feat_half = query_map.shape
    feat_size = 2 * feat_half
    half = heads_here // 2
    wide = half * head_size
    depth = out_weight.shape[0] // heads
    strip_width = out_weight.shape[1]
    c = lax.axis_index("ctx")
    h = lax.axis_index("head")
    odd = c & 1

    def swap(x, by_ctx, by_head=0, keep=lambda c: True):
        pairs = [
            (i * heads + j, (i ^ by_ctx) * heads + (j ^ by_head))
            for i in range(ctx)
            for j in range(heads)
            if keep(i)
        ]
        return lax.ppermute(x, AXES, pairs)

    def of(*shape):
        return jax.ShapeDtypeStruct(shape, jnp.float32)

    def cost(products, count, exps=0):
        return pl.CostEstimate(flops=2 * products, bytes_accessed=4 * count, transcendentals=exps)

    def params(mib):
        return pltpu.CompilerParams(vmem_limit_bytes=mib * MIB)

    def head_block(size, lanes):
        return pl.BlockSpec((1, size, lanes), lambda i, *_: (i, 0, 0))

    def key_part(first):
        columns = pl.BlockSpec((rows, wide), lambda i, first: (0, first[0]))
        maps = pl.BlockSpec((half, head_size, feat_half), lambda i, first: (first[0], 0, 0))
        shapes = [of(half, feat_size + EXTRA, head_size), of(half, rows, feat_size)]
        return pl.pallas_call(
            key_kernel,
            grid_spec=pltpu.PrefetchScalarGridSpec(
                num_scalar_prefetch=1,
                grid=(1,),
                in_specs=[columns, maps, columns],
                out_specs=[pl.BlockSpec(s.shape, lambda i, first: (0, 0, 0)) for s in shapes],
            ),
            out_shape=shapes,
            compiler_params=params(60),
            name="key_part",
            cost_estimate=cost(
                6 * half * rows * head_size * (feat_half + feat_size),
                half * rows * (2 * head_size + 2 * feat_size),
                half * rows * feat_size,
            ),
        )(first, keys, key_map, values)

    columns = pl.BlockSpec((rows, head_size), lambda i, first: (0, first[0] * half + i))
    maps = pl.BlockSpec((1, head_size, feat_half), lambda i, first: (first[0] * half + i, 0, 0))
    query_shapes = [of(half, rows, feat_size), of(half, rows, head_size), of(half, rows, head_size)]
    query_specs = [head_block(*shape.shape[1:]) for shape in query_shapes]

    def own_part(first):
        outs = pl.pallas_call(
            own_kernel,
            grid_spec=pltpu.PrefetchScalarGridSpec(
                num_scalar_prefetch=1,
                grid=(half,),
                in_specs=[columns, maps, columns, maps, columns],
                out_specs=[head_block(feat_size + EXTRA, head_size), *query_specs],
            ),
            out_shape=[of(half, feat_size + EXTRA, head_size), *query_shapes],
            compiler_params=params(48),
            name="own_part",
            cost_estimate=cost(
                6 * half * rows * (head_size * (2 * feat_half + feat_size) + rows * (feat_size + head_size)),
                half * rows * (5 * head_size + 3 * feat_size),
                2 * half * rows * feat_size,
            ),
        )(first, keys, key_map, queries, query_map, values)
        return outs[0], outs[1:]

    def query_part(first, key_feat):
        return pl.pallas_call(
            query_kernel,
            grid_spec=pltpu.PrefetchScalarGridSpec(
                num_scalar_prefetch=1,
                grid=(half,),
                in_specs=[columns, maps, columns, head_block(rows, feat_size)],
                out_specs=query_specs,
            ),
            out_shape=query_shapes,
            compiler_params=params(32),
            name="query_part",
            cost_estimate=cost(
                6 * half * rows * (head_size * feat_half + rows * (feat_size + head_size)),
                half * rows * (4 * head_size + 2 * feat_size),
                half * rows * feat_size,
            ),
        )(first, queries, query_map, values, key_feat)

    def mix(qfeat, numer, denom, prior, below=None):
        columns = pl.BlockSpec((rows, head_size), lambda i: (0, i))
        out_specs, shapes = columns, of(rows, wide)
        if below is not None:
            out_specs = [columns, pl.BlockSpec((2 * rows, head_size), lambda i: (0, i))]
            shapes = [shapes, of(2 * rows, wide)]
        return pl.pallas_call(
            mix_kernel,
            grid=(half,),
            in_specs=[
                head_block(rows, feat_size),
                head_block(rows, head_size),
                head_block(rows, head_size),
                head_block(feat_size + EXTRA, head_size),
            ]
            + [columns] * (below is not None),
            out_specs=out_specs,
            out_shape=shapes,
            compiler_params=params(12),
            name="mix",
            cost_estimate=cost(
                3 * half * rows * feat_size * head_size, half * rows * (3 * head_size + 2 * feat_size)
            ),
        )(qfeat, numer, denom, prior, *([] if below is None else [below]))

    even = range(0, heads, 2)
    blocks = heads // 2
    bits = [1 << b for b in reversed(range(ctx.bit_length() - 1)) if 1 << b != PAIR]
    far, near = bits[-2:]
    rels = [0]
    for bit in bits[:-2]:
        rels = rels + [r | bit for r in rels]
    rels = [r | s for s in (0, near, far, far | near) for r in rels]

    def arranged(weight, starts, plan):
        shapes = [of(len(picks) * wide, strip_width) for picks in plan]
        count = sum(len(picks) for picks in plan)
        return pl.pallas_call(
            functools.partial(arrange_kernel, plan, wide),
            grid_spec=pltpu.PrefetchScalarGridSpec(
                num_scalar_prefetch=1,
                grid=(1,),
                in_specs=[pl.BlockSpec(memory_space=pl.ANY)],
                out_specs=[pl.BlockSpec(memory_space=pl.ANY)] * len(plan),
                scratch_shapes=[pltpu.SemaphoreType.DMA((count,))],
            ),
            out_shape=shapes,
            compiler_params=params(12),
            name="arrange",
            cost_estimate=cost(0, 2 * count * wide * strip_width),
        )(starts, weight)

    def widen(x):
        for bit in bits[:-2]:
            x = jnp.concatenate([x, swap(x, bit)], axis=1)
        return x

    order = [(which, d) for which in (0, 1) for d in even]
    part = len(order) // 4
    own = odd ^ np.array([0], np.int32)
    other = odd ^ np.array([1], np.int32)
    other_state, other_feat = key_part(other)
    flags = {1 << b: (c & 1 << b) != 0 for b in range(ctx.bit_length() - 1)}
    out_weight, other_state, flags = together((out_weight, other_state, flags))
    count = len(order)
    head_masks = np.array([flip ^ d for flip in (0, 1) for _, d in order], np.int32)
    half_masks = np.array([which for _ in (0, 1) for which, _ in order], np.int32)
    starts = (h ^ head_masks) * depth + (odd ^ half_masks) * wide
    (first_part,) = arranged(out_weight, starts, [list(range(part))])
    first_part = widen(first_part)
    far_1 = swap(first_part, far)
    from_neighbour = swap(other_state, 1)
    own_state, own_query = own_part(own)
    out_weight, own_state = together((out_weight, own_state))
    spans = [(part, 3 * part), (3 * part, count), (0, count)]
    spans += [(count, count + 2 * part), (count + 2 * part, 2 * count), (count, 2 * count)]
    kept_2, kept_3, kept, given_1, given_2, given = arranged(out_weight, starts, [list(range(*span)) for span in spans])
    kept_2, kept_3, kept = [widen(x) for x in (kept_2, kept_3, kept)]
    groups, perms, send, place = route_tables(ctx, heads, rels)
    steps, size = len(perms), len(groups[0])
    send_here, place_here = [
        lax.dynamic_slice(
            x.reshape(ctx, heads, -1), (c, h, 0), (1, 1, x.shape[1]), allow_negative_indices=False
        ).reshape(-1)
        for x in (send, place)
    ]

    from_neighbour, own_state, far_1, kept_2, kept, given_1, given_2, given = together(
        (from_neighbour, own_state, far_1, kept_2, kept, given_1, given_2, given)
    )
    far_2 = swap(kept_2, far)
    kept_near = swap(kept, near)
    taken, taken_1, taken_2 = [widen(swap(x, 0, 1)) for x in (given, given_1, given_2)]
    earlier = jnp.where(flags[1], from_neighbour, own_state)
    total = own_state + from_neighbour
    parts = []
    bit = 2
    while 2 * bit < ctx:
        if parts:
            total = total + parts[-1]
        parts.append(swap(total, bit))
        bit *= 2
    total, parts, far_2, kept_near, taken, taken_1, taken_2, far_1 = together(
        (total, parts, far_2, kept_near, taken, taken_1, taken_2, far_1)
    )
    taken_near = swap(taken, near)
    both_1 = swap(far_1, near)
    second = flags[PAIR]
    sent = sum(jnp.where(second, x[half // 2 :], x[: half // 2]) for x in (total, *parts[-1:]))
    got = swap(sent, bit, keep=lambda i: not i & bit)
    got, taken_1 = together((got, taken_1))
    met = swap(got, PAIR, keep=lambda i: i & bit)
    far_4 = swap(taken_1, far)
    got = jnp.concatenate([jnp.where(second, met, got), jnp.where(second, got, met)])
    got, taken_near, both_1, kept_3, far_2, other_feat = together(
        (got, taken_near, both_1, kept_3, far_2, other_feat)
    )
    before = got
    for b, part_sum in enumerate(parts):
        before = before + jnp.where(flags[2 << b], part_sum, 0.0)

    other_prior = swap(before + jnp.where(flags[1], 0.0, earlier), 1)
    own_mixed = mix(*own_query, before + jnp.where(flags[1], earlier, 0.0))
    head_bits = [1 << b for b in range(1, heads.bit_length() - 1)]

    def spread(pieces):
        for bit in head_bits[1:]:
            for (d, j), (x, i) in list(pieces.items()):
                pieces[d, j | bit] = (swap(x[i * rows : (i + 1) * rows], 0, bit), 0)
        return [(pieces[0, j], pieces[PAIR, j]) for j in even]

    own_mixed, far_4 = together((own_mixed, far_4))
    met, across = swap(own_mixed, PAIR), swap(own_mixed, 0, head_bits[0])
    far_3 = swap(kept_3, far)
    both_2 = swap(far_2, near)
    other_mixed, both = mix(*query_part(other, other_feat), other_prior, met)
    other_mixed, both, across, far_3, far_4, both_2, taken_2 = together(
        (other_mixed, both, across, far_3, far_4, both_2, taken_2)
    )
    other_met = swap(other_mixed, PAIR)
    both = swap(both, 0, head_bits[0])
    far_5 = swap(taken_2, far)
    both_3 = swap(far_3, near)
    both_4 = swap(far_4, near)
    other_met, both, far_5, both_3, both_4, send_here, place_here = together(
        (other_met, both, far_5, both_3, both_4, send_here, place_here)
    )
    both_5 = swap(far_5, near)
    last = swap(other_met, 0, head_bits[0])
    own_pieces = spread(
        {(0, 0): (own_mixed, 0), (PAIR, 0): (met, 0), (0, head_bits[0]): (across, 0), (PAIR, head_bits[0]): (both, 1)}
    )

    def other_pieces(last):
        pieces = {(0, 0): (other_mixed, 0), (PAIR, 0): (other_met, 0), (0, head_bits[0]): (both, 0)}
        return spread({**pieces, (PAIR, head_bits[0]): (last, 0)})

    lanes = kept.shape[1]

    def strip(parts, crossed=False):
        places = [(x, start * part + i) for x, start, stop in parts for i in range((stop - start) * part)]
        return places[blocks:] + places[:blocks] if crossed else places

    def project(pieces, strips, runs, total=None, column=0):
        runs = [(u, start, stop) for q, start, stop in runs for u in range(q * part, (q + 1) * part)]
        used = sorted({u for u, _, _ in runs})
        weights = [strips[s][u] for u, start, stop in runs for s in range(start, stop)]
        shape = (2 * rows, len(strips) * lanes)
        extra = [] if total is None else [total]
        terms = [(used.index(u), start, stop) for u, start, stop in runs]
        return pl.pallas_call(
            functools.partial(project_kernel, terms, len(used)),
            grid=(1,),
            in_specs=[pl.BlockSpec((rows, wide), lambda i, block=block: (block, 0)) for u in used for _, block in pieces[u]]
            + [pl.BlockSpec((wide, lanes), lambda i, unit=unit: (unit, 0)) for _, unit in weights]
            + [pl.BlockSpec(shape, lambda i: (0, column))] * len(extra),
            out_specs=pl.BlockSpec(shape, lambda i: (0, 0)),
            out_shape=of(*shape),
            compiler_params=params(24),
            name="project",
            cost_estimate=cost(6 * rows * wide * len(weights) * lanes, wide * lanes * len(weights) + 2 * rows * shape[1]),
        )(*[x for u in used for x, _ in pieces[u]], *[x for x, _ in weights], *extra)

    theirs = [
        strip([(taken, 0, 4)]),
        strip([(taken_near, 0, 4)], True),
        strip([(far_4, 0, 2), (far_5, 0, 2)]),
        strip([(both_4, 0, 2), (both_5, 0, 2)], True),
    ]
    mine = [
        strip([(kept, 0, 4)]),
        strip([(kept_near, 0, 4)], True),
        strip([(far_1, 0, 1), (far_2, 0, 2), (far_3, 0, 1)]),
        strip([(both_1, 0, 1), (both_2, 0, 2), (both_3, 0, 1)], True),
    ]
    pieces = own_pieces + other_pieces(last)
    product = project(pieces, theirs + mine, [(0, 0, 3), (0, 4, 8), (1, 0, 3), (1, 4, 8)])
    product = project(pieces, theirs + mine, [(2, 0, 8)], product)
    product, last = together((product, last))
    pieces = own_pieces + other_pieces(last)
    from_them = swap(project(pieces, theirs, [(3, 0, 4), (0, 3, 4), (1, 3, 4)], product, 0), 0, 1)
    product = project(pieces, mine, [(3, 0, 4)], product, 1)

    if strip_width % 128 == 0:
        parts = pl.pallas_call(
            functools.partial(route_kernel, groups, strip_width),
            grid_spec=pltpu.PrefetchScalarGridSpec(
                num_scalar_prefetch=1,
                grid=(1,),
                in_specs=[pl.BlockSpec(x.shape, lambda i, send: (0, 0)) for x in (product, from_them)],
                out_specs=[pl.BlockSpec((rows, size * strip_width), lambda i, send: (0, 0))] * steps,
                scratch_shapes=[pltpu.VMEM((steps, rows, size * strip_width), jnp.float32)],
            ),
            out_shape=[of(rows, size * strip_width)] * steps,
            compiler_params=params(12),
            name="route",
            cost_estimate=cost(0, 6 * rows * steps * size * strip_width),
        )(send_here, product, from_them)
    else:
        parts = jnp.stack(pieces_of(product + from_them, groups, strip_width))
        parts = [lax.dynamic_index_in_dim(parts, send_here[k], 0, False) for k in range(steps)]
    arrived = [lax.ppermute(part, AXES, perm) for part, perm in zip(parts, perms)]
    if strip_width % 128 == 0:
        return pl.pallas_call(
            functools.partial(assemble_kernel, size),
            grid_spec=pltpu.PrefetchScalarGridSpec(
                num_scalar_prefetch=1,
                grid=(1,),
                in_specs=[pl.BlockSpec(x.shape, lambda i, place: (0, 0)) for x in (*arrived, residual)],
                out_specs=pl.BlockSpec(residual.shape, lambda i, place: (0, 0)),
                scratch_shapes=[pltpu.VMEM((ctx, rows, strip_width), jnp.float32)],
            ),
            out_shape=of(*residual.shape),
            compiler_params=params(12),
            name="assemble",
            cost_estimate=cost(0, 3 * residual.size),
        )(place_here, *arrived, residual)
    blocks = jnp.stack([a[:, b * strip_width : (b + 1) * strip_width] for a in arrived for b in range(size)])
    projected = [lax.dynamic_index_in_dim(blocks, place_here[p], 0, False) for p in range(ctx)]
    return residual + jnp.concatenate(projected, axis=1)


def solution(mesh):
    placed = (
        P("ctx", "head"),
        P("ctx", "head"),
        P("ctx", "head"),
        P("head", None, None),
        P("head", None, None),
        P(None, ("ctx", "head")),
        P("ctx", "head"),
    )
    return jax.shard_map(
        functools.partial(body, mesh.shape["ctx"], mesh.shape["head"]),
        mesh=mesh,
        in_specs=placed,
        out_specs=P("ctx", "head"),
        check_vma=False,
    )
```

```python
import functools

import numpy as np

import jax
import jax.numpy as jnp
from jax import lax
from jax.experimental import pallas as pl
from jax.experimental.pallas import tpu as pltpu
from jax.sharding import PartitionSpec as P

HIGH = lax.Precision.HIGHEST
together = lax.optimization_barrier
AXES = ("ctx", "head")
PAIR = 2
EXTRA = 8
MIB = 1024 * 1024


def split(x):
    high = x.astype(jnp.bfloat16)
    return high, (x - high.astype(jnp.float32)).astype(jnp.bfloat16)


def dot3(a, b, dims=(((1,), (0,)), ((), ()))):
    a_high, a_low = split(a)
    b_high, b_low = split(b)
    dot = functools.partial(lax.dot_general, dimension_numbers=dims, preferred_element_type=jnp.float32)
    return dot(a_high, b_high) + (dot(a_high, b_low) + dot(a_low, b_high))


def features(rows, weights):
    scores = jnp.dot(rows, weights, precision=HIGH, preferred_element_type=jnp.float32)
    up = jnp.exp(scores - jnp.max(scores, axis=-1, keepdims=True))
    down = jnp.exp(jnp.min(scores, axis=-1, keepdims=True) - scores)
    up = up / jnp.sum(up, axis=-1, keepdims=True)
    down = down / jnp.sum(down, axis=-1, keepdims=True)
    return jnp.concatenate([up, down], axis=-1)


def arrange_kernel(plan, wide, starts, weight_ref, *refs):
    out_refs, sems = refs[:-1], refs[-1]
    copies = []
    for out_ref, picks in zip(out_refs, plan):
        for i, pick in enumerate(picks):
            source = weight_ref.at[pl.ds(pl.multiple_of(starts[pick], wide), wide), :]
            copies.append(pltpu.make_async_copy(source, out_ref.at[pl.ds(i * wide, wide), :], sems.at[len(copies)]))
            copies[-1].start()
    for copy in copies:
        copy.wait()


def key_kernel(first, k_ref, map_ref, v_ref, state_ref, feat_ref):
    heads, head_size, feat_half = map_ref.shape
    size = 2 * feat_half
    row = lax.broadcasted_iota(jnp.int32, (EXTRA, feat_half), 0)
    for i in range(heads):
        columns = slice(i * head_size, (i + 1) * head_size)
        feat = features(k_ref[:, columns], map_ref[i])
        feat_ref[i] = feat
        state_ref[i, :size, :] = dot3(feat, v_ref[:, columns], (((0,), (0,)), ((), ())))
        norm = jnp.sum(feat, axis=0, keepdims=True)
        state_ref[i, size:, :] = jnp.where(row < EXTRA // 2, norm[:, :feat_half], norm[:, feat_half:])


def attend(feat, key_feat, values, numer_ref, denom_ref):
    weights = dot3(feat, key_feat, (((1,), (1,)), ((), ())))
    row = lax.broadcasted_iota(jnp.int32, weights.shape, 0)
    column = lax.broadcasted_iota(jnp.int32, weights.shape, 1)
    weights = jnp.where(column <= row, weights, 0.0)
    numer_ref[0] = dot3(weights, values)
    denom_ref[0] = jnp.broadcast_to(jnp.sum(weights, axis=-1, keepdims=True), denom_ref.shape[1:])


def own_kernel(first, k_ref, k_map_ref, q_ref, q_map_ref, v_ref, state_ref, feat_ref, numer_ref, denom_ref):
    feat_half = k_map_ref.shape[2]
    size = 2 * feat_half
    row = lax.broadcasted_iota(jnp.int32, (EXTRA, feat_half), 0)
    key_feat = features(k_ref[...], k_map_ref[0])
    state_ref[0, :size, :] = dot3(key_feat, v_ref[...], (((0,), (0,)), ((), ())))
    norm = jnp.sum(key_feat, axis=0, keepdims=True)
    state_ref[0, size:, :] = jnp.where(row < EXTRA // 2, norm[:, :feat_half], norm[:, feat_half:])
    feat = features(q_ref[...], q_map_ref[0])
    feat_ref[0] = feat
    attend(feat, key_feat, v_ref[...], numer_ref, denom_ref)


def query_kernel(first, q_ref, q_map_ref, v_ref, key_feat_ref, feat_ref, numer_ref, denom_ref):
    feat = features(q_ref[...], q_map_ref[0])
    feat_ref[0] = feat
    attend(feat, key_feat_ref[0], v_ref[...], numer_ref, denom_ref)


def mix_kernel(qfeat_ref, numer_ref, denom_ref, prior_ref, *refs):
    feat = qfeat_ref[0]
    size = feat.shape[1]
    norm = jnp.concatenate(
        [prior_ref[0, size : size + 1, :], prior_ref[0, size + EXTRA // 2 : size + EXTRA // 2 + 1, :]], axis=1
    )
    denom = denom_ref[0] + jnp.sum(feat * norm, axis=-1, keepdims=True)
    mixed = (numer_ref[0] + dot3(feat, prior_ref[0, :size, :])) / denom
    if len(refs) == 1:
        refs[0][...] = mixed
    else:
        below_ref, out_ref, both_ref = refs
        out_ref[...] = mixed
        both_ref[...] = jnp.concatenate([mixed, below_ref[...]], axis=0)


def project_kernel(terms, units, *refs):
    rows_refs, refs = refs[: 2 * units], refs[2 * units :]
    count = sum(stop - start for _, start, stop in terms)
    w_refs, rest, out_ref = refs[:count], refs[count:-1], refs[-1]
    out_ref[...] = rest[0][...] if rest else jnp.zeros_like(out_ref)
    lanes = w_refs[0].shape[1]
    for unit, start, stop in terms:
        a = jnp.concatenate([rows_refs[2 * unit][...], rows_refs[2 * unit + 1][...]], axis=0)
        w = jnp.concatenate([ref[...] for ref in w_refs[: stop - start]], axis=1)
        w_refs = w_refs[stop - start :]
        out_ref[:, start * lanes : stop * lanes] += dot3(a, w)


def pieces_of(product, groups, width):
    rows = product.shape[0] // 2
    return [
        jnp.concatenate([product[d * rows : (d + 1) * rows, b * width : (b + 1) * width] for b in group], axis=1)
        for d in range(2)
        for group in groups
    ]


def route_kernel(groups, width, send, mine_ref, other_ref, *refs):
    out_refs, pieces_ref = refs[:-1], refs[-1]
    product = mine_ref[...] + other_ref[...]
    for j, piece in enumerate(pieces_of(product, groups, width)):
        pieces_ref[j] = piece
    for k, out_ref in enumerate(out_refs):
        out_ref[...] = pieces_ref[send[k]]


def assemble_kernel(size, place, *refs):
    arrived, (residual_ref, out_ref, blocks_ref) = refs[:-3], refs[-3:]
    width = blocks_ref.shape[2]
    for k, ref in enumerate(arrived):
        for b in range(size):
            blocks_ref[k * size + b] = ref[:, b * width : (b + 1) * width]
    for p in range(blocks_ref.shape[0]):
        columns = slice(p * width, (p + 1) * width)
        out_ref[:, columns] = residual_ref[:, columns] + blocks_ref[place[p]]


def route_tables(ctx, heads, rels):
    groups = {}
    for column, rel in enumerate(rels):
        groups.setdefault(rel * heads // ctx, []).append(column)
    groups = [groups[key] for key in sorted(groups)]
    size = len(groups[0])
    targets = {}
    for c in range(ctx):
        for h in range(heads):
            found = {}
            for d, step in enumerate((0, PAIR)):
                for g, columns in enumerate(groups):
                    to = (c ^ step) * heads + (c ^ rels[columns[0]]) * heads // ctx
                    found[to] = d * len(groups) + g
            targets[c * heads + h] = found
    classes = {}

    def turn(device):
        c, h = divmod(device, heads)
        return c, h & 1, (h >> 1) ^ (h & 1)

    for device in sorted(targets, key=turn):
        classes.setdefault(tuple(sorted(targets[device])), []).append(device)
    steps = 2 * len(groups)
    perms = [[] for _ in range(steps)]
    send = np.zeros((ctx * heads, steps), np.int32)
    arrives = {}
    for ends, sources in classes.items():
        for i, source in enumerate(sources):
            for k in range(steps):
                to = ends[i ^ k]
                perms[k].append((source, to))
                send[source, k] = targets[source][to]
                arrives[to, source] = k
    place = np.zeros((ctx * heads, ctx), np.int32)
    for c in range(ctx):
        for h in range(heads):
            for p in range(ctx):
                column_ctx, source_h = divmod(h * ctx + p, heads)
                source_c = (c & ~PAIR) | (column_ctx & PAIR)
                k = arrives[c * heads + h, source_c * heads + source_h]
                rel = source_c ^ column_ctx
                group = [g for g in groups if rels.index(rel) in g][0]
                place[c * heads + h, p] = k * size + group.index(rels.index(rel))
    return groups, perms, send, place


def body(ctx, heads, queries, keys, values, query_map, key_map, out_weight, residual):
    rows = queries.shape[0]
    heads_here, head_size, feat_half = query_map.shape
    feat_size = 2 * feat_half
    half = heads_here // 2
    wide = half * head_size
    depth = out_weight.shape[0] // heads
    strip_width = out_weight.shape[1]
    c = lax.axis_index("ctx")
    h = lax.axis_index("head")
    odd = c & 1

    def swap(x, by_ctx, by_head=0, keep=lambda c: True):
        pairs = [
            (i * heads + j, (i ^ by_ctx) * heads + (j ^ by_head))
            for i in range(ctx)
            for j in range(heads)
            if keep(i)
        ]
        return lax.ppermute(x, AXES, pairs)

    def of(*shape):
        return jax.ShapeDtypeStruct(shape, jnp.float32)

    def cost(products, count, exps=0):
        return pl.CostEstimate(flops=2 * products, bytes_accessed=4 * count, transcendentals=exps)

    def params(mib):
        return pltpu.CompilerParams(vmem_limit_bytes=mib * MIB)

    def head_block(size, lanes):
        return pl.BlockSpec((1, size, lanes), lambda i, *_: (i, 0, 0))

    def key_part(first):
        columns = pl.BlockSpec((rows, wide // 2), lambda i, first: (0, 2 * first[0] + i))
        maps = pl.BlockSpec((half // 2, head_size, feat_half), lambda i, first: (2 * first[0] + i, 0, 0))
        shapes = [of(half, feat_size + EXTRA, head_size), of(half, rows, feat_size)]
        return pl.pallas_call(
            key_kernel,
            grid_spec=pltpu.PrefetchScalarGridSpec(
                num_scalar_prefetch=1,
                grid=(2,),
                in_specs=[columns, maps, columns],
                out_specs=[pl.BlockSpec((half // 2, *s.shape[1:]), lambda i, first: (i, 0, 0)) for s in shapes],
            ),
            out_shape=shapes,
            compiler_params=params(60),
            name="key_part",
            cost_estimate=cost(
                6 * half * rows * head_size * (feat_half + feat_size),
                half * rows * (2 * head_size + 2 * feat_size),
                half * rows * feat_size,
            ),
        )(first, keys, key_map, values)

    columns = pl.BlockSpec((rows, head_size), lambda i, first: (0, first[0] * half + i))
    maps = pl.BlockSpec((1, head_size, feat_half), lambda i, first: (first[0] * half + i, 0, 0))
    query_shapes = [of(half, rows, feat_size), of(half, rows, head_size), of(half, rows, head_size)]
    query_specs = [head_block(*shape.shape[1:]) for shape in query_shapes]

    def own_part(first):
        outs = pl.pallas_call(
            own_kernel,
            grid_spec=pltpu.PrefetchScalarGridSpec(
                num_scalar_prefetch=1,
                grid=(half,),
                in_specs=[columns, maps, columns, maps, columns],
                out_specs=[head_block(feat_size + EXTRA, head_size), *query_specs],
            ),
            out_shape=[of(half, feat_size + EXTRA, head_size), *query_shapes],
            compiler_params=params(48),
            name="own_part",
            cost_estimate=cost(
                6 * half * rows * (head_size * (2 * feat_half + feat_size) + rows * (feat_size + head_size)),
                half * rows * (5 * head_size + 3 * feat_size),
                2 * half * rows * feat_size,
            ),
        )(first, keys, key_map, queries, query_map, values)
        return outs[0], outs[1:]

    def query_part(first, key_feat):
        return pl.pallas_call(
            query_kernel,
            grid_spec=pltpu.PrefetchScalarGridSpec(
                num_scalar_prefetch=1,
                grid=(half,),
                in_specs=[columns, maps, columns, head_block(rows, feat_size)],
                out_specs=query_specs,
            ),
            out_shape=query_shapes,
            compiler_params=params(32),
            name="query_part",
            cost_estimate=cost(
                6 * half * rows * (head_size * feat_half + rows * (feat_size + head_size)),
                half * rows * (4 * head_size + 2 * feat_size),
                half * rows * feat_size,
            ),
        )(first, queries, query_map, values, key_feat)

    def mix(qfeat, numer, denom, prior, below=None):
        columns = pl.BlockSpec((rows, head_size), lambda i: (0, i))
        out_specs, shapes = columns, of(rows, wide)
        if below is not None:
            out_specs = [columns, pl.BlockSpec((2 * rows, head_size), lambda i: (0, i))]
            shapes = [shapes, of(2 * rows, wide)]
        return pl.pallas_call(
            mix_kernel,
            grid=(half,),
            in_specs=[
                head_block(rows, feat_size),
                head_block(rows, head_size),
                head_block(rows, head_size),
                head_block(feat_size + EXTRA, head_size),
            ]
            + [columns] * (below is not None),
            out_specs=out_specs,
            out_shape=shapes,
            compiler_params=params(12),
            name="mix",
            cost_estimate=cost(
                3 * half * rows * feat_size * head_size, half * rows * (3 * head_size + 2 * feat_size)
            ),
        )(qfeat, numer, denom, prior, *([] if below is None else [below]))

    even = range(0, heads, 2)
    blocks = heads // 2
    bits = [1 << b for b in reversed(range(ctx.bit_length() - 1)) if 1 << b != PAIR]
    far, near = bits[-2:]
    rels = [0]
    for bit in bits[:-2]:
        rels = rels + [r | bit for r in rels]
    rels = [r | s for s in (0, near, far, far | near) for r in rels]

    def arranged(weight, starts, plan):
        shapes = [of(len(picks) * wide, strip_width) for picks in plan]
        count = sum(len(picks) for picks in plan)
        return pl.pallas_call(
            functools.partial(arrange_kernel, plan, wide),
            grid_spec=pltpu.PrefetchScalarGridSpec(
                num_scalar_prefetch=1,
                grid=(1,),
                in_specs=[pl.BlockSpec(memory_space=pl.ANY)],
                out_specs=[pl.BlockSpec(memory_space=pl.ANY)] * len(plan),
                scratch_shapes=[pltpu.SemaphoreType.DMA((count,))],
            ),
            out_shape=shapes,
            compiler_params=params(12),
            name="arrange",
            cost_estimate=cost(0, 2 * count * wide * strip_width),
        )(starts, weight)

    def widen(x):
        for bit in bits[:-2]:
            x = jnp.concatenate([x, swap(x, bit)], axis=1)
        return x

    order = [(which, d) for which in (0, 1) for d in even]
    part = len(order) // 4
    own = odd ^ np.array([0], np.int32)
    other = odd ^ np.array([1], np.int32)
    other_state, other_feat = key_part(other)
    flags = {1 << b: (c & 1 << b) != 0 for b in range(ctx.bit_length() - 1)}
    out_weight, other_state, flags = together((out_weight, other_state, flags))
    count = len(order)
    head_masks = np.array([flip ^ d for flip in (0, 1) for _, d in order], np.int32)
    half_masks = np.array([which for _ in (0, 1) for which, _ in order], np.int32)
    starts = (h ^ head_masks) * depth + (odd ^ half_masks) * wide
    (first_part,) = arranged(out_weight, starts, [list(range(part))])
    first_part = widen(first_part)
    far_1 = swap(first_part, far)
    from_neighbour = swap(other_state, 1)
    own_state, own_query = own_part(own)
    out_weight, own_state = together((out_weight, own_state))
    spans = [(part, 3 * part), (3 * part, count), (0, count)]
    spans += [(count, count + 2 * part), (count + 2 * part, 2 * count), (count, 2 * count)]
    kept_2, kept_3, kept, given_1, given_2, given = arranged(out_weight, starts, [list(range(*span)) for span in spans])
    kept_2, kept_3, kept = [widen(x) for x in (kept_2, kept_3, kept)]
    groups, perms, send, place = route_tables(ctx, heads, rels)
    steps, size = len(perms), len(groups[0])
    send_here, place_here = [
        lax.dynamic_slice(
            x.reshape(ctx, heads, -1), (c, h, 0), (1, 1, x.shape[1]), allow_negative_indices=False
        ).reshape(-1)
        for x in (send, place)
    ]

    from_neighbour, own_state, far_1, kept_2, kept, given_1, given_2, given = together(
        (from_neighbour, own_state, far_1, kept_2, kept, given_1, given_2, given)
    )
    far_2 = swap(kept_2, far)
    kept_near = swap(kept, near)
    taken, taken_1, taken_2 = [widen(swap(x, 0, 1)) for x in (given, given_1, given_2)]
    earlier = jnp.where(flags[1], from_neighbour, own_state)
    total = own_state + from_neighbour
    parts = []
    bit = 2
    while 2 * bit < ctx:
        if parts:
            total = total + parts[-1]
        parts.append(swap(total, bit))
        bit *= 2
    total, parts, far_2, kept_near, taken, taken_1, taken_2, far_1 = together(
        (total, parts, far_2, kept_near, taken, taken_1, taken_2, far_1)
    )
    taken_near = swap(taken, near)
    both_1 = swap(far_1, near)
    second = flags[PAIR]
    sent = sum(jnp.where(second, x[half // 2 :], x[: half // 2]) for x in (total, *parts[-1:]))
    got = swap(sent, bit, keep=lambda i: not i & bit)
    got, kept_3 = together((got, kept_3))
    met = swap(got, PAIR, keep=lambda i: i & bit)
    far_3 = swap(kept_3, far)
    got = jnp.concatenate([jnp.where(second, met, got), jnp.where(second, got, met)])
    got, taken_near, both_1, taken_1, far_2, other_feat = together(
        (got, taken_near, both_1, taken_1, far_2, other_feat)
    )
    before = got
    for b, part_sum in enumerate(parts):
        before = before + jnp.where(flags[2 << b], part_sum, 0.0)

    other_prior = swap(before + jnp.where(flags[1], 0.0, earlier), 1)
    own_mixed = mix(*own_query, before + jnp.where(flags[1], earlier, 0.0))
    head_bits = [1 << b for b in range(1, heads.bit_length() - 1)]

    def spread(pieces):
        for bit in head_bits[1:]:
            for (d, j), (x, i) in list(pieces.items()):
                pieces[d, j | bit] = (swap(x[i * rows : (i + 1) * rows], 0, bit), 0)
        return [(pieces[0, j], pieces[PAIR, j]) for j in even]

    own_mixed, far_3 = together((own_mixed, far_3))
    met, across = swap(own_mixed, PAIR), swap(own_mixed, 0, head_bits[0])
    far_4 = swap(taken_1, far)
    both_2 = swap(far_2, near)
    other_mixed, both = mix(*query_part(other, other_feat), other_prior, met)
    other_mixed, both, across, far_3, far_4, both_2, taken_2 = together(
        (other_mixed, both, across, far_3, far_4, both_2, taken_2)
    )
    other_met = swap(other_mixed, PAIR)
    both = swap(both, 0, head_bits[0])
    far_5 = swap(taken_2, far)
    both_3 = swap(far_3, near)
    both_4 = swap(far_4, near)
    other_met, both, far_5, both_3, both_4, send_here, place_here = together(
        (other_met, both, far_5, both_3, both_4, send_here, place_here)
    )
    both_5 = swap(far_5, near)
    last = swap(other_met, 0, head_bits[0])
    own_pieces = spread(
        {(0, 0): (own_mixed, 0), (PAIR, 0): (met, 0), (0, head_bits[0]): (across, 0), (PAIR, head_bits[0]): (both, 1)}
    )

    def other_pieces(last):
        pieces = {(0, 0): (other_mixed, 0), (PAIR, 0): (other_met, 0), (0, head_bits[0]): (both, 0)}
        return spread({**pieces, (PAIR, head_bits[0]): (last, 0)})

    lanes = kept.shape[1]

    def strip(parts, crossed=False):
        places = [(x, start * part + i) for x, start, stop in parts for i in range((stop - start) * part)]
        return places[blocks:] + places[:blocks] if crossed else places

    def project(pieces, strips, runs, total=None, column=0):
        runs = [(u, start, stop) for q, start, stop in runs for u in range(q * part, (q + 1) * part)]
        used = sorted({u for u, _, _ in runs})
        weights = [strips[s][u] for u, start, stop in runs for s in range(start, stop)]
        shape = (2 * rows, len(strips) * lanes)
        extra = [] if total is None else [total]
        terms = [(used.index(u), start, stop) for u, start, stop in runs]
        return pl.pallas_call(
            functools.partial(project_kernel, terms, len(used)),
            grid=(1,),
            in_specs=[pl.BlockSpec((rows, wide), lambda i, block=block: (block, 0)) for u in used for _, block in pieces[u]]
            + [pl.BlockSpec((wide, lanes), lambda i, unit=unit: (unit, 0)) for _, unit in weights]
            + [pl.BlockSpec(shape, lambda i: (0, column))] * len(extra),
            out_specs=pl.BlockSpec(shape, lambda i: (0, 0)),
            out_shape=of(*shape),
            compiler_params=params(24),
            name="project",
            cost_estimate=cost(6 * rows * wide * len(weights) * lanes, wide * lanes * len(weights) + 2 * rows * shape[1]),
        )(*[x for u in used for x, _ in pieces[u]], *[x for x, _ in weights], *extra)

    theirs = [
        strip([(taken, 0, 4)]),
        strip([(taken_near, 0, 4)], True),
        strip([(far_4, 0, 2), (far_5, 0, 2)]),
        strip([(both_4, 0, 2), (both_5, 0, 2)], True),
    ]
    mine = [
        strip([(kept, 0, 4)]),
        strip([(kept_near, 0, 4)], True),
        strip([(far_1, 0, 1), (far_2, 0, 2), (far_3, 0, 1)]),
        strip([(both_1, 0, 1), (both_2, 0, 2), (both_3, 0, 1)], True),
    ]
    pieces = own_pieces + other_pieces(last)
    product = project(pieces, theirs + mine, [(0, 0, 3), (0, 4, 8), (1, 0, 3), (1, 4, 8)])
    product = project(pieces, theirs + mine, [(2, 0, 8)], product)
    product, last = together((product, last))
    pieces = own_pieces + other_pieces(last)
    from_them = swap(project(pieces, theirs, [(3, 0, 4), (0, 3, 4), (1, 3, 4)], product, 0), 0, 1)
    product = project(pieces, mine, [(3, 0, 4)], product, 1)

    if strip_width % 128 == 0:
        parts = pl.pallas_call(
            functools.partial(route_kernel, groups, strip_width),
            grid_spec=pltpu.PrefetchScalarGridSpec(
                num_scalar_prefetch=1,
                grid=(1,),
                in_specs=[pl.BlockSpec(x.shape, lambda i, send: (0, 0)) for x in (product, from_them)],
                out_specs=[pl.BlockSpec((rows, size * strip_width), lambda i, send: (0, 0))] * steps,
                scratch_shapes=[pltpu.VMEM((steps, rows, size * strip_width), jnp.float32)],
            ),
            out_shape=[of(rows, size * strip_width)] * steps,
            compiler_params=params(12),
            name="route",
            cost_estimate=cost(0, 6 * rows * steps * size * strip_width),
        )(send_here, product, from_them)
    else:
        parts = jnp.stack(pieces_of(product + from_them, groups, strip_width))
        parts = [lax.dynamic_index_in_dim(parts, send_here[k], 0, False) for k in range(steps)]
    arrived = [lax.ppermute(part, AXES, perm) for part, perm in zip(parts, perms)]
    if strip_width % 128 == 0:
        return pl.pallas_call(
            functools.partial(assemble_kernel, size),
            grid_spec=pltpu.PrefetchScalarGridSpec(
                num_scalar_prefetch=1,
                grid=(1,),
                in_specs=[pl.BlockSpec(x.shape, lambda i, place: (0, 0)) for x in (*arrived, residual)],
                out_specs=pl.BlockSpec(residual.shape, lambda i, place: (0, 0)),
                scratch_shapes=[pltpu.VMEM((ctx, rows, strip_width), jnp.float32)],
            ),
            out_shape=of(*residual.shape),
            compiler_params=params(12),
            name="assemble",
            cost_estimate=cost(0, 3 * residual.size),
        )(place_here, *arrived, residual)
    blocks = jnp.stack([a[:, b * strip_width : (b + 1) * strip_width] for a in arrived for b in range(size)])
    projected = [lax.dynamic_index_in_dim(blocks, place_here[p], 0, False) for p in range(ctx)]
    return residual + jnp.concatenate(projected, axis=1)


def solution(mesh):
    placed = (
        P("ctx", "head"),
        P("ctx", "head"),
        P("ctx", "head"),
        P("head", None, None),
        P("head", None, None),
        P(None, ("ctx", "head")),
        P("ctx", "head"),
    )
    return jax.shard_map(
        functools.partial(body, mesh.shape["ctx"], mesh.shape["head"]),
        mesh=mesh,
        in_specs=placed,
        out_specs=P("ctx", "head"),
        check_vma=False,
    )
```
